32 devices in a mesh: dp: 8 (over z, y), mp: 4 (over x, core).
Axes of the slice: x: 2, y: 2, z: 4, core: 2. Of those that a mesh axis runs over, the one named last changes fastest.
Arguments:
- tokens: bfloat16 [2, 8192, 1024], P(None, ('dp', 'mp')), may hold values from -6 to 6
- lengths: int32 [8, 2, 2], P('dp'), may hold values from 0 to 1024, as said below
- cotangent: bfloat16 [2, 8192, 1024], P(None, ('dp', 'mp')), may hold values from -6 to 6
- attn_gain: float32 [1024], replicated, may hold values from 0.5 to 1.5
- in_weights: bfloat16 [1024, 4, 1024], P(None, None, 'mp'), may hold values from -0.1875 to 0.1875
- ssm_rate: float32 [16, 1024], P(None, 'mp'), may hold values from 0.00048828125 to 0.015625
- ssm_input: float32 [16, 1024], P(None, 'mp'), may hold values from -4 to 4
- ssm_output: float32 [16, 1024], P(None, 'mp'), may hold values from -1.5 to 1.5
- ctx_weights: bfloat16 [8, 128, 256], P('mp'), may hold values from -0.5 to 0.5
- out_weights: bfloat16 [1024, 1024], P('mp'), may hold values from -1.5 to 1.5
- mlp_gain: float32 [1024], replicated, may hold values from 0.5 to 1.5
- up_weights: bfloat16 [1024, 4096], P(None, 'mp'), may hold values from -0.1875 to 0.1875
- down_weights: bfloat16 [4096, 1024], P('mp'), may hold values from -0.09375 to 0.09375
Outputs:
- mixed: bfloat16 [2, 8192, 1024], P(None, ('dp', 'mp'))
- grad_tokens: float32 [2, 8192, 1024], P(None, ('dp', 'mp'))
- grad_attn_gain: float32 [1024], replicated
- grad_in_weights: float32 [1024, 4, 1024], P(None, None, 'mp')
- grad_ssm_rate: float32 [16, 1024], P(None, 'mp')
- grad_ssm_input: float32 [16, 1024], P(None, 'mp')
- grad_ssm_output: float32 [16, 1024], P(None, 'mp')
- grad_ctx_weights: float32 [8, 128, 256], P('mp')
- grad_out_weights: float32 [1024, 1024], P('mp')
- grad_mlp_gain: float32 [1024], replicated
- grad_up_weights: float32 [1024, 4096], P(None, 'mp')
- grad_down_weights: float32 [4096, 1024], P('mp')
The draws below stay inside these ranges and needn't reach their ends.
Inputs may be any that keep to these rules, and one draw needn't show every extreme that they name: `lengths`: entry 0 is a document of 512 tokens or more; entry 1 is 0 or a second document of 512 tokens or more; each document starts on a block of 512 rows and both fit in 1024 rows; in micro-batch 0 the first document of every group is longer than 768 tokens.
All inputs are finite; a program needn't handle non-finite values.
Results may differ from the reference program's by a relative error of at most 0.012.
Values may be sent and summed in bfloat16 or wider, within the bound.
A program may use at most 192 MiB of HBM per device.

```python
import math
import jax
import jax.numpy as jnp
from jax import lax

D = 1024
H = 8
HD = 128
FF = 4096
NS = 16
BLK = 512
CTX = 128
MINLEN = 512
MB = 2
TOK_DEV = 256
GROUP_TOK = 1024
ROWS = 8192
N_DP = 8


def draw_lengths(key, part):
    key = jax.random.fold_in(key, 7)
    block_key, first_key, span_key, second_key, coin_key = jax.random.split(key, 5)
    nblocks = GROUP_TOK // BLK
    first_count = jax.random.randint(block_key, (N_DP, MB), 1, nblocks + 1)
    lowest = jnp.maximum((first_count - 1) * BLK + 1, MINLEN)
    first = jax.random.randint(first_key, (N_DP, MB), lowest, first_count * BLK + 1)
    spanning = jax.random.randint(span_key, (N_DP,), max(MINLEN, GROUP_TOK - TOK_DEV + 1), GROUP_TOK + 1)
    first = first.at[:, 0].set(spanning)
    first = first.at[0, 0].set(GROUP_TOK)
    room = (nblocks - (first + BLK - 1) // BLK) * BLK
    upper = jnp.maximum(room, MINLEN)
    second = jax.random.randint(second_key, (N_DP, MB), MINLEN, upper + 1)
    coin = jax.random.randint(coin_key, (N_DP, MB), 0, 2)
    second = jnp.where((room >= MINLEN) & (coin == 1), second, 0)
    return jnp.stack([first, second], axis=-1).astype(jnp.int32)


def block_scale(rng, dims, shards, low, high):
    def one(axis_at, parts):
        steps = jax.random.uniform(jax.random.fold_in(jax.random.fold_in(rng, 6), axis_at), (parts,), jnp.float32, low / len(shards), high / len(shards))
        return jnp.repeat(jnp.exp(steps), dims[axis_at] // parts).reshape((-1,) + (1,) * (len(dims) - axis_at - 1))

    level = one(*shards[0])
    for cut in shards[1:]:
        level = level * one(*cut)
    return level


def centred(own_key, extent, spread, limit, cuts=(), kind=jnp.bfloat16):
    factor_of = block_scale(own_key, extent, cuts, -0.22, 0.18) if cuts else 1.0
    values = jax.random.normal(own_key, extent, jnp.float32) * spread * factor_of
    return jnp.minimum(jnp.maximum(values, -limit), limit).astype(kind)


def setup_inputs(seed: int = 0) -> dict:
    splits = jax.random.split(jax.random.key(seed), 14)
    tokens = centred(splits[0], (MB, ROWS, D), 1.0, 6.0, ((1, 32),))
    lengths = draw_lengths(jax.random.fold_in(splits[13], 71), 0)
    cotangent = centred(splits[2], (MB, ROWS, D), 1.0, 6.0, ((1, 32),))
    attn_gain = jnp.clip(1.0 + 0.1 * jax.random.normal(splits[3], (D,), jnp.float32), 0.5, 1.5)
    in_weights = centred(splits[4], (D, 4, D), D ** -0.5, 0.1875, ((2, 4),))
    ssm_rate = jnp.clip(jnp.exp(math.log(0.015625) - 3.465736 * jax.random.uniform(splits[5], (NS, D), jnp.float32) ** block_scale(splits[5], (NS, D), ((1, 4),), -0.2, 0.2)), 0.00048828125, 0.015625)
    ssm_input = centred(splits[6], (NS, D), 1.0, 4.0, ((1, 4),), jnp.float32)
    ssm_output = centred(splits[7], (NS, D), NS ** -0.5, 1.5, ((1, 4),), jnp.float32)
    ctx_weights = centred(splits[8], (H, HD, 2 * HD), HD ** -0.5, 0.5, ((0, 4),))
    out_weights = centred(splits[9], (D, D), (max(D // 64, 4)) ** -0.5, 1.5, ((0, 4),))
    mlp_gain = jnp.clip(1.0 + 0.1 * jax.random.normal(splits[10], (D,), jnp.float32), 0.5, 1.5)
    up_weights = centred(splits[11], (D, FF), D ** -0.5, 0.1875, ((1, 4),))
    down_weights = centred(splits[12], (FF, D), FF ** -0.5, 0.09375, ((0, 4),))
    return dict(tokens=tokens, lengths=lengths, cotangent=cotangent, attn_gain=attn_gain, in_weights=in_weights, ssm_rate=ssm_rate, ssm_input=ssm_input, ssm_output=ssm_output, ctx_weights=ctx_weights, out_weights=out_weights, mlp_gain=mlp_gain, up_weights=up_weights, down_weights=down_weights)


@jax.custom_vjp
def low(v):
    return lax.optimization_barrier(v.astype(jnp.bfloat16)).astype(jnp.float32)

@jax.custom_vjp
def low_back(v):
    return v

def low_keep(v):
    return (low(v), None)

def low_pass(kept, grad):
    return (grad,)

def back_keep(v):
    return (v, None)

def back_low(kept, grad):
    return (low(grad),)
low.defvjp(low_keep, low_pass)
low_back.defvjp(back_keep, back_low)
highest = lax.Precision.HIGHEST

def rms_norm(values, gain):
    return values * lax.rsqrt(lax.optimization_barrier(jnp.mean(values * values, axis=-1, keepdims=True)) + 1e-05) * gain

def block_layout(doc_lengths, nblocks):
    first_blocks = (doc_lengths[0] + BLK - 1) // BLK
    second_blocks = (doc_lengths[1] + BLK - 1) // BLK
    block_index = jnp.arange(nblocks, dtype=jnp.int32)
    document = jnp.where(block_index < first_blocks, 0, jnp.where(block_index < first_blocks + second_blocks, 1, 2))
    start_block = jnp.where(document == 0, 0, first_blocks)
    doc_extent = jnp.where(document == 0, doc_lengths[0], jnp.where(document == 1, doc_lengths[1], 0))
    within_doc = (block_index - start_block)[:, None] * BLK + jnp.arange(BLK, dtype=jnp.int32)[None, :]
    token_valid = within_doc < doc_extent[:, None]
    linked = jnp.concatenate([jnp.zeros((1,), dtype=bool), document[1:] == document[:-1]])
    return (token_valid, linked.astype(jnp.float32))

def ssm_context(driver, rate, input_coef, output_coef, linked):
    chans = driver.shape[1]
    nblocks = driver.shape[0] // BLK
    head_len = BLK - CTX
    blocks = driver.reshape(nblocks, BLK, chans)
    in_gain = input_coef * jnp.sqrt(1.0 - jnp.exp(-2.0 * rate))
    head_pos = jnp.arange(head_len, dtype=jnp.float32)
    head_table = jnp.exp(-rate[:, :, None] * (head_len - 1.0 - head_pos)) * in_gain[:, :, None]
    head_decay = jnp.exp(-rate * head_len)
    tail_pos = jnp.arange(CTX, dtype=jnp.float32)
    rising = jnp.exp(rate[None] * tail_pos[:, None, None]) * in_gain[None]
    falling = jnp.exp(-rate[None] * tail_pos[:, None, None])
    lower = (tail_pos[:, None] >= tail_pos[None, :]).astype(jnp.float32)
    single = jnp.exp(-rate)

    def advance(state, packed):
        block, keep = packed
        state = state * keep
        middle = head_decay * state + jnp.einsum('ncj,jc->nc', head_table, block[:head_len], precision=highest)
        weighted = rising * block[head_len:, None, :]
        prefix = jnp.dot(lower, weighted.reshape(CTX, -1), precision=highest).reshape(weighted.shape)
        states = falling * (single[None] * middle[None] + prefix)
        context = lax.optimization_barrier(jnp.sum(output_coef[None] * states, axis=1))
        return (states[-1], context)
    _, contexts = lax.scan(jax.checkpoint(advance), jnp.zeros(rate.shape, jnp.float32), (blocks, linked))
    return jnp.concatenate([jnp.zeros_like(contexts[:1]), contexts[:-1]], axis=0)

def attend(queries, keys_tok, values_tok, context, ctx_weights, token_valid, linked):
    rows, chans = queries.shape
    heads = chans // HD
    nblocks = rows // BLK
    ctx_heads = context.reshape(nblocks, CTX, heads, HD)
    ctx_keys = low_back(low(jnp.einsum('bjhd,hde->bjhe', ctx_heads, ctx_weights[:, :, :HD], precision=highest)))
    ctx_vals = low_back(low(jnp.einsum('bjhd,hde->bjhe', ctx_heads, ctx_weights[:, :, HD:], precision=highest)))
    query_blocks = queries.reshape(nblocks, BLK, heads, HD)
    key_blocks = keys_tok.reshape(nblocks, BLK, heads, HD)
    value_blocks = values_tok.reshape(nblocks, BLK, heads, HD)
    scale = 1.0 / math.sqrt(HD)

    def one_block(packed):
        query_b, key_b, value_b, ckey_b, cval_b, keep, valid_b = packed
        scores = jnp.concatenate([jnp.einsum('thd,jhd->htj', query_b, ckey_b, precision=highest), jnp.einsum('thd,jhd->htj', query_b, key_b, precision=highest)], axis=-1) * scale
        scores = low_back(scores)
        places = jnp.arange(BLK, dtype=jnp.int32)
        earlier = places[None, :] <= places[:, None]
        seen = earlier & (valid_b[None, :] | (places[None, :] == places[:, None]))
        linked_keys = jnp.broadcast_to(keep > 0.5, (BLK, CTX))
        allowed = jnp.concatenate([linked_keys, seen], axis=1)
        scores = jnp.where(allowed[None], scores, -1e+30)
        probs = low(jax.nn.softmax(scores, axis=-1))
        return jnp.einsum('htj,jhd->thd', probs[:, :, :CTX], cval_b, precision=highest) + jnp.einsum('htj,jhd->thd', probs[:, :, CTX:], value_b, precision=highest)
    result = lax.map(jax.checkpoint(one_block), (query_blocks, key_blocks, value_blocks, ctx_keys, ctx_vals, linked, token_valid))
    return result.reshape(rows, chans)

def mixer(normed, in_weights, ssm_rate, ssm_input, ssm_output, ctx_weights, out_weights, token_valid, linked):
    rows = normed.shape[0]
    chans = in_weights.shape[2]
    projected = jnp.dot(normed, in_weights.reshape(in_weights.shape[0], 4 * chans), precision=highest).reshape(rows, 4, chans)
    queries = low_back(low(projected[:, 0]))
    keys_tok = low_back(low(projected[:, 1]))
    values_tok = low_back(low(projected[:, 2]))
    driver = low_back(projected[:, 3])
    context = low(ssm_context(driver, ssm_rate, ssm_input, ssm_output, linked))
    heads_out = low_back(low(attend(queries, keys_tok, values_tok, context, ctx_weights, token_valid, linked)))
    return jnp.dot(heads_out, out_weights, precision=highest)

def feed_forward(normed, up_weights, down_weights):
    before = low_back(jnp.dot(normed, up_weights, precision=highest))
    hidden = low(jax.nn.gelu(before, approximate=True))
    return jnp.dot(hidden, down_weights, precision=highest)

def sequence_layer(inputs, weights, token_valid, linked):
    attn_gain, in_weights, ssm_rate, ssm_input, ssm_output, ctx_weights, out_weights, mlp_gain, up_weights, down_weights = weights
    normed = low(rms_norm(inputs, attn_gain))
    branch = low_back(mixer(normed, in_weights, ssm_rate, ssm_input, ssm_output, ctx_weights, out_weights, token_valid, linked))
    middle = inputs + branch
    normed_two = low(rms_norm(middle, mlp_gain))
    return middle + low_back(feed_forward(normed_two, up_weights, down_weights))

def reference(tokens, lengths, cotangent, attn_gain, in_weights, ssm_rate, ssm_input, ssm_output, ctx_weights, out_weights, mlp_gain, up_weights, down_weights):
    weights = (attn_gain.astype(jnp.float32), in_weights.astype(jnp.float32), ssm_rate.astype(jnp.float32), ssm_input.astype(jnp.float32), ssm_output.astype(jnp.float32), ctx_weights.astype(jnp.float32), out_weights.astype(jnp.float32), mlp_gain.astype(jnp.float32), up_weights.astype(jnp.float32), down_weights.astype(jnp.float32))
    nblocks = GROUP_TOK // BLK
    inputs = tokens.astype(jnp.float32).reshape(MB * N_DP, GROUP_TOK, D)
    grads = cotangent.astype(jnp.float32).reshape(MB * N_DP, GROUP_TOK, D)
    doc_lengths = jnp.transpose(lengths, (1, 0, 2)).reshape(MB * N_DP, 2)

    def one_sequence(totals, packed):
        seq_in, seq_grad, seq_len = packed
        token_valid, linked = block_layout(seq_len, nblocks)
        outputs, pullback = jax.vjp(lambda seq_vals, weight_vals: sequence_layer(seq_vals, weight_vals, token_valid, linked), seq_in, weights)
        grad_in, grad_weights = pullback(seq_grad)
        totals = tuple((left + right for left, right in zip(totals, grad_weights)))
        return (totals, (outputs, grad_in))
    zeros = tuple((jnp.zeros(weight.shape, jnp.float32) for weight in weights))
    totals, (outputs, grad_in) = lax.scan(one_sequence, zeros, (inputs, grads, doc_lengths))
    mixed = outputs.reshape(MB, ROWS, D).astype(jnp.bfloat16)
    grad_tokens = grad_in.reshape(MB, ROWS, D)
    return (mixed, grad_tokens, totals[0], totals[1], totals[2], totals[3], totals[4], totals[5], totals[6], totals[7], totals[8], totals[9])
```

```python
import functools
import math

import jax
import jax.numpy as jnp
from jax import lax
from jax.experimental import pallas as pl
from jax.experimental.pallas import tpu as pltpu
from jax.sharding import PartitionSpec as P

HD = 128
BLK = 512
CTX = 128
HEAD = BLK - CTX
NS = 16
EPS = 1e-05
SCALE = 1.0 / math.sqrt(HD)
SCALE2 = SCALE * math.log2(math.e)
NEG = -1e30
F32 = jnp.float32
BF16 = jnp.bfloat16

VMEM = pl.BlockSpec(memory_space=pltpu.VMEM)
SMEM = pl.BlockSpec(memory_space=pltpu.SMEM)
ANY = pl.BlockSpec(memory_space=pl.ANY)


def params(mib):
    return pltpu.CompilerParams(vmem_limit_bytes=mib << 20)


def cost(flops, nbytes):
    return pl.CostEstimate(flops=int(flops), bytes_accessed=int(nbytes), transcendentals=0)


def dot(a, b):
    return lax.dot_general(a, b, (((1,), (0,)), ((), ())), preferred_element_type=F32)


def dot_nt(a, b):
    return lax.dot_general(a, b, (((1,), (1,)), ((), ())), preferred_element_type=F32)


def dot_tn(a, b):
    return lax.dot_general(a, b, (((0,), (0,)), ((), ())), preferred_element_type=F32)


def shape(dims, kind):
    return jax.ShapeDtypeStruct(dims, kind)


def norm_one(tokens, gain, micro):
    rows, width = tokens.shape[1:]

    def kernel(x_ref, g_ref, o_ref):
        x = x_ref[0].astype(F32)
        scale = lax.rsqrt(jnp.mean(x * x, axis=-1, keepdims=True) + EPS)
        o_ref[...] = (x * scale * g_ref[...]).astype(BF16)

    return pl.pallas_call(
        kernel,
        grid=(1,),
        in_specs=[
            pl.BlockSpec((1, rows, width), lambda i: (micro, 0, 0)),
            pl.BlockSpec((1, width), lambda i: (0, 0)),
        ],
        out_specs=pl.BlockSpec((rows, width), lambda i: (0, 0)),
        out_shape=shape((rows, width), BF16),
        compiler_params=params(16),
        cost_estimate=cost(0, rows * width * 4),
    )(tokens, gain)


def first_of(rows, width):
    return pl.BlockSpec((1, rows, width), lambda i: (0, 0, 0))


def norm_two(tokens, part, sib, far, gain, micro):
    rows, width = tokens.shape[1:]

    def kernel(x_ref, p_ref, s_ref, r_ref, g_ref, mid_ref, o_ref):
        mid = (
            x_ref[0].astype(F32)
            + p_ref[0].astype(F32)
            + s_ref[0].astype(F32)
            + r_ref[...].astype(F32)
        )
        mid_ref[...] = mid
        scale = lax.rsqrt(jnp.mean(mid * mid, axis=-1, keepdims=True) + EPS)
        o_ref[...] = (mid * scale * g_ref[...]).astype(BF16)

    flat = pl.BlockSpec((rows, width), lambda i: (0, 0))
    return pl.pallas_call(
        kernel,
        grid=(1,),
        in_specs=[
            pl.BlockSpec((1, rows, width), lambda i: (micro, 0, 0)),
            first_of(rows, width),
            first_of(rows, width),
            flat,
            pl.BlockSpec((1, width), lambda i: (0, 0)),
        ],
        out_specs=[flat, flat],
        out_shape=[shape((rows, width), F32), shape((rows, width), BF16)],
        compiler_params=params(24),
        cost_estimate=cost(0, rows * width * 14),
    )(tokens, part, sib, far, gain)


def mix_out(middle, part, sib, far, prior, micro, count):
    rows, width = middle.shape

    def kernel(*refs):
        m_ref, p_ref, s_ref, r_ref = refs[:4]
        o_ref = refs[-1]
        branch = p_ref[0].astype(F32) + s_ref[0].astype(F32) + r_ref[...].astype(F32)
        o_ref[0] = (m_ref[...] + branch).astype(BF16)

    flat = pl.BlockSpec((rows, width), lambda i: (0, 0))
    specs = [flat, first_of(rows, width), first_of(rows, width), flat]
    args = [middle, part, sib, far]
    alias = {}
    if prior is not None:
        specs.append(ANY)
        args.append(prior)
        alias = {4: 0}
    return pl.pallas_call(
        kernel,
        grid=(1,),
        in_specs=specs,
        out_specs=pl.BlockSpec((1, rows, width), lambda i: (micro, 0, 0)),
        out_shape=shape((count, rows, width), BF16),
        input_output_aliases=alias,
        compiler_params=params(24),
        cost_estimate=cost(0, rows * width * 12),
    )(*args)


def norm_two_back(middle, part, sib, far, cotangent, gain, micro):
    rows, width = middle.shape

    def kernel(m_ref, p_ref, s_ref, r_ref, c_ref, g_ref, gm_ref, low_ref, gg_ref):
        mid = m_ref[...]
        grad = p_ref[0].astype(F32) + s_ref[0].astype(F32) + r_ref[...].astype(F32)
        scale = lax.rsqrt(jnp.mean(mid * mid, axis=-1, keepdims=True) + EPS)
        unit = mid * scale
        gg_ref[...] = jnp.sum(grad * unit, axis=0, keepdims=True)
        inner = grad * g_ref[...]
        pull = scale * (inner - unit * jnp.mean(inner * unit, axis=-1, keepdims=True))
        total = c_ref[0].astype(F32) + pull
        gm_ref[...] = total
        low_ref[...] = total.astype(BF16)

    flat = pl.BlockSpec((rows, width), lambda i: (0, 0))
    line = pl.BlockSpec((1, width), lambda i: (0, 0))
    return pl.pallas_call(
        kernel,
        grid=(1,),
        in_specs=[
            flat,
            first_of(rows, width),
            first_of(rows, width),
            flat,
            pl.BlockSpec((1, rows, width), lambda i: (micro, 0, 0)),
            line,
        ],
        out_specs=[flat, flat, line],
        out_shape=[
            shape((rows, width), F32),
            shape((rows, width), BF16),
            shape((1, width), F32),
        ],
        compiler_params=params(24),
        cost_estimate=cost(0, rows * width * 18),
    )(middle, part, sib, far, cotangent, gain)


def norm_one_back(tokens, part, sib, far, grad_middle, gain, prior, micro, count):
    rows, width = grad_middle.shape

    def kernel(*refs):
        x_ref, p_ref, s_ref, r_ref, gm_ref, g_ref = refs[:6]
        o_ref, gg_ref = refs[-2:]
        x = x_ref[0].astype(F32)
        grad = p_ref[0].astype(F32) + s_ref[0].astype(F32) + r_ref[...].astype(F32)
        scale = lax.rsqrt(jnp.mean(x * x, axis=-1, keepdims=True) + EPS)
        unit = x * scale
        gg_ref[...] = jnp.sum(grad * unit, axis=0, keepdims=True)
        inner = grad * g_ref[...]
        pull = scale * (inner - unit * jnp.mean(inner * unit, axis=-1, keepdims=True))
        o_ref[0] = gm_ref[...] + pull

    flat = pl.BlockSpec((rows, width), lambda i: (0, 0))
    line = pl.BlockSpec((1, width), lambda i: (0, 0))
    here = pl.BlockSpec((1, rows, width), lambda i: (micro, 0, 0))
    specs = [here, first_of(rows, width), first_of(rows, width), flat, flat, line]
    args = [tokens, part, sib, far, grad_middle, gain]
    alias = {}
    if prior is not None:
        specs.append(ANY)
        args.append(prior)
        alias = {6: 0}
    return pl.pallas_call(
        kernel,
        grid=(1,),
        in_specs=specs,
        out_specs=[here, line],
        out_shape=[shape((count, rows, width), F32), shape((1, width), F32)],
        input_output_aliases=alias,
        compiler_params=params(24),
        cost_estimate=cost(0, rows * width * 16),
    )(*args)


def add_second(part, sib):
    rows, width = part.shape[1:]

    def kernel(p_ref, s_ref, o_ref):
        o_ref[...] = (p_ref[0].astype(F32) + s_ref[0].astype(F32)).astype(BF16)

    second = pl.BlockSpec((1, rows, width), lambda i: (1, 0, 0))
    return pl.pallas_call(
        kernel,
        grid=(1,),
        in_specs=[second, second],
        out_specs=pl.BlockSpec((rows, width), lambda i: (0, 0)),
        out_shape=shape((rows, width), BF16),
        compiler_params=params(16),
        cost_estimate=cost(0, rows * width * 6),
    )(part, sib)


def flip(value, axis, bit):
    count = lax.axis_size(axis)
    return lax.ppermute(value, axis, [(i, i ^ bit) for i in range(count)])


def gather_mp(value):
    near = flip(value, "mp", 1)
    far = flip(value, "mp", 2)
    both = flip(far, "mp", 1)
    return (value, near, far, both)


def scatter_mp(keep, give):
    sib = flip(give, "mp", 1)
    far = flip(add_second(keep, sib), "mp", 2)
    return (keep, sib, far)


def triangle(upper):
    row = lax.broadcasted_iota(jnp.int32, (CTX, 2 * CTX), 0)
    col = lax.broadcasted_iota(jnp.int32, (CTX, 2 * CTX), 1) % CTX
    keep = (row <= col) if upper else (row >= col)
    return jnp.where(keep, 1.0, 0.0).astype(BF16)


def running(tri, values):
    high = values.astype(BF16)
    rest = (values - high.astype(F32)).astype(BF16)
    return dot(tri, jnp.concatenate([high, rest], axis=0))


def head_sums(u_ref, rate_ref, moment):
    width = rate_ref.shape[1]
    place = lax.broadcasted_iota(jnp.int32, (8, width), 0).astype(F32)
    sums, moments = [], []
    group = 4 if moment else 8
    for base in range(0, NS, group):
        rates = [rate_ref[n : n + 1, :] for n in range(base, base + group)]
        steps = [jnp.broadcast_to(jnp.exp(-8.0 * r), (8, width)) for r in rates]

        def body(chunk, carry):
            start = pl.multiple_of(chunk * 8, 8)
            rows = u_ref[pl.ds(start, 8), :]
            first = [acc * step + rows for acc, step in zip(carry[0], steps)]
            if not moment:
                return (first, carry[1])
            scaled = rows * (place + (chunk * 8 - HEAD).astype(F32))
            second = [acc * step + scaled for acc, step in zip(carry[1], steps)]
            return (first, second)

        zero = [jnp.zeros((8, width), F32) for _ in range(group)]
        first, second = lax.fori_loop(
            0, HEAD // 8, body, (zero, list(zero) if moment else []), unroll=4
        )
        for k, rate in enumerate(rates):
            last = jnp.exp(rate * (place - 8.0))
            sums.append(jnp.sum(first[k] * last, axis=0, keepdims=True))
            if moment:
                moments.append(jnp.sum(second[k] * last, axis=0, keepdims=True))
    return sums, moments


def state_forward(u_ref, rate_ref, in_ref, out_ref):
    width = rate_ref.shape[1]
    sums, _ = head_sums(u_ref, rate_ref, False)
    tail = u_ref[pl.ds(HEAD, CTX), :]
    time = lax.broadcasted_iota(jnp.int32, (CTX, width), 0).astype(F32)
    tri = triangle(False)
    total = jnp.zeros((CTX, width), F32)
    for n in range(NS):
        rate = rate_ref[n : n + 1, :]
        gain = in_ref[n : n + 1, :] * jnp.sqrt(1.0 - jnp.exp(-2.0 * rate))
        weight = gain * out_ref[n : n + 1, :]
        prefix = running(tri, jnp.exp(rate * time) * tail)
        total = total + weight * (jnp.exp(-rate * time) * (sums[n] + prefix))
    return total


def state_backward(grad, u_ref, du_ref, rate_ref, in_ref, out_ref, gs_ref):
    width = rate_ref.shape[1]
    sums, moments = head_sums(u_ref, rate_ref, True)
    tail = u_ref[pl.ds(HEAD, CTX), :]
    time = lax.broadcasted_iota(jnp.int32, (CTX, width), 0).astype(F32)
    place = lax.broadcasted_iota(jnp.int32, (8, width), 0).astype(F32)
    lower, upper = triangle(False), triangle(True)
    total = jnp.zeros((CTX, width), F32)
    starts = []
    for n in range(NS):
        rate = rate_ref[n : n + 1, :]
        root = jnp.sqrt(1.0 - jnp.exp(-2.0 * rate))
        enter = in_ref[n : n + 1, :]
        leave = out_ref[n : n + 1, :]
        gain = enter * root
        rising = jnp.exp(rate * time)
        driven = rising * tail
        states = sums[n] + running(lower, driven)
        seen = jnp.exp(-rate * time) * grad
        later = running(upper, seen)
        product = seen * states
        energy = jnp.sum(product, axis=0, keepdims=True)
        slope = jnp.sum(time * (product - driven * later), axis=0, keepdims=True)
        slope = slope - later[0:1] * moments[n]
        total = total + (gain * leave) * (rising * later)
        starts.append((gain * leave) * later[0:1])
        gs_ref[0, n : n + 1, :] = leave * (
            energy * enter * jnp.exp(-2.0 * rate) / root - gain * slope
        )
        gs_ref[1, n : n + 1, :] = leave * energy * root
        gs_ref[2, n : n + 1, :] = gain * energy
    du_ref[pl.ds(HEAD, CTX), :] = total
    group = 8
    for base in range(0, NS, group):
        rates = [rate_ref[n : n + 1, :] for n in range(base, base + group)]
        steps = [jnp.broadcast_to(jnp.exp(-8.0 * r), (8, width)) for r in rates]
        begin = [
            starts[base + k] * jnp.exp(rate * (place - 8.0)) for k, rate in enumerate(rates)
        ]

        def body(index, carry):
            start = pl.multiple_of(HEAD - 8 - index * 8, 8)
            value = functools.reduce(lambda a, b: a + b, carry)
            if base:
                value = value + du_ref[pl.ds(start, 8), :]
            du_ref[pl.ds(start, 8), :] = value
            return [c * step for c, step in zip(carry, steps)]

        lax.fori_loop(0, HEAD // 8, body, begin, unroll=4)


def layout_scalars(len_ref, micro):
    first, second = len_ref[micro, 0], len_ref[micro, 1]
    first_blocks = (first + (BLK - 1)) // BLK
    second_blocks = (second + (BLK - 1)) // BLK
    docs, valid = [], []
    for b in range(2):
        doc = jnp.where(b < first_blocks, 0, jnp.where(b < first_blocks + second_blocks, 1, 2))
        start = jnp.where(doc == 0, 0, first_blocks)
        extent = jnp.where(doc == 0, first, jnp.where(doc == 1, second, 0))
        docs.append(doc)
        valid.append(extent - (b - start) * BLK)
    return valid, docs[0] == docs[1]


def load_pieces(pieces, scratch, sems):
    for j, piece in enumerate(pieces):
        pltpu.make_async_copy(piece, scratch.at[j], sems.at[j]).start()


def wait_piece(pieces, scratch, sems, j):
    pltpu.make_async_copy(pieces[0], scratch.at[j], sems.at[j]).wait()


def attn_forward(pieces, in_w, rate, enter, leave, ctx_w, out_w, lengths, where, micro):
    rows, width = pieces[0].shape
    chans = out_w.shape[0]
    heads = chans // HD
    total = 4 * rows

    def kernel(
        me_ref, len_ref, n0, n1, n2, n3, w_ref, rate_ref, in_ref, out_ref, cw_ref, ow_ref,
        q_ref, k_ref, v_ref, u_ref, ctx_ref, ckv_ref, pr_ref, ho_ref, keep_ref, give_ref,
        xs, sems,
    ):
        me = me_ref[0]
        ns = (n0, n1, n2, n3)
        load_pieces(ns, xs, sems)

        def project(j, carry):
            wait_piece(ns, xs, sems, j)
            base = pl.multiple_of((me ^ j) * rows, rows)
            x = xs[j]
            q_ref[pl.ds(base, rows), :] = dot(x, w_ref[:, :chans]).astype(BF16)
            k_ref[pl.ds(base, rows), :] = dot(x, w_ref[:, chans : 2 * chans]).astype(BF16)
            v_ref[pl.ds(base, rows), :] = dot(x, w_ref[:, 2 * chans : 3 * chans]).astype(BF16)

            @pl.when(base < BLK)
            def _():
                u_ref[pl.ds(base, rows), :] = dot(x, w_ref[:, 3 * chans :])

            return carry

        lax.fori_loop(0, 4, project, 0)
        context = state_forward(u_ref, rate_ref, in_ref, out_ref).astype(BF16)
        ctx_ref[...] = context
        for h in range(heads):
            ckv_ref[h] = dot(context[:, h * HD : (h + 1) * HD], cw_ref[h]).astype(BF16)
        valid, linked = layout_scalars(len_ref, micro)
        for h in range(heads):
            lanes = slice(h * HD, (h + 1) * HD)
            for b in range(2):
                for half in range(2):
                    row0 = half * rows
                    keys = row0 + rows
                    q = q_ref[b * BLK + row0 : b * BLK + row0 + rows, lanes]
                    k = k_ref[b * BLK : b * BLK + keys, lanes]
                    v = v_ref[b * BLK : b * BLK + keys, lanes]
                    s = dot_nt(q, k) * SCALE2
                    row = lax.broadcasted_iota(jnp.int32, (rows, keys), 0) + row0
                    col = lax.broadcasted_iota(jnp.int32, (rows, keys), 1)
                    allowed = (col < jnp.minimum(row, valid[b])) | (col == row)
                    s = jnp.where(allowed, s, NEG)
                    peak = jnp.max(s, axis=-1, keepdims=True)
                    if b:
                        sc = dot_nt(q, ckv_ref[h, :, :HD]) * SCALE2
                        sc = jnp.where(linked, sc, NEG)
                        peak = jnp.maximum(peak, jnp.max(sc, axis=-1, keepdims=True))
                        ec = jnp.exp2(sc - peak)
                    e = jnp.exp2(s - peak)
                    norm = jnp.sum(e, axis=-1, keepdims=True)
                    if b:
                        norm = norm + jnp.sum(ec, axis=-1, keepdims=True)
                    inverse = 1.0 / norm
                    p = (e * inverse).astype(BF16)
                    pr_ref[h, b, row0 : row0 + rows, CTX : CTX + keys] = p
                    o = dot(p, v)
                    if b:
                        pc = (ec * inverse).astype(BF16)
                        pr_ref[h, b, row0 : row0 + rows, :CTX] = pc
                        o = o + dot(pc, ckv_ref[h, :, HD:])
                    ho_ref[me ^ (2 * b + half), :, lanes] = o.astype(BF16)
        for slot, j in enumerate((0, 2)):
            keep_ref[slot] = dot(ho_ref[j], ow_ref[...]).astype(BF16)
        for slot, j in enumerate((1, 3)):
            give_ref[slot] = dot(ho_ref[j], ow_ref[...]).astype(BF16)

    return pl.pallas_call(
        kernel,
        in_specs=[SMEM, SMEM] + [ANY] * 4 + [VMEM] * 6,
        out_specs=[VMEM] * 10,
        out_shape=[
            shape((total, chans), BF16),
            shape((total, chans), BF16),
            shape((total, chans), BF16),
            shape((BLK, chans), F32),
            shape((CTX, chans), BF16),
            shape((heads, CTX, 2 * HD), BF16),
            shape((heads, 2, BLK, BLK + CTX), BF16),
            shape((4, rows, chans), BF16),
            shape((2, rows, width), BF16),
            shape((2, rows, width), BF16),
        ],
        scratch_shapes=[pltpu.VMEM((4, rows, width), BF16), pltpu.SemaphoreType.DMA((4,))],
        compiler_params=params(48),
        cost_estimate=cost(12e9, 16e6),
    )(where, lengths, *pieces, in_w, rate, enter, leave, ctx_w, out_w)


def attn_backward(pieces, saved, in_w, rate, enter, leave, ctx_w, out_w, where):
    rows, width = pieces[0].shape
    chans = out_w.shape[0]
    heads = chans // HD
    total = 4 * rows
    q, k, v, u, ctx, ckv, probs = saved

    def kernel(
        me_ref, g0, g1, g2, g3, q_ref, k_ref, v_ref, u_ref, ctx_ref, ckv_ref, pr_ref,
        w_ref, rate_ref, in_ref, out_ref, cw_ref, ow_ref,
        gp_ref, keep_ref, give_ref, gcw_ref, gs_ref,
        gs, sems, dh, du, gctx,
    ):
        me = me_ref[0]
        gbs = (g0, g1, g2, g3)
        load_pieces(gbs, gs, sems)

        def heads_grad(j, carry):
            wait_piece(gbs, gs, sems, j)
            base = pl.multiple_of((me ^ j) * rows, rows)
            dh[pl.ds(base, rows), :] = dot_nt(gs[j], ow_ref[...]).astype(BF16)
            return carry

        lax.fori_loop(0, 4, heads_grad, 0)
        for h in range(heads):
            lanes = slice(h * HD, (h + 1) * HD)
            for b in range(2):
                grad_k = [None, None]
                grad_v = [None, None]
                grad_c = None
                grad_cv = None
                for half in (1, 0):
                    row0 = half * rows
                    keys = row0 + rows
                    spot = slice(b * BLK + row0, b * BLK + row0 + rows)
                    go = dh[spot, lanes]
                    qh = q_ref[spot, lanes]
                    kh = k_ref[b * BLK : b * BLK + keys, lanes]
                    vh = v_ref[b * BLK : b * BLK + keys, lanes]
                    p = pr_ref[h, b, row0 : row0 + rows, CTX : CTX + keys]
                    pf = p.astype(F32)
                    dp = dot_nt(go, vh)
                    delta = jnp.sum(dp * pf, axis=-1, keepdims=True)
                    if b:
                        pc = pr_ref[h, b, row0 : row0 + rows, :CTX]
                        pcf = pc.astype(F32)
                        dpc = dot_nt(go, ckv_ref[h, :, HD:])
                        delta = delta + jnp.sum(dpc * pcf, axis=-1, keepdims=True)
                        dsc = (pcf * (dpc - delta)).astype(BF16)
                    ds = (pf * (dp - delta)).astype(BF16)
                    dq = dot(ds, kh)
                    if b:
                        dq = dq + dot(dsc, ckv_ref[h, :, :HD])
                        one = dot_tn(dsc, qh)
                        two = dot_tn(pc, go)
                        grad_c = one if grad_c is None else grad_c + one
                        grad_cv = two if grad_cv is None else grad_cv + two
                    gp_ref[me ^ (2 * b + half), :, lanes] = (dq * SCALE).astype(BF16)
                    dk = dot_tn(ds, qh)
                    dv = dot_tn(p, go)
                    for part in range(half + 1):
                        cut = slice(part * rows, (part + 1) * rows)
                        if half:
                            grad_k[part] = dk[cut]
                            grad_v[part] = dv[cut]
                        else:
                            grad_k[0] = grad_k[0] + dk
                            grad_v[0] = grad_v[0] + dv
                for part in range(2):
                    slot = me ^ (2 * b + part)
                    gp_ref[slot, :, chans + h * HD : chans + (h + 1) * HD] = (
                        grad_k[part] * SCALE
                    ).astype(BF16)
                    gp_ref[slot, :, 2 * chans + h * HD : 2 * chans + (h + 1) * HD] = grad_v[
                        part
                    ].astype(BF16)
                if b:
                    low_c = (grad_c * SCALE).astype(BF16)
                    low_cv = grad_cv.astype(BF16)
                    ch = ctx_ref[:, lanes]
                    gcw_ref[h, :, :HD] = dot_tn(ch, low_c)
                    gcw_ref[h, :, HD:] = dot_tn(ch, low_cv)
                    gctx[:, lanes] = dot_nt(low_c, cw_ref[h, :, :HD]) + dot_nt(
                        low_cv, cw_ref[h, :, HD:]
                    )
        state_backward(gctx[...], u_ref, du, rate_ref, in_ref, out_ref, gs_ref)
        for b in range(2):
            for half in range(2):
                slot = me ^ (2 * b + half)
                if b:
                    gp_ref[slot, :, 3 * chans :] = jnp.zeros((rows, chans), BF16)
                else:
                    gp_ref[slot, :, 3 * chans :] = du[half * rows : (half + 1) * rows, :].astype(
                        BF16
                    )

        def back(slot, carry):
            keep_ref[slot] = dot_nt(gp_ref[2 * slot], w_ref[...]).astype(BF16)
            give_ref[slot] = dot_nt(gp_ref[2 * slot + 1], w_ref[...]).astype(BF16)
            return carry

        lax.fori_loop(0, 2, back, 0)

    return pl.pallas_call(
        kernel,
        in_specs=[SMEM] + [ANY] * 4 + [VMEM] * 13,
        out_specs=[VMEM] * 5,
        out_shape=[
            shape((4, rows, 4 * chans), BF16),
            shape((2, rows, width), BF16),
            shape((2, rows, width), BF16),
            shape((heads, CTX, 2 * HD), F32),
            shape((3, NS, chans), F32),
        ],
        scratch_shapes=[
            pltpu.VMEM((4, rows, width), BF16),
            pltpu.SemaphoreType.DMA((4,)),
            pltpu.VMEM((total, chans), BF16),
            pltpu.VMEM((BLK, chans), F32),
            pltpu.VMEM((CTX, chans), F32),
        ],
        compiler_params=params(48),
        cost_estimate=cost(20e9, 18e6),
    )(where, *pieces, q, k, v, u, ctx, ckv, probs, in_w, rate, enter, leave, ctx_w, out_w)


def feed(pieces, grads, up, down):
    rows, width = pieces[0].shape
    hidden = up.shape[1]
    root = math.sqrt(2.0 / math.pi)

    def kernel(
        n0, n1, n2, n3, c0, c1, c2, c3, up_ref, down_ref,
        hid_ref, gb_ref, fk_ref, fg_ref, gk_ref, gg_ref,
        xs, cs, xsem, csem,
    ):
        i = pl.program_id(0)
        order = (0, 2, 1, 3)
        ns, cots = (n0, n1, n2, n3), (c0, c1, c2, c3)

        @pl.when(i == 0)
        def _():
            for step, j in enumerate(order):
                pltpu.make_async_copy(ns[j], xs.at[step], xsem.at[step]).start()
                pltpu.make_async_copy(cots[j], cs.at[step], csem.at[step]).start()

        wait_piece(ns, xs, xsem, i)
        wait_piece(cots, cs, csem, i)
        before = dot(xs[i], up_ref[...])
        square = before * before
        t = jnp.tanh(root * (before * (1.0 + 0.044715 * square)))
        half = 0.5 + 0.5 * t
        hid = (before * half).astype(BF16)
        hid_ref[0] = hid
        slope = half + (0.5 * root) * before * (1.0 - t * t) * (1.0 + 0.134145 * square)
        branch = dot(hid, down_ref[...]).astype(BF16)
        gh = dot_nt(cs[i], down_ref[...])
        gb = (gh * slope).astype(BF16)
        gb_ref[0] = gb
        gn = dot_nt(gb, up_ref[...]).astype(BF16)

        @pl.when(i < 2)
        def _():
            fk_ref[0] = branch
            gk_ref[0] = gn

        @pl.when(i >= 2)
        def _():
            fg_ref[0] = branch
            gg_ref[0] = gn

    whole = pl.BlockSpec(memory_space=pltpu.VMEM)
    low = pl.BlockSpec((1, rows, width), lambda i: (jnp.minimum(i, 1), 0, 0))
    high = pl.BlockSpec((1, rows, width), lambda i: (jnp.maximum(i - 2, 0), 0, 0))
    at = pl.BlockSpec((1, rows, hidden), lambda i: (i, 0, 0))
    return pl.pallas_call(
        kernel,
        grid=(4,),
        in_specs=[ANY] * 8 + [whole] * 2,
        out_specs=[at, at, low, high, low, high],
        out_shape=[
            shape((4, rows, hidden), BF16),
            shape((4, rows, hidden), BF16),
        ]
        + [shape((2, rows, width), BF16)] * 4,
        scratch_shapes=[
            pltpu.VMEM((4, rows, width), BF16),
            pltpu.VMEM((4, rows, width), BF16),
            pltpu.SemaphoreType.DMA((4,)),
            pltpu.SemaphoreType.DMA((4,)),
        ],
        compiler_params=params(40),
        cost_estimate=cost(30e9, 16e6),
    )(*pieces, *grads, up, down)


def weight_grad(lefts, rights, left_order, right_order, flag):
    def expand(values, order):
        refs, picks = [], []
        for value in values:
            if isinstance(value, tuple):
                for j in order:
                    picks.append((len(refs) + j, None))
                refs.extend(value)
            else:
                for j in order:
                    picks.append((len(refs), j))
                refs.append(value)
        return refs, picks

    lrefs, lpicks = expand(lefts, left_order)
    rrefs, rpicks = expand(rights, right_order)
    count = len(lpicks)
    rows = lrefs[0].shape[-2]
    m, n = lrefs[0].shape[-1], rrefs[0].shape[-1]
    nl, nr = len(lrefs), len(rrefs)

    def kernel(*refs):
        flag_ref = refs[0]
        ls, rs = refs[1 : 1 + nl], refs[1 + nl : 1 + nl + nr]
        keep_ref, give_ref, acc, lbuf, rbuf, lsem, rsem = refs[1 + nl + nr :]
        i = pl.program_id(0)

        def fetch(step):
            lk, lj = lpicks[step]
            rk, rj = rpicks[step]
            lsrc = ls[lk] if lj is None else ls[lk].at[lj]
            rsrc = rs[rk] if rj is None else rs[rk].at[rj]
            pltpu.make_async_copy(lsrc, lbuf.at[step], lsem.at[step]).start()
            pltpu.make_async_copy(rsrc, rbuf.at[step], rsem.at[step]).start()

        @pl.when(i == 0)
        def _():
            for step in range(count):
                fetch(step)

        lany = ls[0] if lpicks[0][1] is None else ls[0].at[0]
        rany = rs[0] if rpicks[0][1] is None else rs[0].at[0]
        pltpu.make_async_copy(lany, lbuf.at[i], lsem.at[i]).wait()
        pltpu.make_async_copy(rany, rbuf.at[i], rsem.at[i]).wait()
        product = dot_tn(lbuf[i], rbuf[i])

        @pl.when(i == 0)
        def _():
            acc[...] = product

        @pl.when(i > 0)
        def _():
            acc[...] += product

        @pl.when(i == count - 1)
        def _():
            mine = flag_ref[1]
            keep_ref[...] = acc[pl.ds(pl.multiple_of(mine * (m // 2), m // 2), m // 2), :].astype(
                BF16
            )
            give_ref[...] = acc[
                pl.ds(pl.multiple_of((1 - mine) * (m // 2), m // 2), m // 2), :
            ].astype(BF16)

    full = pl.BlockSpec((m // 2, n), lambda i: (0, 0))
    return pl.pallas_call(
        kernel,
        grid=(count,),
        in_specs=[SMEM] + [ANY] * (nl + nr),
        out_specs=[full, full],
        out_shape=[shape((m // 2, n), BF16)] * 2,
        scratch_shapes=[
            pltpu.VMEM((m, n), F32),
            pltpu.VMEM((count, rows, m), BF16),
            pltpu.VMEM((count, rows, n), BF16),
            pltpu.SemaphoreType.DMA((count,)),
            pltpu.SemaphoreType.DMA((count,)),
        ],
        compiler_params=params(40),
        cost_estimate=cost(2 * count * rows * m * n * 2, 2 * count * rows * (m + n)),
    )(flag, *lrefs, *rrefs)


def split_sum(keep, got, flag, nz):
    rows, width = keep.shape
    piece = rows // nz

    def kernel(flag_ref, a_ref, b_ref, *outs):
        own = flag_ref[2]
        for k in range(nz):
            at = pl.ds(pl.multiple_of((own ^ k) * piece, piece), piece)
            outs[k][...] = (a_ref[at, :].astype(F32) + b_ref[at, :].astype(F32)).astype(BF16)

    return pl.pallas_call(
        kernel,
        in_specs=[SMEM, VMEM, VMEM],
        out_specs=[VMEM] * nz,
        out_shape=[shape((piece, width), BF16)] * nz,
        compiler_params=params(16),
        cost_estimate=cost(0, rows * width * 6),
    )(flag, keep, got)


def add_all(values):
    rows, width = values[0].shape

    def kernel(*refs):
        total = refs[0][...].astype(F32)
        for ref in refs[1:-1]:
            total = total + ref[...].astype(F32)
        refs[-1][...] = total.astype(BF16)

    return pl.pallas_call(
        kernel,
        in_specs=[VMEM] * len(values),
        out_specs=VMEM,
        out_shape=shape((rows, width), BF16),
        compiler_params=params(16),
        cost_estimate=cost(0, rows * width * 2 * len(values)),
    )(*values)


def join(values, flag):
    piece, width = values[0].shape
    nz = len(values)

    def kernel(flag_ref, *refs):
        own = flag_ref[2]
        for k in range(nz):
            at = pl.ds(pl.multiple_of((own ^ k) * piece, piece), piece)
            refs[-1][at, :] = refs[k][...]

    return pl.pallas_call(
        kernel,
        in_specs=[SMEM] + [VMEM] * nz,
        out_specs=VMEM,
        out_shape=shape((nz * piece, width), BF16),
        compiler_params=params(16),
        cost_estimate=cost(0, nz * piece * width * 4),
    )(flag, *values)


def unpack(half, other, flag):
    rows, width = half.shape

    def kernel(flag_ref, a_ref, b_ref, o_ref):
        mine = flag_ref[1]
        o_ref[pl.ds(pl.multiple_of(mine * rows, rows), rows), :] = a_ref[...].astype(F32)
        o_ref[pl.ds(pl.multiple_of((1 - mine) * rows, rows), rows), :] = b_ref[...].astype(F32)

    return pl.pallas_call(
        kernel,
        in_specs=[SMEM, VMEM, VMEM],
        out_specs=VMEM,
        out_shape=shape((2 * rows, width), F32),
        compiler_params=params(24),
        cost_estimate=cost(0, rows * width * 12),
    )(flag, half, other)


def reduce_dp(keep, give, flag, nz):
    got = flip(give, "dp", 1)
    pieces = split_sum(keep, got, flag, nz)
    parts = [pieces[0]] + [flip(pieces[k], "dp", 2 * k) for k in range(1, nz)]
    own = add_all(parts)
    half = join([own] + [flip(own, "dp", 2 * k) for k in range(1, nz)], flag)
    return unpack(half, flip(half, "dp", 1), flag)


def body(
    tokens,
    lengths,
    cotangent,
    attn_gain,
    in_weights,
    ssm_rate,
    ssm_input,
    ssm_output,
    ctx_weights,
    out_weights,
    mlp_gain,
    up_weights,
    down_weights,
):
    count, rows, width = tokens.shape
    chans = out_weights.shape[0]
    nz = lax.axis_size("dp") // 2
    dp = lax.axis_index("dp")
    flag = jnp.stack([lax.axis_index("mp"), dp % 2, dp // 2]).astype(jnp.int32)
    lens = lengths[0]
    flat_in = in_weights.reshape(width, 4 * chans)
    gain_one = attn_gain.reshape(1, width)
    gain_two = mlp_gain.reshape(1, width)
    ssm = (ssm_rate, ssm_input, ssm_output)
    micros = range(count)

    normed = [gather_mp(norm_one(tokens, gain_one, m)) for m in micros]
    cots = [gather_mp(cotangent[m]) for m in micros]
    saved, heads_out, middles, normed_two = [], [], [], []
    for m in micros:
        *kept, ho, keep, give = attn_forward(
            normed[m], flat_in, *ssm, ctx_weights, out_weights, lens, flag, m
        )
        saved.append(kept)
        heads_out.append(ho)
        middle, low = norm_two(tokens, *scatter_mp(keep, give), gain_two, m)
        middles.append(middle)
        normed_two.append(gather_mp(low))
    hidden, grad_before, grad_mid, branch, gain_two_parts = [], [], [], [], []
    mixed = None
    for m in micros:
        hid, gb, fk, fg, gk, gg = feed(normed_two[m], cots[m], up_weights, down_weights)
        hidden.append(hid)
        grad_before.append(gb)
        gm, low, part = norm_two_back(
            middles[m], *scatter_mp(gk, gg), cotangent, gain_two, m
        )
        grad_mid.append(gm)
        gain_two_parts.append(part)
        branch.append(gather_mp(low))
        mixed = mix_out(middles[m], *scatter_mp(fk, fg), mixed, m, count)
    natural, mixed_order = (0, 1, 2, 3), (0, 2, 1, 3)
    up_parts = weight_grad(normed_two, grad_before, mixed_order, natural, flag)
    grad_up = reduce_dp(*up_parts, flag, nz)
    down_parts = weight_grad(hidden, cots, natural, mixed_order, flag)
    grad_down = reduce_dp(*down_parts, flag, nz)
    grad_proj, small, gain_one_parts = [], [], []
    grad_tokens = None
    for m in micros:
        gp, keep, give, gcw, gs = attn_backward(
            branch[m], saved[m], flat_in, *ssm, ctx_weights, out_weights, flag
        )
        grad_proj.append(gp)
        small.append((gcw, gs))
        grad_tokens, part = norm_one_back(
            tokens, *scatter_mp(keep, give), grad_mid[m], gain_one, grad_tokens, m, count
        )
        gain_one_parts.append(part)
    in_parts = weight_grad(normed, grad_proj, natural, natural, flag)
    grad_in = reduce_dp(*in_parts, flag, nz)
    out_parts = weight_grad(heads_out, branch, natural, natural, flag)
    grad_out = reduce_dp(*out_parts, flag, nz)

    gcw = functools.reduce(lambda a, b: a + b, [s[0] for s in small])
    gs = functools.reduce(lambda a, b: a + b, [s[1] for s in small])
    gains = jnp.concatenate(
        [
            functools.reduce(lambda a, b: a + b, gain_one_parts),
            functools.reduce(lambda a, b: a + b, gain_two_parts),
        ]
    )
    gains = gains + flip(gains, "mp", 1)
    gains = gains + flip(gains, "mp", 2)
    packed = jnp.concatenate(
        [gcw.reshape(-1, width), gs.reshape(-1, width), gains], axis=0
    ).astype(BF16)
    need = packed.shape[0]
    unit = 2 * nz * 16
    padded = jnp.pad(packed, ((0, -need % unit), (0, 0)))
    two = padded.reshape(2, padded.shape[0] // 2, width)
    pack = reduce_dp(
        lax.dynamic_index_in_dim(two, dp % 2, keepdims=False),
        lax.dynamic_index_in_dim(two, 1 - dp % 2, keepdims=False),
        flag,
        nz,
    )
    n_ctx = gcw.size // width
    n_ssm = gs.size // width
    grad_ctx = pack[:n_ctx].reshape(gcw.shape)
    grad_ssm = pack[n_ctx : n_ctx + n_ssm].reshape(gs.shape)
    return (
        mixed,
        grad_tokens,
        pack[n_ctx + n_ssm],
        grad_in.reshape(in_weights.shape),
        grad_ssm[0],
        grad_ssm[1],
        grad_ssm[2],
        grad_ctx,
        grad_out,
        pack[n_ctx + n_ssm + 1],
        grad_up,
        grad_down,
    )


def solution(mesh):
    rows = P(None, ("dp", "mp"), None)
    return jax.shard_map(
        body,
        mesh=mesh,
        in_specs=(
            rows,
            P("dp", None, None),
            rows,
            P(),
            P(None, None, "mp"),
            P(None, "mp"),
            P(None, "mp"),
            P(None, "mp"),
            P("mp", None, None),
            P("mp", None),
            P(),
            P(None, "mp"),
            P("mp", None),
        ),
        out_specs=(
            rows,
            rows,
            P(),
            P(None, None, "mp"),
            P(None, "mp"),
            P(None, "mp"),
            P(None, "mp"),
            P("mp", None, None),
            P("mp", None),
            P(),
            P(None, "mp"),
            P("mp", None),
        ),
        check_vma=False,
    )
```

```python
import functools
import math

import jax
import jax.numpy as jnp
from jax import lax
from jax.experimental import pallas as pl
from jax.experimental.pallas import tpu as pltpu
from jax.sharding import PartitionSpec as P

HD = 128
BLK = 512
CTX = 128
HEAD = BLK - CTX
NS = 16
EPS = 1e-05
SCALE = 1.0 / math.sqrt(HD)
SCALE2 = SCALE * math.log2(math.e)
NEG = -1e30
F32 = jnp.float32
BF16 = jnp.bfloat16

VMEM = pl.BlockSpec(memory_space=pltpu.VMEM)
SMEM = pl.BlockSpec(memory_space=pltpu.SMEM)
ANY = pl.BlockSpec(memory_space=pl.ANY)


def params(mib):
    return pltpu.CompilerParams(vmem_limit_bytes=mib << 20)


def cost(flops, nbytes):
    return pl.CostEstimate(flops=int(flops), bytes_accessed=int(nbytes), transcendentals=0)


def dot(a, b):
    return lax.dot_general(a, b, (((1,), (0,)), ((), ())), preferred_element_type=F32)


def dot_nt(a, b):
    return lax.dot_general(a, b, (((1,), (1,)), ((), ())), preferred_element_type=F32)


def dot_tn(a, b):
    return lax.dot_general(a, b, (((0,), (0,)), ((), ())), preferred_element_type=F32)


def shape(dims, kind):
    return jax.ShapeDtypeStruct(dims, kind)


def triangle(upper):
    row = lax.broadcasted_iota(jnp.int32, (CTX, 2 * CTX), 0)
    col = lax.broadcasted_iota(jnp.int32, (CTX, 2 * CTX), 1) % CTX
    keep = (row <= col) if upper else (row >= col)
    return jnp.where(keep, 1.0, 0.0).astype(BF16)


def running(tri, values):
    high = values.astype(BF16)
    rest = (values - high.astype(F32)).astype(BF16)
    return dot(tri, jnp.concatenate([high, rest], axis=0))


def head_sums(u_ref, rate_ref, moment):
    width = rate_ref.shape[1]
    place = lax.broadcasted_iota(jnp.int32, (8, width), 0).astype(F32)
    sums, moments = [], []
    group = 4 if moment else 8
    for base in range(0, NS, group):
        rates = [rate_ref[n : n + 1, :] for n in range(base, base + group)]
        steps = [jnp.broadcast_to(jnp.exp(-8.0 * r), (8, width)) for r in rates]

        def body(chunk, carry):
            start = pl.multiple_of(chunk * 8, 8)
            rows = u_ref[pl.ds(start, 8), :]
            first = [acc * step + rows for acc, step in zip(carry[0], steps)]
            if not moment:
                return (first, carry[1])
            scaled = rows * (place + (chunk * 8 - HEAD).astype(F32))
            second = [acc * step + scaled for acc, step in zip(carry[1], steps)]
            return (first, second)

        zero = [jnp.zeros((8, width), F32) for _ in range(group)]
        first, second = lax.fori_loop(
            0, HEAD // 8, body, (zero, list(zero) if moment else []), unroll=4
        )
        for k, rate in enumerate(rates):
            last = jnp.exp(rate * (place - 8.0))
            sums.append(jnp.sum(first[k] * last, axis=0, keepdims=True))
            if moment:
                moments.append(jnp.sum(second[k] * last, axis=0, keepdims=True))
    return sums, moments


def state_forward(u_ref, rate_ref, in_ref, out_ref):
    width = rate_ref.shape[1]
    sums, _ = head_sums(u_ref, rate_ref, False)
    tail = u_ref[pl.ds(HEAD, CTX), :]
    time = lax.broadcasted_iota(jnp.int32, (CTX, width), 0).astype(F32)
    tri = triangle(False)
    total = jnp.zeros((CTX, width), F32)
    for n in range(NS):
        rate = rate_ref[n : n + 1, :]
        gain = in_ref[n : n + 1, :] * jnp.sqrt(1.0 - jnp.exp(-2.0 * rate))
        weight = gain * out_ref[n : n + 1, :]
        prefix = running(tri, jnp.exp(rate * time) * tail)
        total = total + weight * (jnp.exp(-rate * time) * (sums[n] + prefix))
    return total


def state_backward(grad, u_ref, du_ref, rate_ref, in_ref, out_ref, gs_ref):
    width = rate_ref.shape[1]
    sums, moments = head_sums(u_ref, rate_ref, True)
    tail = u_ref[pl.ds(HEAD, CTX), :]
    time = lax.broadcasted_iota(jnp.int32, (CTX, width), 0).astype(F32)
    place = lax.broadcasted_iota(jnp.int32, (8, width), 0).astype(F32)
    lower, upper = triangle(False), triangle(True)
    total = jnp.zeros((CTX, width), F32)
    starts = []
    for n in range(NS):
        rate = rate_ref[n : n + 1, :]
        root = jnp.sqrt(1.0 - jnp.exp(-2.0 * rate))
        enter = in_ref[n : n + 1, :]
        leave = out_ref[n : n + 1, :]
        gain = enter * root
        rising = jnp.exp(rate * time)
        driven = rising * tail
        states = sums[n] + running(lower, driven)
        seen = jnp.exp(-rate * time) * grad
        later = running(upper, seen)
        product = seen * states
        energy = jnp.sum(product, axis=0, keepdims=True)
        slope = jnp.sum(time * (product - driven * later), axis=0, keepdims=True)
        slope = slope - later[0:1] * moments[n]
        total = total + (gain * leave) * (rising * later)
        starts.append((gain * leave) * later[0:1])
        gs_ref[0, n : n + 1, :] = leave * (
            energy * enter * jnp.exp(-2.0 * rate) / root - gain * slope
        )
        gs_ref[1, n : n + 1, :] = leave * energy * root
        gs_ref[2, n : n + 1, :] = gain * energy
    du_ref[pl.ds(HEAD, CTX), :] = total
    group = 8
    for base in range(0, NS, group):
        rates = [rate_ref[n : n + 1, :] for n in range(base, base + group)]
        steps = [jnp.broadcast_to(jnp.exp(-8.0 * r), (8, width)) for r in rates]
        begin = [
            starts[base + k] * jnp.exp(rate * (place - 8.0)) for k, rate in enumerate(rates)
        ]

        def body(index, carry):
            start = pl.multiple_of(HEAD - 8 - index * 8, 8)
            value = functools.reduce(lambda a, b: a + b, carry)
            if base:
                value = value + du_ref[pl.ds(start, 8), :]
            du_ref[pl.ds(start, 8), :] = value
            return [c * step for c, step in zip(carry, steps)]

        lax.fori_loop(0, HEAD // 8, body, begin, unroll=4)


def layout_scalars(len_ref, micro):
    first, second = len_ref[micro, 0], len_ref[micro, 1]
    first_blocks = (first + (BLK - 1)) // BLK
    second_blocks = (second + (BLK - 1)) // BLK
    docs, valid = [], []
    for b in range(2):
        doc = jnp.where(b < first_blocks, 0, jnp.where(b < first_blocks + second_blocks, 1, 2))
        start = jnp.where(doc == 0, 0, first_blocks)
        extent = jnp.where(doc == 0, first, jnp.where(doc == 1, second, 0))
        docs.append(doc)
        valid.append(extent - (b - start) * BLK)
    return valid, docs[0] == docs[1]


class Copies:
    def __init__(self, send, recv):
        self.send, self.recv, self.used, self.open = send, recv, 0, []

    def start(self, source, target, device):
        copy = pltpu.make_async_remote_copy(
            src_ref=source,
            dst_ref=target,
            send_sem=self.send.at[self.used],
            recv_sem=self.recv.at[self.used],
            device_id=device,
            device_id_type=pl.DeviceIdType.MESH,
        )
        self.used += 1
        copy.start()
        self.open.append(copy)
        return copy

    def sent(self, copy):
        copy.wait_send()
        self.open = [other for other in self.open if other is not copy]

    def drain(self):
        for copy in self.open:
            copy.wait_send()
        self.open = []


class Moves:
    def __init__(self, sems):
        self.sems, self.used = sems, 0

    def start(self, source, target):
        copy = pltpu.make_async_copy(source, target, self.sems.at[self.used])
        self.used += 1
        copy.start()
        return copy


def layer(
    nz, tokens, lengths, cotangent, gain_one, gain_two, w_in, ssm, ctx_w, w_out, w_up, w_down
):
    count, rows, width = tokens.shape
    chans = w_out.shape[0]
    heads = chans // HD
    hidden = w_up.shape[1]
    total = 4 * rows
    pair = 2 * rows
    small_rows = heads * CTX + 3 * NS + 8
    unit = 2 * nz * 16
    misc_rows = width + small_rows + (-small_rows % unit)
    sizes = dict(down=(hidden, width), up=(width, hidden), inp=(width, 4 * chans), misc=(misc_rows, chans))
    names = list(sizes)
    root = math.sqrt(2.0 / math.pi)
    n_remote = 51 + 4 * (1 + 2 * (nz - 1) + nz)
    n_local = 24 + 4 * nz

    def kernel(*refs):
        (
            len_ref, tok, cot_hbm, g1, g2, in_hbm, rate, enter, leave, cw, out_hbm, up_hbm, down_hbm,
        ) = refs[:13]
        mixed_hbm, gtok_hbm, pr_hbm = refs[13:16]
        grads = dict(zip(names, refs[16:20]))
        ry = dict(zip(names, refs[20:24]))
        rz = dict(zip(names, refs[24:28]))
        (
            w_i, w_o, w_u, w_d, xn, cot, n2, gbr, hid, gbf, qkv, u0, pr, ho, cx, ckv, dh, gctx,
            give, keep_a, keep_b, sib_a, sib_b, far_a, far_b, mid, acc, tmp, misc,
            gain_acc, gain_got, gcw, gss, send_sems, recv_sems, local_sems,
        ) = refs[28:]
        me = lax.axis_index("mp")
        core, chip = me % 2, me // 2
        near, far, both = chip * 2 + 1 - core, (1 - chip) * 2 + core, (1 - chip) * 2 + 1 - core
        dp = lax.axis_index("dp")
        y, z = dp % 2, dp // 2
        to_near, to_far, to_both = {"mp": near}, {"mp": far}, {"mp": both}
        to_y = {"dp": z * 2 + 1 - y}
        zs = [(z + k) % nz for k in range(nz)]
        to_z = [{"dp": zk * 2 + y} for zk in zs]
        remote, local = Copies(send_sems, recv_sems), Moves(local_sems)

        loads = {
            "in": local.start(in_hbm, w_i),
            "cot0": local.start(cot_hbm.at[0], cot.at[0, me]),
            "cot1": local.start(cot_hbm.at[1], cot.at[1, me]),
            "out": local.start(out_hbm, w_o),
            "up": local.start(up_hbm, w_u),
            "down": local.start(down_hbm, w_d),
        }
        barrier = pltpu.get_barrier_semaphore()
        for device in [to_near, to_far, to_both, to_y] + to_z[1:]:
            pl.semaphore_signal(
                barrier, inc=1, device_id=device, device_id_type=pl.DeviceIdType.MESH
            )
        pl.semaphore_wait(barrier, 3 + nz)

        def share(buf, m):
            return remote.start(buf.at[m, me], buf.at[m, me], to_near)

        def cross(buf, m):
            return remote.start(buf.at[m, me], buf.at[m, me], to_far)

        def pass_on(buf, m, copy):
            copy.wait_recv()
            return remote.start(buf.at[m, far], buf.at[m, far], to_near)

        def offer(kind, slot, sib, m):
            return remote.start(give.at[kind, slot], sib.at[m, slot], to_near)

        def by_rows(work):
            step = 64

            def body(i, carry):
                work(pl.ds(pl.multiple_of(i * step, step), step))
                return carry

            lax.fori_loop(0, rows // step, body, 0)

        def owed(offers, keep, sib, far_buf, m):
            offers[1].wait_recv()

            def work(at):
                keep[m, 1, at, :] = (
                    keep[m, 1, at, :].astype(F32) + sib[m, 1, at, :].astype(F32)
                ).astype(BF16)

            by_rows(work)
            return remote.start(keep.at[m, 1], far_buf.at[m], to_far)

        def summed(offers, copy, keep, sib, far_buf, m):
            offers[0].wait_recv()
            copy.wait_recv()
            return lambda at: (
                keep[m, 0, at, :].astype(F32)
                + sib[m, 0, at, :].astype(F32)
                + far_buf[m, at, :].astype(F32)
            )

        def inverse_root(value):
            return lax.rsqrt(jnp.mean(value * value, axis=-1, keepdims=True) + EPS)

        def norm_first(m):
            def work(at):
                x = tok[m, at, :].astype(F32)
                xn[m, me, at, :] = (x * inverse_root(x) * g1[...]).astype(BF16)

            by_rows(work)

        def norm_second(m, branch):
            def work(at):
                value = tok[m, at, :].astype(F32) + branch(at)
                mid[m, at, :] = value
                n2[m, me, at, :] = (value * inverse_root(value) * g2[...]).astype(BF16)

            by_rows(work)

        def pulled(value, grad, gain, line):
            scale = inverse_root(value)
            unit_row = value * scale
            gain_acc[line : line + 1, :] += jnp.sum(grad * unit_row, axis=0, keepdims=True)
            inner = grad * gain[...]
            return scale * (inner - unit_row * jnp.mean(inner * unit_row, axis=-1, keepdims=True))

        def norm_second_back(m, grad):
            def work(at):
                value = cot[m, me, at, :].astype(F32) + pulled(mid[m, at, :], grad(at), g2, 1)
                gbr[m, me, at, :] = value.astype(BF16)

            by_rows(work)

        def norm_first_back(m, grad):
            def work(at):
                x = tok[m, at, :].astype(F32)
                mid[m, at, :] = gbr[m, me, at, :].astype(F32) + pulled(x, grad(at), g1, 0)

            by_rows(work)
            return local.start(mid.at[m], gtok_hbm.at[m])

        def mix(m, branch):
            def work(at):
                keep_a[m, 0, at, :] = (mid[m, at, :] + branch(at)).astype(BF16)

            by_rows(work)
            return local.start(keep_a.at[m, 0], mixed_hbm.at[m])

        def project(m, side):
            def body(i, carry):
                t = side * 2 + i
                at = pl.ds(pl.multiple_of(t * rows, rows), rows)
                x = xn[m, t]
                qkv[m, at, :] = dot(x, w_i[:, : 3 * chans]).astype(BF16)

                @pl.when(t < 2)
                def _():
                    u0[m, at, :] = dot(x, w_i[:, 3 * chans :])

                return carry

            lax.fori_loop(0, 2, body, 0)

        def scan(m):
            context = state_forward(u0.at[m], rate, enter, leave).astype(BF16)
            cx[m] = context
            for h in range(heads):
                ckv[m, h] = dot(context[:, h * HD : (h + 1) * HD], cw[h]).astype(BF16)

        def attend(m):
            valid, linked = layout_scalars(len_ref, m)
            for h in range(heads):
                lanes = slice(h * HD, (h + 1) * HD)
                klanes = slice(chans + h * HD, chans + (h + 1) * HD)
                vlanes = slice(2 * chans + h * HD, 2 * chans + (h + 1) * HD)
                for b in range(2):
                    for half in range(2):
                        row0 = half * rows
                        keys = row0 + rows
                        spot = b * BLK + row0
                        q = qkv[m, spot : spot + rows, lanes]
                        k = qkv[m, b * BLK : b * BLK + keys, klanes]
                        v = qkv[m, b * BLK : b * BLK + keys, vlanes]
                        s = dot_nt(q, k) * SCALE2
                        row = lax.broadcasted_iota(jnp.int32, (rows, keys), 0) + row0
                        col = lax.broadcasted_iota(jnp.int32, (rows, keys), 1)
                        allowed = (col < jnp.minimum(row, valid[b])) | (col == row)
                        s = jnp.where(allowed, s, NEG)
                        peak = jnp.max(s, axis=-1, keepdims=True)
                        if b:
                            sc = dot_nt(q, ckv[m, h, :, :HD]) * SCALE2
                            sc = jnp.where(linked, sc, NEG)
                            peak = jnp.maximum(peak, jnp.max(sc, axis=-1, keepdims=True))
                            ec = jnp.exp2(sc - peak)
                        e = jnp.exp2(s - peak)
                        norm = jnp.sum(e, axis=-1, keepdims=True)
                        if b:
                            norm = norm + jnp.sum(ec, axis=-1, keepdims=True)
                        inverse = 1.0 / norm
                        p = (e * inverse).astype(BF16)
                        pr[h, b, row0 : row0 + rows, CTX : CTX + keys] = p
                        o = dot(p, v)
                        if b:
                            pc = (ec * inverse).astype(BF16)
                            pr[h, b, row0 : row0 + rows, :CTX] = pc
                            o = o + dot(pc, ckv[m, h, :, HD:])
                        ho[m, 2 * b + half, :, lanes] = o.astype(BF16)

        def spread(product, keep, kind, sib, m, before):
            for copy in before:
                remote.sent(copy)
            give[kind, 1] = product(both).astype(BF16)
            second = offer(kind, 1, sib, m)
            give[kind, 0] = product(near).astype(BF16)
            first = offer(kind, 0, sib, m)
            keep[m, 1] = product(far).astype(BF16)
            keep[m, 0] = product(me).astype(BF16)
            return [first, second]

        def feed(m, side, other):
            slot = 1 if other else 0

            def body(i, carry):
                t = side * 2 + jnp.where(i == 0, 1 - core, core)
                for start in range(0, hidden, 256):
                    cut = slice(start, start + 256)
                    before = dot(n2[m, t], w_u[:, cut])
                    square = before * before
                    th = jnp.tanh(root * (before * (1.0 + 0.044715 * square)))
                    half = 0.5 + 0.5 * th
                    hid[m, t, :, cut] = (before * half).astype(BF16)
                    slope = half + (0.5 * root) * before * (1.0 - th * th) * (
                        1.0 + 0.134145 * square
                    )
                    gbf[m, t, :, cut] = (dot_nt(cot[m, t], w_d[cut, :]) * slope).astype(BF16)
                branch = dot(hid[m, t], w_d[...]).astype(BF16)
                gn = dot_nt(gbf[m, t], w_u[...]).astype(BF16)

                @pl.when(i == 0)
                def _():
                    give[0, slot] = branch
                    give[1, slot] = gn

                @pl.when(i == 1)
                def _():
                    keep_a[m, slot] = branch
                    keep_b[m, slot] = gn

                return carry

            lax.fori_loop(0, 2, body, 0)
            return offer(0, slot, sib_a, m), offer(1, slot, sib_b, m)

        def heads_back(m, side):
            def body(i, carry):
                t = side * 2 + i
                at = pl.ds(pl.multiple_of(t * rows, rows), rows)
                dh[at, :] = dot_nt(gbr[m, t], w_o[...]).astype(BF16)
                return carry

            lax.fori_loop(0, 2, body, 0)

        def attend_back(m):
            for h in range(heads):
                lanes = slice(h * HD, (h + 1) * HD)
                klanes = slice(chans + h * HD, chans + (h + 1) * HD)
                vlanes = slice(2 * chans + h * HD, 2 * chans + (h + 1) * HD)
                for b in range(2):
                    grad_k, grad_v = [None, None], [None, None]
                    grad_c = grad_cv = None
                    for half in (1, 0):
                        row0 = half * rows
                        keys = row0 + rows
                        spot = slice(b * BLK + row0, b * BLK + row0 + rows)
                        go = dh[spot, lanes]
                        qh = qkv[m, spot, lanes]
                        kh = qkv[m, b * BLK : b * BLK + keys, klanes]
                        vh = qkv[m, b * BLK : b * BLK + keys, vlanes]
                        p = pr[h, b, row0 : row0 + rows, CTX : CTX + keys]
                        pf = p.astype(F32)
                        dprob = dot_nt(go, vh)
                        delta = jnp.sum(dprob * pf, axis=-1, keepdims=True)
                        if b:
                            pc = pr[h, b, row0 : row0 + rows, :CTX]
                            pcf = pc.astype(F32)
                            dpc = dot_nt(go, ckv[m, h, :, HD:])
                            delta = delta + jnp.sum(dpc * pcf, axis=-1, keepdims=True)
                            dsc = (pcf * (dpc - delta)).astype(BF16)
                        ds = (pf * (dprob - delta)).astype(BF16)
                        dq = dot(ds, kh)
                        if b:
                            dq = dq + dot(dsc, ckv[m, h, :, :HD])
                            one = dot_tn(dsc, qh)
                            two = dot_tn(pc, go)
                            grad_c = one if grad_c is None else grad_c + one
                            grad_cv = two if grad_cv is None else grad_cv + two
                        hid[m, 2 * b + half, :, lanes] = (dq * SCALE).astype(BF16)
                        dk = dot_tn(ds, qh)
                        dv = dot_tn(p, go)
                        if half:
                            grad_k = [dk[:rows], dk[rows:]]
                            grad_v = [dv[:rows], dv[rows:]]
                        else:
                            grad_k[0] = grad_k[0] + dk
                            grad_v[0] = grad_v[0] + dv
                    for part in range(2):
                        t = 2 * b + part
                        hid[m, t, :, klanes] = (grad_k[part] * SCALE).astype(BF16)
                        hid[m, t, :, vlanes] = grad_v[part].astype(BF16)
                    if b:
                        low_c = (grad_c * SCALE).astype(BF16)
                        low_cv = grad_cv.astype(BF16)
                        ch = cx[m, :, lanes]
                        gcw[m, h, :, :HD] = dot_tn(ch, low_c)
                        gcw[m, h, :, HD:] = dot_tn(ch, low_cv)
                        gctx[:, lanes] = dot_nt(low_c, cw[h, :, :HD]) + dot_nt(
                            low_cv, cw[h, :, HD:]
                        )

        def scan_back(m):
            state_backward(gctx[...], u0.at[m], u0.at[m], rate, enter, leave, gss.at[m])
            for t in range(2):
                hid[m, t, :, 3 * chans :] = u0[m, t * rows : (t + 1) * rows, :].astype(BF16)
                hid[m, 2 + t, :, 3 * chans :] = jnp.zeros((rows, chans), BF16)

        def gather_tile(left, right, tile):
            lanes = pl.ds(pl.multiple_of(tile * rows, rows), rows)
            acc[...] = jnp.zeros_like(acc)

            def body(i, carry):
                m, t = i // 4, i % 4
                acc[...] += dot_tn(left[m, t, :, lanes], right[m, t])
                return carry

            lax.fori_loop(0, 4 * count, body, 0)

        def tiles(left, right, stage, which):
            span = stage.shape[0] // (2 * rows)

            def body(i, carry):
                tile = which * span + i
                gather_tile(left, right, tile)
                at = pl.ds(pl.multiple_of(tile * rows, rows), rows)
                stage[at, :] = acc[...].astype(BF16)
                return carry

            lax.fori_loop(0, span, body, 0)

        def part(ref, start, size):
            return ref.at[pl.ds(pl.multiple_of(start, 16), size), :]

        def swap_y(name, stage):
            span = sizes[name][0] // 2
            return remote.start(part(stage, (1 - y) * span, span), ry[name], to_y)

        def landing(name, row, size):
            if sizes[name][1] != width:
                return tmp.at[pl.ds(row, size), :]
            return gbf.at[0, row // rows, pl.ds(row % rows, size), :]

        def sum_y(name, stage, copy):
            span = sizes[name][0] // 2
            piece, block = span // nz, min(span, rows) if sizes[name][1] == width else span
            copy.wait_recv()
            spots = range(0, span, block)
            moves = [
                local.start(ry[name].at[pl.ds(row, block), :], landing(name, row, block))
                for row in spots
            ]
            for row, move in zip(spots, moves):
                move.wait()
                at = pl.ds(pl.multiple_of(y * span + row, 16), block)
                got = landing(name, row, block)
                stage[at, :] = (stage[at, :].astype(F32) + got[...].astype(F32)).astype(BF16)
            return [
                remote.start(part(stage, y * span + zs[k] * piece, piece), rz[name].at[k - 1], to_z[k])
                for k in range(1, nz)
            ]

        def sum_z(name, stage, copies):
            span = sizes[name][0] // 2
            piece = span // nz
            for copy in copies:
                copy.wait_recv()
            moves = [
                local.start(rz[name].at[k], landing(name, k * piece, piece)) for k in range(nz - 1)
            ]
            for move in moves:
                move.wait()
            spot = y * span + z * piece
            at = pl.ds(pl.multiple_of(spot, 16), piece)
            value = stage[at, :].astype(F32)
            for k in range(nz - 1):
                value = value + landing(name, k * piece, piece)[...].astype(F32)
            stage[at, :] = value.astype(BF16)
            mine = part(stage, spot, piece)
            place = part(grads[name], spot, piece)
            outs = [remote.start(mine, place, to_z[k]) for k in range(1, nz)]
            last = [remote.start(mine, place, to_y)]
            return outs, last, local.start(mine, place)

        def spread_y(name, state):
            high, _ = sizes[name]
            span, piece = high // 2, high // 2 // nz
            outs, last, move = state
            for k in range(1, nz):
                outs[k - 1].wait_recv()
                place = part(grads[name], y * span + ((z + nz - k) % nz) * piece, piece)
                last.append(remote.start(place, place, to_y))
            return last, move

        def finish(state):
            last, move = state
            for copy in last:
                copy.wait_recv()
            move.wait()

        gain_acc[...] = jnp.zeros_like(gain_acc)
        norm_first(0)
        n_near = [share(xn, 0), None]
        n_far = [cross(xn, 0), None]
        norm_first(1)
        n_near[1] = share(xn, 1)
        loads["cot0"].wait()
        loads["cot1"].wait()
        c_near = [share(cot, 0), share(cot, 1)]
        loads["in"].wait()
        n_near[0].wait_recv()
        project(0, chip)
        n_both = [pass_on(xn, 0, n_far[0]), None]
        n_far[1] = cross(xn, 1)
        n_both[0].wait_recv()
        project(0, 1 - chip)
        scan(0)
        attend(0)
        save = local.start(pr, pr_hbm.at[0])
        n_both[1] = pass_on(xn, 1, n_far[1])
        c_far = [cross(cot, 0), None]
        loads["out"].wait()
        offers = [spread(lambda t: dot(ho[0, t], w_o[...]), keep_a, 0, sib_a, 0, []), None]
        n_near[1].wait_recv()
        project(1, chip)
        branch_far = [owed(offers[0], keep_a, sib_a, far_a, 0), None]
        n_both[1].wait_recv()
        project(1, 1 - chip)
        scan(1)
        save.wait()
        attend(1)
        save = local.start(pr, pr_hbm.at[1])
        c_both = [pass_on(cot, 0, c_far[0]), None]
        offers[1] = spread(
            lambda t: dot(ho[1, t], w_o[...]), keep_a, 0, sib_a, 1, offers[0]
        )
        branch_far[1] = owed(offers[1], keep_a, sib_a, far_a, 1)
        norm_second(0, summed(offers[0], branch_far[0], keep_a, sib_a, far_a, 0))
        m_near = [share(n2, 0), None]
        m_far = [cross(n2, 0), None]
        loads["up"].wait()
        loads["down"].wait()
        c_near[0].wait_recv()
        m_near[0].wait_recv()
        for copy in offers[1]:
            remote.sent(copy)
        remote.sent(branch_far[0])
        feed_offers = [[None, None], [None, None]]
        first = feed(0, chip, False)
        norm_second(1, summed(offers[1], branch_far[1], keep_a, sib_a, far_a, 1))
        m_near[1] = share(n2, 1)
        m_both = [pass_on(n2, 0, m_far[0]), None]
        m_far[1] = cross(n2, 1)
        c_far[1] = cross(cot, 1)
        c_both[0].wait_recv()
        m_both[0].wait_recv()
        second = feed(0, 1 - chip, True)
        out_offers = [(first[0], second[0]), None]
        back_offers = [(first[1], second[1]), None]
        back_far = [owed(back_offers[0], keep_b, sib_b, far_b, 0), None]
        c_near[1].wait_recv()
        m_near[1].wait_recv()
        remote.sent(branch_far[1])
        for copy in (first[0], first[1]):
            remote.sent(copy)
        first = feed(1, chip, False)
        m_both[1] = pass_on(n2, 1, m_far[1])
        c_both[1] = pass_on(cot, 1, c_far[1])
        m_both[1].wait_recv()
        c_both[1].wait_recv()
        for copy in (second[0], second[1]):
            remote.sent(copy)
        second = feed(1, 1 - chip, True)
        out_offers[1] = (first[0], second[0])
        back_offers[1] = (first[1], second[1])
        back_far[1] = owed(back_offers[1], keep_b, sib_b, far_b, 1)
        save.wait()
        fetch = local.start(pr_hbm.at[0], pr)
        norm_second_back(0, summed(back_offers[0], back_far[0], keep_b, sib_b, far_b, 0))
        b_near = [share(gbr, 0), None]
        b_far = [cross(gbr, 0), None]
        tiles(hid, cot, w_d, 1 - y)
        down = swap_y("down", w_d)
        out_far = [owed(out_offers[0], keep_a, sib_a, far_a, 0), None]
        norm_second_back(1, summed(back_offers[1], back_far[1], keep_b, sib_b, far_b, 1))
        b_near[1] = share(gbr, 1)
        b_both = [pass_on(gbr, 0, b_far[0]), None]
        b_far[1] = cross(gbr, 1)
        tiles(hid, cot, w_d, y)
        tiles(n2, gbf, w_u, 1 - y)
        up = swap_y("up", w_u)
        tiles(n2, gbf, w_u, y)
        for copy in (first[0], first[1], second[0], second[1], back_far[0]):
            remote.sent(copy)
        b_near[0].wait_recv()
        b_both[0].wait_recv()
        heads_back(0, 0)
        heads_back(0, 1)
        fetch.wait()
        attend_back(0)
        fetch = local.start(pr_hbm.at[1], pr)
        b_both[1] = pass_on(gbr, 1, b_far[1])
        scan_back(0)
        norm_offers = [
            spread(lambda t: dot_nt(hid[0, t], w_i[...]), keep_b, 1, sib_b, 0, []),
            None,
        ]
        down = sum_y("down", w_d, down)
        norm_far = [owed(norm_offers[0], keep_b, sib_b, far_b, 0), None]
        b_near[1].wait_recv()
        b_both[1].wait_recv()
        heads_back(1, 0)
        heads_back(1, 1)
        fetch.wait()
        attend_back(1)
        scan_back(1)
        remote.sent(back_far[1])
        norm_offers[1] = spread(
            lambda t: dot_nt(hid[1, t], w_i[...]), keep_b, 1, sib_b, 1, norm_offers[0]
        )
        up = sum_y("up", w_u, up)
        norm_far[1] = owed(norm_offers[1], keep_b, sib_b, far_b, 1)
        out_far[1] = owed(out_offers[1], keep_a, sib_a, far_a, 1)
        tiles(xn, hid, w_i, 1 - y)
        inp = swap_y("inp", w_i)
        down = sum_z("down", w_d, down)
        tiles(xn, hid, w_i, y)
        gather_tile(ho, gbr, 0)
        for j in range(width // chans):
            misc[j * chans : (j + 1) * chans, :] = acc[:, j * chans : (j + 1) * chans].astype(BF16)
        ends = [mix(0, summed(out_offers[0], out_far[0], keep_a, sib_a, far_a, 0))]
        ends.append(
            norm_first_back(0, summed(norm_offers[0], norm_far[0], keep_b, sib_b, far_b, 0))
        )
        down = spread_y("down", down)
        ends.append(mix(1, summed(out_offers[1], out_far[1], keep_a, sib_a, far_a, 1)))
        ends.append(
            norm_first_back(1, summed(norm_offers[1], norm_far[1], keep_b, sib_b, far_b, 1))
        )
        gains = [
            remote.start(gain_acc, gain_got.at[k], device)
            for k, device in enumerate((to_near, to_far, to_both))
        ]
        up = sum_z("up", w_u, up)
        base = width
        for h in range(heads):
            misc[base + h * CTX : base + (h + 1) * CTX, :] = (gcw[0, h] + gcw[1, h]).astype(BF16)
        base += heads * CTX
        for k in range(3):
            misc[base + k * NS : base + (k + 1) * NS, :] = (gss[0, k] + gss[1, k]).astype(BF16)
        base += 3 * NS
        for copy in gains:
            copy.wait_recv()
        value = gain_acc[...] + gain_got[0] + gain_got[1] + gain_got[2]
        tail_rows = misc_rows - base
        line = jnp.concatenate(
            [value[r : r + 1, j * chans : (j + 1) * chans] for r in range(2) for j in range(4)],
            axis=0,
        )
        misc[base:, :] = jnp.concatenate(
            [line, jnp.zeros((tail_rows - 8, chans), F32)], axis=0
        ).astype(BF16)
        mis = swap_y("misc", misc)
        inp = sum_y("inp", w_i, inp)
        up = spread_y("up", up)
        mis = sum_y("misc", misc, mis)
        inp = sum_z("inp", w_i, inp)
        mis = sum_z("misc", misc, mis)
        inp = spread_y("inp", inp)
        mis = spread_y("misc", mis)
        for state in (down, up, inp, mis):
            finish(state)
        for end in ends:
            end.wait()
        remote.drain()
        assert remote.used <= n_remote and local.used <= n_local, (remote.used, local.used)

    pieces = (count, 4, rows)
    vm = pltpu.VMEM
    any_out = [
        shape((count, rows, width), BF16),
        shape((count, rows, width), F32),
        shape((count, heads, 2, BLK, BLK + CTX), BF16),
    ]
    any_out += [shape(sizes[n], BF16) for n in names]
    any_out += [shape((sizes[n][0] // 2, sizes[n][1]), BF16) for n in names]
    any_out += [
        shape((nz - 1, sizes[n][0] // 2 // nz, sizes[n][1]), BF16) for n in names
    ]
    results = pl.pallas_call(
        kernel,
        in_specs=[SMEM, VMEM, ANY, VMEM, VMEM, ANY, VMEM, VMEM, VMEM, VMEM, ANY, ANY, ANY],
        out_specs=[ANY] * len(any_out),
        out_shape=any_out,
        scratch_shapes=[
            vm(w_in.shape, BF16),
            vm(w_out.shape, BF16),
            vm(w_up.shape, BF16),
            vm(w_down.shape, BF16),
            vm(pieces + (width,), BF16),
            vm(pieces + (width,), BF16),
            vm(pieces + (width,), BF16),
            vm(pieces + (width,), BF16),
            vm(pieces + (hidden,), BF16),
            vm(pieces + (hidden,), BF16),
            vm((count, total, 3 * chans), BF16),
            vm((count, BLK, chans), F32),
            vm((heads, 2, BLK, BLK + CTX), BF16),
            vm(pieces + (chans,), BF16),
            vm((count, CTX, chans), BF16),
            vm((count, heads, CTX, 2 * HD), BF16),
            vm((total, chans), BF16),
            vm((CTX, chans), F32),
            vm((2, 2, rows, width), BF16),
            vm((count, 2, rows, width), BF16),
            vm((count, 2, rows, width), BF16),
            vm((count, 2, rows, width), BF16),
            vm((count, 2, rows, width), BF16),
            vm((count, rows, width), BF16),
            vm((count, rows, width), BF16),
            vm((count, rows, width), F32),
            vm((rows, width), F32),
            vm((misc_rows // 2, chans), BF16),
            vm((misc_rows, chans), BF16),
            vm((8, width), F32),
            vm((3, 8, width), F32),
            vm((count, heads, CTX, 2 * HD), F32),
            vm((count, 3, NS, chans), F32),
            pltpu.SemaphoreType.DMA((n_remote,)),
            pltpu.SemaphoreType.DMA((n_remote,)),
            pltpu.SemaphoreType.DMA((n_local,)),
        ],
        compiler_params=pltpu.CompilerParams(
            collective_id=0, has_side_effects=True, vmem_limit_bytes=63 << 20
        ),
        cost_estimate=cost(45e9, 60e6),
    )(lengths, tokens, cotangent, gain_one, gain_two, w_in, *ssm, ctx_w, w_out, w_up, w_down)
    return results[0], results[1], dict(zip(names, results[3:7]))


def body(
    tokens,
    lengths,
    cotangent,
    attn_gain,
    in_weights,
    ssm_rate,
    ssm_input,
    ssm_output,
    ctx_weights,
    out_weights,
    mlp_gain,
    up_weights,
    down_weights,
):
    width = tokens.shape[2]
    chans = out_weights.shape[0]
    heads = ctx_weights.shape[0]
    mixed, grad_tokens, grads = layer(
        lax.axis_size("dp") // 2,
        tokens,
        lengths[0],
        cotangent,
        attn_gain.reshape(1, width),
        mlp_gain.reshape(1, width),
        in_weights.reshape(width, 4 * chans),
        (ssm_rate, ssm_input, ssm_output),
        ctx_weights,
        out_weights,
        up_weights,
        down_weights,
    )
    misc = grads["misc"].astype(F32)
    parts = width // chans
    grad_out = jnp.concatenate([misc[j * chans : (j + 1) * chans] for j in range(parts)], axis=1)
    at = width
    grad_ctx = misc[at : at + heads * CTX].reshape(ctx_weights.shape)
    at += heads * CTX
    grad_ssm = misc[at : at + 3 * NS].reshape(3, NS, chans)
    at += 3 * NS
    gains = misc[at : at + 2 * parts].reshape(2, width)
    return (
        mixed,
        grad_tokens,
        gains[0],
        grads["inp"].astype(F32).reshape(in_weights.shape),
        grad_ssm[0],
        grad_ssm[1],
        grad_ssm[2],
        grad_ctx,
        grad_out,
        gains[1],
        grads["up"].astype(F32),
        grads["down"].astype(F32),
    )


def solution(mesh):
    rows = P(None, ("dp", "mp"), None)
    return jax.shard_map(
        body,
        mesh=mesh,
        in_specs=(
            rows,
            P("dp", None, None),
            rows,
            P(),
            P(None, None, "mp"),
            P(None, "mp"),
            P(None, "mp"),
            P(None, "mp"),
            P("mp", None, None),
            P("mp", None),
            P(),
            P(None, "mp"),
            P("mp", None),
        ),
        out_specs=(
            rows,
            rows,
            P(),
            P(None, None, "mp"),
            P(None, "mp"),
            P(None, "mp"),
            P(None, "mp"),
            P("mp", None, None),
            P("mp", None),
            P(),
            P(None, "mp"),
            P("mp", None),
        ),
        check_vma=False,
    )
```

```python
import functools
import math
import types

import jax
import jax.numpy as jnp
from jax import lax
from jax.experimental import pallas as pl
from jax.experimental.pallas import tpu as pltpu
from jax.sharding import PartitionSpec as P

HD = 128
BLK = 512
CTX = 128
HEAD = BLK - CTX
NS = 16
EPS = 1e-05
SCALE = 1.0 / math.sqrt(HD)
SCALE2 = SCALE * math.log2(math.e)
NEG = -1e30
F32 = jnp.float32
BF16 = jnp.bfloat16

VMEM = pl.BlockSpec(memory_space=pltpu.VMEM)
SMEM = pl.BlockSpec(memory_space=pltpu.SMEM)
ANY = pl.BlockSpec(memory_space=pl.ANY)


def params(mib):
    return pltpu.CompilerParams(vmem_limit_bytes=mib << 20)


def cost(flops, nbytes):
    return pl.CostEstimate(flops=int(flops), bytes_accessed=int(nbytes), transcendentals=0)


def dot(a, b):
    return lax.dot_general(a, b, (((1,), (0,)), ((), ())), preferred_element_type=F32)


def dot_nt(a, b):
    return lax.dot_general(a, b, (((1,), (1,)), ((), ())), preferred_element_type=F32)


def dot_tn(a, b):
    return lax.dot_general(a, b, (((0,), (0,)), ((), ())), preferred_element_type=F32)


def shape(dims, kind):
    return jax.ShapeDtypeStruct(dims, kind)


def triangle(upper):
    row = lax.broadcasted_iota(jnp.int32, (CTX, 2 * CTX), 0)
    col = lax.broadcasted_iota(jnp.int32, (CTX, 2 * CTX), 1) % CTX
    keep = (row <= col) if upper else (row >= col)
    return jnp.where(keep, 1.0, 0.0).astype(BF16)


def running(tri, values):
    high = values.astype(BF16)
    rest = (values - high.astype(F32)).astype(BF16)
    return dot(tri, jnp.concatenate([high, rest], axis=0))


def head_sums(u_ref, rate_ref, moment):
    width = rate_ref.shape[1]
    place = lax.broadcasted_iota(jnp.int32, (8, width), 0).astype(F32)
    sums, moments = [], []
    group = 4 if moment else 8
    for base in range(0, NS, group):
        rates = [rate_ref[n : n + 1, :] for n in range(base, base + group)]
        steps = [jnp.broadcast_to(jnp.exp(-8.0 * r), (8, width)) for r in rates]

        def body(chunk, carry):
            start = pl.multiple_of(chunk * 8, 8)
            rows = u_ref[pl.ds(start, 8), :]
            first = [acc * step + rows for acc, step in zip(carry[0], steps)]
            if not moment:
                return (first, carry[1])
            scaled = rows * (place + (chunk * 8 - HEAD).astype(F32))
            second = [acc * step + scaled for acc, step in zip(carry[1], steps)]
            return (first, second)

        zero = [jnp.zeros((8, width), F32) for _ in range(group)]
        first, second = lax.fori_loop(
            0, HEAD // 8, body, (zero, list(zero) if moment else []), unroll=4
        )
        for k, rate in enumerate(rates):
            last = jnp.exp(rate * (place - 8.0))
            sums.append(jnp.sum(first[k] * last, axis=0, keepdims=True))
            if moment:
                moments.append(jnp.sum(second[k] * last, axis=0, keepdims=True))
    return sums, moments


def state_forward(u_ref, rate_ref, in_ref, out_ref):
    width = rate_ref.shape[1]
    sums, _ = head_sums(u_ref, rate_ref, False)
    tail = u_ref[pl.ds(HEAD, CTX), :]
    time = lax.broadcasted_iota(jnp.int32, (CTX, width), 0).astype(F32)
    tri = triangle(False)
    total = jnp.zeros((CTX, width), F32)
    for n in range(NS):
        rate = rate_ref[n : n + 1, :]
        gain = in_ref[n : n + 1, :] * jnp.sqrt(1.0 - jnp.exp(-2.0 * rate))
        weight = gain * out_ref[n : n + 1, :]
        prefix = running(tri, jnp.exp(rate * time) * tail)
        total = total + weight * (jnp.exp(-rate * time) * (sums[n] + prefix))
    return total


def state_backward(grad, u_ref, du_ref, rate_ref, in_ref, out_ref, gs_ref):
    width = rate_ref.shape[1]
    sums, moments = head_sums(u_ref, rate_ref, True)
    tail = u_ref[pl.ds(HEAD, CTX), :]
    time = lax.broadcasted_iota(jnp.int32, (CTX, width), 0).astype(F32)
    place = lax.broadcasted_iota(jnp.int32, (8, width), 0).astype(F32)
    lower, upper = triangle(False), triangle(True)
    total = jnp.zeros((CTX, width), F32)
    starts = []
    for n in range(NS):
        rate = rate_ref[n : n + 1, :]
        root = jnp.sqrt(1.0 - jnp.exp(-2.0 * rate))
        enter = in_ref[n : n + 1, :]
        leave = out_ref[n : n + 1, :]
        gain = enter * root
        rising = jnp.exp(rate * time)
        driven = rising * tail
        states = sums[n] + running(lower, driven)
        seen = jnp.exp(-rate * time) * grad
        later = running(upper, seen)
        product = seen * states
        energy = jnp.sum(product, axis=0, keepdims=True)
        slope = jnp.sum(time * (product - driven * later), axis=0, keepdims=True)
        slope = slope - later[0:1] * moments[n]
        total = total + (gain * leave) * (rising * later)
        starts.append((gain * leave) * later[0:1])
        gs_ref[0, n : n + 1, :] = leave * (
            energy * enter * jnp.exp(-2.0 * rate) / root - gain * slope
        )
        gs_ref[1, n : n + 1, :] = leave * energy * root
        gs_ref[2, n : n + 1, :] = gain * energy
    du_ref[pl.ds(HEAD, CTX), :] = total
    group = 8
    for base in range(0, NS, group):
        rates = [rate_ref[n : n + 1, :] for n in range(base, base + group)]
        steps = [jnp.broadcast_to(jnp.exp(-8.0 * r), (8, width)) for r in rates]
        begin = [
            starts[base + k] * jnp.exp(rate * (place - 8.0)) for k, rate in enumerate(rates)
        ]

        def body(index, carry):
            start = pl.multiple_of(HEAD - 8 - index * 8, 8)
            value = functools.reduce(lambda a, b: a + b, carry)
            if base:
                value = value + du_ref[pl.ds(start, 8), :]
            du_ref[pl.ds(start, 8), :] = value
            return [c * step for c, step in zip(carry, steps)]

        lax.fori_loop(0, HEAD // 8, body, begin, unroll=4)


def layout_scalars(len_ref, micro):
    first, second = len_ref[micro, 0], len_ref[micro, 1]
    first_blocks = (first + (BLK - 1)) // BLK
    second_blocks = (second + (BLK - 1)) // BLK
    docs, valid = [], []
    for b in range(2):
        doc = jnp.where(b < first_blocks, 0, jnp.where(b < first_blocks + second_blocks, 1, 2))
        start = jnp.where(doc == 0, 0, first_blocks)
        extent = jnp.where(doc == 0, first, jnp.where(doc == 1, second, 0))
        docs.append(doc)
        valid.append(extent - (b - start) * BLK)
    return valid, docs[0] == docs[1]


JOBS = (("down", 0), ("down", 1), ("up", 0), ("up", 1), ("inp", 0), ("inp", 1), ("misc", 0))


ORDER = (
    "nf0", "nx0", "cn", "nf1", "pa0", "pa1", "nx1", "np0", "pb0", "sc0", "at0", "cx0", "np1",
    "br0", "pb1", "oa0", "sc1", "at1", "cp0", "br1", "fe0", "oa1", "ns0", "mx0", "fa0", "ns1",
    "mx1", "mp0", "fb0", "cx1", "fa1", "mp1", "ob0", "cp1", "fb1", "gdown1", "kup0", "gdown0",
    "kdown0", "kdown1", "nb0", "ydown1", "bx0", "gup1", "kup1", "ob1", "gup0", "ydown0", "bp0",
    "zdown1", "hb0", "ab0", "zdown0", "nb1", "bx1", "sb0", "pu0", "sdown1", "yup0", "oc1",
    "od0", "fe1", "yup1", "bp1", "hb1", "ab1", "sdown0", "sb1", "pu1", "zup0", "kinp1", "od1",
    "ginp0", "ginp1", "zup1", "mi1", "mo", "oc0", "kinp0", "nr1", "sup0", "yinp0", "mi0",
    "nr0", "gs", "yinp1", "pk", "gmisc0", "sup1", "zinp0", "ymisc0", "zinp1", "sinp0",
    "zmisc0", "sinp1", "smisc0",
)


def make_tasks(o, st):
    tasks, needs = {}, {}

    def task(name, *before):
        def put(work):
            tasks[name] = work
            needs[name] = before

        return put

    def recv(*names):
        for name in names:
            st[name].wait_recv()

    def sent(*names):
        for name in names:
            for copy in st[name] if isinstance(st[name], (list, tuple)) else [st[name]]:
                o.sent(copy)

    @task("cn")
    def _():
        o.loads["cot0"].wait()
        o.loads["cot1"].wait()
        st["c_near0"] = o.share("cot", 0)
        st["c_near1"] = o.share("cot", 1)

    def per_micro(m):
        n = str(m)
        other = str(1 - m)

        @task("nf" + n)
        def _():
            o.norm_first(m)
            st["n_near" + n] = o.share("xn", m)

        @task("nx" + n, "nf" + n)
        def _():
            st["n_far" + n] = o.cross("xn", m)

        @task("np" + n, "nx" + n)
        def _():
            st["n_both" + n] = o.pass_on("xn", m, st["n_far" + n])

        @task("pa" + n, "nf" + n)
        def _():
            if m == 0:
                o.loads["in"].wait()
            recv("n_near" + n)
            o.project(m, False)

        @task("pb" + n, "np" + n, *(["pa0"] if m else []))
        def _():
            recv("n_both" + n)
            o.project(m, True)

        @task("sc" + n, "pa" + n, "pb" + n)
        def _():
            o.scan(m)

        @task("at" + n, "sc" + n, *(["at0"] if m else []))
        def _():
            if m:
                st["save"].wait()
            o.attend(m)
            st["save"] = o.save(m)

        @task("cx" + n, "cn")
        def _():
            st["c_far" + n] = o.cross("cot", m)

        @task("cp" + n, "cx" + n)
        def _():
            st["c_both" + n] = o.pass_on("cot", m, st["c_far" + n])

        @task("br" + n, "at" + n, *(["br0"] if m else []))
        def _():
            if m == 0:
                o.loads["out"].wait()
            st["br" + n] = o.branch(m, st["br0"] if m else [])

        @task("oa" + n, "br" + n)
        def _():
            st["oa" + n] = o.owed("a", st["br" + n], m)

        @task("ns" + n, "oa" + n)
        def _():
            o.norm_second(m, st["br" + n], st["oa" + n])
            st["m_near" + n] = o.share("n2", m)

        @task("mx" + n, "ns" + n)
        def _():
            st["m_far" + n] = o.cross("n2", m)

        @task("mp" + n, "mx" + n)
        def _():
            st["m_both" + n] = o.pass_on("n2", m, st["m_far" + n])

        @task("fa" + n, "ns" + n, "cn", *(["fb0"] if m else ["br1"]))
        def _():
            if m == 0:
                o.loads["up"].wait()
                o.loads["down"].wait()
                sent("br1")
            else:
                sent("fa0")
            sent("oa" + n)
            recv("c_near" + n, "m_near" + n)
            st["fa" + n] = o.feed(m, False)

        @task("fb" + n, "fa" + n, "mp" + n, "cp" + n)
        def _():
            if m:
                sent("fb0")
            recv("c_both" + n, "m_both" + n)
            st["fb" + n] = o.feed(m, True)

        @task("ob" + n, "fb" + n)
        def _():
            st["ob" + n] = o.owed("b", (st["fa" + n][1], st["fb" + n][1]), m)

        @task("oc" + n, "fb" + n)
        def _():
            st["oc" + n] = o.owed("a", (st["fa" + n][0], st["fb" + n][0]), m)

        @task("nb" + n, "ob" + n)
        def _():
            o.norm_second_back(m, (st["fa" + n][1], st["fb" + n][1]), st["ob" + n])
            st["b_near" + n] = o.share("gbr", m)

        @task("bx" + n, "nb" + n)
        def _():
            st["b_far" + n] = o.cross("gbr", m)

        @task("bp" + n, "bx" + n)
        def _():
            st["b_both" + n] = o.pass_on("gbr", m, st["b_far" + n])

        @task("fe" + n, "at1", *(["ab0"] if m else []))
        def _():
            if m == 0:
                st["save"].wait()
            st["fetch"] = o.fetch(m)

        @task("hb" + n, "bp" + n, *(["ab0"] if m else ["gdown0", "gdown1", "kdown0", "kdown1"]))
        def _():
            recv("b_near" + n, "b_both" + n)
            o.heads_back(m)

        @task("ab" + n, "hb" + n, "fe" + n, *(["sb0"] if m else []))
        def _():
            st["fetch"].wait()
            o.attend_back(m)

        @task("sb" + n, "ab" + n)
        def _():
            o.scan_back(m)

        @task("pu" + n, "sb" + n, *(["pu0"] if m else ["fb1"]))
        def _():
            sent("ob" + n)
            if m == 0:
                sent("fa1", "fb1")
            st["pu" + n] = o.pull_back(m, st["pu0"] if m else [])

        @task("od" + n, "pu" + n)
        def _():
            st["od" + n] = o.owed("b", st["pu" + n], m)

        @task("mi" + n, "oc" + n)
        def _():
            sent("oc" + n)
            st["end" + n] = o.mix(m, (st["fa" + n][0], st["fb" + n][0]), st["oc" + n])

        @task("nr" + n, "od" + n, "mi" + n)
        def _():
            st["fin" + n] = o.norm_first_back(m, st["pu" + n], st["od" + n])

    per_micro(0)
    per_micro(1)

    @task("mo", "hb0", "hb1", "br1")
    def _():
        o.make_out()

    @task("gs", "nr0", "nr1", "nb0", "nb1")
    def _():
        st["gains"] = o.send_gains()

    @task("pk", "gs", "mo", "sb0", "sb1")
    def _():
        o.pack(st["gains"])

    ready = dict(down=("fb0", "fb1"), up=("fb0", "fb1"), inp=("pu0", "pu1"), misc=("pk",))

    def per_job(job):
        name = job[0] + str(job[1])
        last = ready[job[0]]
        if job[0] != "misc":

            @task("g" + name, *last)
            def _():
                o.tile_give(job)
                st[name] = o.swap_y(job)

            @task("k" + name, *last)
            def _():
                o.tile_keep(job)

            ahead = ("g" + name, "k" + name)
        else:

            @task("g" + name, *last)
            def _():
                st[name] = o.swap_y(job)

            ahead = ("g" + name,)

        @task("y" + name, *ahead)
        def _():
            st[name] = o.sum_y(job, st[name])

        @task("z" + name, "y" + name)
        def _():
            st[name] = o.sum_z(job, st[name])

        @task("s" + name, "z" + name)
        def _():
            st[name] = o.spread_y(job, st[name])

    for job in JOBS:
        per_job(job)
    return tasks, needs


def run(o):
    st = {}
    tasks, needs = make_tasks(o, st)
    done = set()
    for name in ORDER:
        assert all(ahead in done for ahead in needs[name]), name
        tasks[name]()
        done.add(name)
    assert len(done) == len(tasks)
    for job in JOBS:
        o.finish(st[job[0] + str(job[1])])
    for name in ("end0", "end1", "fin0", "fin1"):
        st[name].wait()


class Copies:
    def __init__(self, send, recv):
        self.send, self.recv, self.used, self.open = send, recv, 0, []

    def start(self, source, target, device):
        copy = pltpu.make_async_remote_copy(
            src_ref=source,
            dst_ref=target,
            send_sem=self.send.at[self.used],
            recv_sem=self.recv.at[self.used],
            device_id=device,
            device_id_type=pl.DeviceIdType.MESH,
        )
        self.used += 1
        copy.start()
        self.open.append(copy)
        return copy

    def sent(self, copy):
        copy.wait_send()
        self.open = [other for other in self.open if other is not copy]

    def drain(self):
        for copy in self.open:
            copy.wait_send()
        self.open = []


class Moves:
    def __init__(self, sems):
        self.sems, self.used = sems, 0

    def start(self, source, target):
        copy = pltpu.make_async_copy(source, target, self.sems.at[self.used])
        self.used += 1
        copy.start()
        return copy


def layer(
    nz, tokens, lengths, cotangent, gain_one, gain_two, w_in, ssm, ctx_w, w_out, w_up, w_down
):
    count, rows, width = tokens.shape
    chans = w_out.shape[0]
    heads = chans // HD
    hidden = w_up.shape[1]
    total = 4 * rows
    pair = 2 * rows
    small_rows = heads * CTX + 3 * NS + 8
    unit = 2 * nz * 16
    misc_rows = width + small_rows + (-small_rows % unit)
    sizes = dict(down=(hidden, width), up=(width, hidden), inp=(width, 4 * chans), misc=(misc_rows, chans))
    names = list(sizes)
    share = {n: rows if sizes[n][1] == width else sizes[n][0] // 2 for n in names}
    n_jobs = sum(sizes[n][0] // 2 // share[n] for n in names)
    root = math.sqrt(2.0 / math.pi)
    n_remote = 51 + n_jobs * (1 + 2 * (nz - 1) + nz)
    n_local = 14 + n_jobs * (nz + 1)

    def kernel(*refs):
        (
            len_ref, tok, cot_hbm, g1, g2, in_hbm, rate, enter, leave, cw, out_hbm, up_hbm, down_hbm,
        ) = refs[:13]
        mixed_hbm, gtok_hbm, pr_hbm = refs[13:16]
        grads = dict(zip(names, refs[16:20]))
        ry = dict(zip(names, refs[20:24]))
        rz = dict(zip(names, refs[24:28]))
        (
            w_i, w_o, w_u, w_d, xn, cot, n2, gbr, hid, gbf, qkv, u0, pr, ho, cx, ckv, dh, gctx,
            give, keep_a, keep_b, sib_a, sib_b, far_a, far_b, mid, acc, tmp, land, misc,
            gain_acc, gain_got, gcw, gss, send_sems, recv_sems, local_sems,
        ) = refs[28:]
        me = lax.axis_index("mp")
        core, chip = me % 2, me // 2
        near, far, both = chip * 2 + 1 - core, (1 - chip) * 2 + core, (1 - chip) * 2 + 1 - core
        dp = lax.axis_index("dp")
        y, z = dp % 2, dp // 2
        to_near, to_far, to_both = {"mp": near}, {"mp": far}, {"mp": both}
        to_y = {"dp": z * 2 + 1 - y}
        zs = [(z + k) % nz for k in range(nz)]
        to_z = [{"dp": zk * 2 + y} for zk in zs]
        remote, local = Copies(send_sems, recv_sems), Moves(local_sems)

        loads = {
            "in": local.start(in_hbm, w_i),
            "cot0": local.start(cot_hbm.at[0], cot.at[0, me]),
            "cot1": local.start(cot_hbm.at[1], cot.at[1, me]),
            "out": local.start(out_hbm, w_o),
            "up": local.start(up_hbm, w_u),
            "down": local.start(down_hbm, w_d),
        }
        barrier = pltpu.get_barrier_semaphore()
        for device in [to_near, to_far, to_both, to_y] + to_z[1:]:
            pl.semaphore_signal(
                barrier, inc=1, device_id=device, device_id_type=pl.DeviceIdType.MESH
            )
        pl.semaphore_wait(barrier, 3 + nz)

        def share_piece(buf, m):
            return remote.start(buf.at[m, me], buf.at[m, me], to_near)

        def cross(buf, m):
            return remote.start(buf.at[m, me], buf.at[m, me], to_far)

        def pass_on(buf, m, copy):
            copy.wait_recv()
            return remote.start(buf.at[m, far], buf.at[m, far], to_near)

        def offer(kind, slot, sib, m):
            return remote.start(give.at[kind, slot], sib.at[m, slot], to_near)

        def by_rows(work):
            step = 64

            def body(i, carry):
                work(pl.ds(pl.multiple_of(i * step, step), step))
                return carry

            lax.fori_loop(0, rows // step, body, 0)

        def owed(offers, keep, sib, far_buf, m):
            offers[1].wait_recv()

            def work(at):
                keep[m, 1, at, :] = (
                    keep[m, 1, at, :].astype(F32) + sib[m, 1, at, :].astype(F32)
                ).astype(BF16)

            by_rows(work)
            return remote.start(keep.at[m, 1], far_buf.at[m], to_far)

        def summed(offers, copy, keep, sib, far_buf, m):
            offers[0].wait_recv()
            copy.wait_recv()
            return lambda at: (
                keep[m, 0, at, :].astype(F32)
                + sib[m, 0, at, :].astype(F32)
                + far_buf[m, at, :].astype(F32)
            )

        def inverse_root(value):
            return lax.rsqrt(jnp.mean(value * value, axis=-1, keepdims=True) + EPS)

        def norm_first(m):
            def work(at):
                x = tok[m, at, :].astype(F32)
                xn[m, me, at, :] = (x * inverse_root(x) * g1[...]).astype(BF16)

            by_rows(work)

        def norm_second(m, branch):
            def work(at):
                value = tok[m, at, :].astype(F32) + branch(at)
                mid[m, at, :] = value
                n2[m, me, at, :] = (value * inverse_root(value) * g2[...]).astype(BF16)

            by_rows(work)

        def pulled(value, grad, gain, line):
            scale = inverse_root(value)
            unit_row = value * scale
            gain_acc[line : line + 1, :] += jnp.sum(grad * unit_row, axis=0, keepdims=True)
            inner = grad * gain[...]
            return scale * (inner - unit_row * jnp.mean(inner * unit_row, axis=-1, keepdims=True))

        def norm_second_back(m, grad):
            def work(at):
                value = cot[m, me, at, :].astype(F32) + pulled(mid[m, at, :], grad(at), g2, 1)
                gbr[m, me, at, :] = value.astype(BF16)

            by_rows(work)

        def norm_first_back(m, grad):
            def work(at):
                x = tok[m, at, :].astype(F32)
                mid[m, at, :] = gbr[m, me, at, :].astype(F32) + pulled(x, grad(at), g1, 0)

            by_rows(work)
            return local.start(mid.at[m], gtok_hbm.at[m])

        def mix(m, branch):
            def work(at):
                keep_a[m, 0, at, :] = (mid[m, at, :] + branch(at)).astype(BF16)

            by_rows(work)
            return local.start(keep_a.at[m, 0], mixed_hbm.at[m])

        def project(m, side):
            def body(i, carry):
                t = side * 2 + i
                at = pl.ds(pl.multiple_of(t * rows, rows), rows)
                x = xn[m, t]
                qkv[m, at, :] = dot(x, w_i[:, : 3 * chans]).astype(BF16)

                @pl.when(t < 2)
                def _():
                    u0[m, at, :] = dot(x, w_i[:, 3 * chans :])

                return carry

            lax.fori_loop(0, 2, body, 0)

        def scan(m):
            context = state_forward(u0.at[m], rate, enter, leave).astype(BF16)
            cx[m] = context
            for h in range(heads):
                ckv[m, h] = dot(context[:, h * HD : (h + 1) * HD], cw[h]).astype(BF16)

        def attend(m):
            valid, linked = layout_scalars(len_ref, m)
            for h in range(heads):
                lanes = slice(h * HD, (h + 1) * HD)
                klanes = slice(chans + h * HD, chans + (h + 1) * HD)
                vlanes = slice(2 * chans + h * HD, 2 * chans + (h + 1) * HD)
                for b in range(2):
                    for half in range(2):
                        row0 = half * rows
                        keys = row0 + rows
                        spot = b * BLK + row0
                        q = qkv[m, spot : spot + rows, lanes]
                        k = qkv[m, b * BLK : b * BLK + keys, klanes]
                        v = qkv[m, b * BLK : b * BLK + keys, vlanes]
                        s = dot_nt(q, k) * SCALE2
                        row = lax.broadcasted_iota(jnp.int32, (rows, keys), 0) + row0
                        col = lax.broadcasted_iota(jnp.int32, (rows, keys), 1)
                        allowed = (col < jnp.minimum(row, valid[b])) | (col == row)
                        s = jnp.where(allowed, s, NEG)
                        peak = jnp.max(s, axis=-1, keepdims=True)
                        if b:
                            sc = dot_nt(q, ckv[m, h, :, :HD]) * SCALE2
                            sc = jnp.where(linked, sc, NEG)
                            peak = jnp.maximum(peak, jnp.max(sc, axis=-1, keepdims=True))
                            ec = jnp.exp2(sc - peak)
                        e = jnp.exp2(s - peak)
                        norm = jnp.sum(e, axis=-1, keepdims=True)
                        if b:
                            norm = norm + jnp.sum(ec, axis=-1, keepdims=True)
                        inverse = 1.0 / norm
                        p = (e * inverse).astype(BF16)
                        pr[h, b, row0 : row0 + rows, CTX : CTX + keys] = p
                        o = dot(p, v)
                        if b:
                            pc = (ec * inverse).astype(BF16)
                            pr[h, b, row0 : row0 + rows, :CTX] = pc
                            o = o + dot(pc, ckv[m, h, :, HD:])
                        ho[m, 2 * b + half, :, lanes] = o.astype(BF16)

        def spread(product, keep, kind, sib, m, before):
            for copy in before:
                remote.sent(copy)
            give[kind, 1] = product(both).astype(BF16)
            second = offer(kind, 1, sib, m)
            give[kind, 0] = product(near).astype(BF16)
            first = offer(kind, 0, sib, m)
            keep[m, 1] = product(far).astype(BF16)
            keep[m, 0] = product(me).astype(BF16)
            return [first, second]

        def feed(m, side, other):
            slot = 1 if other else 0

            def body(i, carry):
                t = side * 2 + jnp.where(i == 0, 1 - core, core)
                for start in range(0, hidden, 256):
                    cut = slice(start, start + 256)
                    before = dot(n2[m, t], w_u[:, cut])
                    square = before * before
                    th = jnp.tanh(root * (before * (1.0 + 0.044715 * square)))
                    half = 0.5 + 0.5 * th
                    hid[m, t, :, cut] = (before * half).astype(BF16)
                    slope = half + (0.5 * root) * before * (1.0 - th * th) * (
                        1.0 + 0.134145 * square
                    )
                    gbf[m, t, :, cut] = (dot_nt(cot[m, t], w_d[cut, :]) * slope).astype(BF16)
                branch = dot(hid[m, t], w_d[...]).astype(BF16)
                gn = dot_nt(gbf[m, t], w_u[...]).astype(BF16)

                @pl.when(i == 0)
                def _():
                    give[0, slot] = branch
                    give[1, slot] = gn

                @pl.when(i == 1)
                def _():
                    keep_a[m, slot] = branch
                    keep_b[m, slot] = gn

                return carry

            lax.fori_loop(0, 2, body, 0)
            return offer(0, slot, sib_a, m), offer(1, slot, sib_b, m)

        def heads_back(m):
            def body(t, carry):
                at = pl.ds(pl.multiple_of(t * rows, rows), rows)
                dh[at, :] = dot_nt(gbr[m, t], w_o[...]).astype(BF16)
                return carry

            lax.fori_loop(0, 4, body, 0)

        def attend_back(m):
            for h in range(heads):
                lanes = slice(h * HD, (h + 1) * HD)
                klanes = slice(chans + h * HD, chans + (h + 1) * HD)
                vlanes = slice(2 * chans + h * HD, 2 * chans + (h + 1) * HD)
                for b in range(2):
                    grad_k, grad_v = [None, None], [None, None]
                    grad_c = grad_cv = None
                    for half in (1, 0):
                        row0 = half * rows
                        keys = row0 + rows
                        spot = slice(b * BLK + row0, b * BLK + row0 + rows)
                        go = dh[spot, lanes]
                        qh = qkv[m, spot, lanes]
                        kh = qkv[m, b * BLK : b * BLK + keys, klanes]
                        vh = qkv[m, b * BLK : b * BLK + keys, vlanes]
                        p = pr[h, b, row0 : row0 + rows, CTX : CTX + keys]
                        pf = p.astype(F32)
                        dprob = dot_nt(go, vh)
                        delta = jnp.sum(dprob * pf, axis=-1, keepdims=True)
                        if b:
                            pc = pr[h, b, row0 : row0 + rows, :CTX]
                            pcf = pc.astype(F32)
                            dpc = dot_nt(go, ckv[m, h, :, HD:])
                            delta = delta + jnp.sum(dpc * pcf, axis=-1, keepdims=True)
                            dsc = (pcf * (dpc - delta)).astype(BF16)
                        ds = (pf * (dprob - delta)).astype(BF16)
                        dq = dot(ds, kh)
                        if b:
                            dq = dq + dot(dsc, ckv[m, h, :, :HD])
                            one = dot_tn(dsc, qh)
                            two = dot_tn(pc, go)
                            grad_c = one if grad_c is None else grad_c + one
                            grad_cv = two if grad_cv is None else grad_cv + two
                        hid[m, 2 * b + half, :, lanes] = (dq * SCALE).astype(BF16)
                        dk = dot_tn(ds, qh)
                        dv = dot_tn(p, go)
                        if half:
                            grad_k = [dk[:rows], dk[rows:]]
                            grad_v = [dv[:rows], dv[rows:]]
                        else:
                            grad_k[0] = grad_k[0] + dk
                            grad_v[0] = grad_v[0] + dv
                    for part in range(2):
                        t = 2 * b + part
                        hid[m, t, :, klanes] = (grad_k[part] * SCALE).astype(BF16)
                        hid[m, t, :, vlanes] = grad_v[part].astype(BF16)
                    if b:
                        low_c = (grad_c * SCALE).astype(BF16)
                        low_cv = grad_cv.astype(BF16)
                        ch = cx[m, :, lanes]
                        gcw[m, h, :, :HD] = dot_tn(ch, low_c)
                        gcw[m, h, :, HD:] = dot_tn(ch, low_cv)
                        gctx[:, lanes] = dot_nt(low_c, cw[h, :, :HD]) + dot_nt(
                            low_cv, cw[h, :, HD:]
                        )

        def scan_back(m):
            state_backward(gctx[...], u0.at[m], u0.at[m], rate, enter, leave, gss.at[m])
            for t in range(2):
                hid[m, t, :, 3 * chans :] = u0[m, t * rows : (t + 1) * rows, :].astype(BF16)
                hid[m, 2 + t, :, 3 * chans :] = jnp.zeros((rows, chans), BF16)

        def gather_tile(left, right, tile):
            lanes = pl.ds(pl.multiple_of(tile * rows, rows), rows)
            acc[...] = jnp.zeros_like(acc)

            def body(i, carry):
                m, t = i // 4, i % 4
                acc[...] += dot_tn(left[m, t, :, lanes], right[m, t])
                return carry

            lax.fori_loop(0, 4 * count, body, 0)

        def part(ref, start, size):
            return ref.at[pl.ds(pl.multiple_of(start, 16), size), :]

        def job_rows(job, side):
            name, i = job
            span = sizes[name][0] // 2
            if sizes[name][1] != width:
                return side * span, span
            return side * span + i * rows, rows

        stages = dict(down=w_d, up=w_u, inp=w_i, misc=misc)
        sides = dict(down=(hid, cot), up=(n2, gbf), inp=(xn, hid))

        def tile(job, side):
            start, size = job_rows(job, side)
            gather_tile(*sides[job[0]], start // size)
            stages[job[0]][pl.ds(pl.multiple_of(start, size), size), :] = acc[...].astype(BF16)

        def tile_give(job):
            tile(job, 1 - y)

        def tile_keep(job):
            tile(job, y)

        def landing(job, size):
            if sizes[job[0]][1] != width:
                return tmp.at[pl.ds(0, size), :]
            return land.at[pl.ds(0, size), :]

        def swap_y(job):
            name, i = job
            start, size = job_rows(job, 1 - y)
            return remote.start(part(stages[name], start, size), ry[name].at[i], to_y)

        def sum_y(job, copy):
            name, i = job
            stage = stages[name]
            start, size = job_rows(job, y)
            piece = size // nz
            copy.wait_recv()
            got = landing(job, size)
            local.start(ry[name].at[i], got).wait()
            at = pl.ds(pl.multiple_of(start, 16), size)
            stage[at, :] = (stage[at, :].astype(F32) + got[...].astype(F32)).astype(BF16)
            return [
                remote.start(
                    part(stage, start + zs[k] * piece, piece), rz[name].at[i, k - 1], to_z[k]
                )
                for k in range(1, nz)
            ]

        def sum_z(job, copies):
            name, i = job
            stage = stages[name]
            start, size = job_rows(job, y)
            piece = size // nz
            for copy in copies:
                copy.wait_recv()
            got = landing(job, (nz - 1) * piece)
            moves = [
                local.start(rz[name].at[i, k], got.at[pl.ds(k * piece, piece), :])
                for k in range(nz - 1)
            ]
            for move in moves:
                move.wait()
            spot = start + z * piece
            at = pl.ds(pl.multiple_of(spot, 16), piece)
            value = stage[at, :].astype(F32)
            for k in range(nz - 1):
                value = value + got[k * piece : (k + 1) * piece, :].astype(F32)
            stage[at, :] = value.astype(BF16)
            mine = part(stage, spot, piece)
            place = part(grads[name], spot, piece)
            outs = [remote.start(mine, place, to_z[k]) for k in range(1, nz)]
            last = [remote.start(mine, place, to_y)]
            return outs, last, local.start(mine, place)

        def spread_y(job, state):
            name, i = job
            start, size = job_rows(job, y)
            piece = size // nz
            outs, last, move = state
            for k in range(1, nz):
                outs[k - 1].wait_recv()
                place = part(grads[name], start + ((z + nz - k) % nz) * piece, piece)
                last.append(remote.start(place, place, to_y))
            return last, move

        def finish(state):
            last, move = state
            for copy in last:
                copy.wait_recv()
            move.wait()

        def make_out():
            gather_tile(ho, gbr, 0)
            for j in range(width // chans):
                misc[j * chans : (j + 1) * chans, :] = acc[:, j * chans : (j + 1) * chans].astype(
                    BF16
                )

        def send_gains():
            return [
                remote.start(gain_acc, gain_got.at[k], device)
                for k, device in enumerate((to_near, to_far, to_both))
            ]

        def pack(copies):
            base = width
            for h in range(heads):
                misc[base + h * CTX : base + (h + 1) * CTX, :] = (gcw[0, h] + gcw[1, h]).astype(BF16)
            base += heads * CTX
            for k in range(3):
                misc[base + k * NS : base + (k + 1) * NS, :] = (gss[0, k] + gss[1, k]).astype(BF16)
            base += 3 * NS
            for copy in copies:
                copy.wait_recv()
            value = gain_acc[...] + gain_got[0] + gain_got[1] + gain_got[2]
            line = jnp.concatenate(
                [value[r : r + 1, j * chans : (j + 1) * chans] for r in range(2) for j in range(4)],
                axis=0,
            )
            misc[base:, :] = jnp.concatenate(
                [line, jnp.zeros((misc_rows - base - 8, chans), F32)], axis=0
            ).astype(BF16)

        def branch(m, before):
            return spread(lambda t: dot(ho[m, t], w_o[...]), keep_a, 0, sib_a, m, before)

        def pull_back(m, before):
            return spread(lambda t: dot_nt(hid[m, t], w_i[...]), keep_b, 1, sib_b, m, before)

        bufs = dict(xn=xn, cot=cot, n2=n2, gbr=gbr)
        sets = dict(a=(keep_a, sib_a, far_a), b=(keep_b, sib_b, far_b))
        o = types.SimpleNamespace(
            count=count,
            norm_first=norm_first,
            share=lambda buf, m: share_piece(bufs[buf], m),
            cross=lambda buf, m: cross(bufs[buf], m),
            pass_on=lambda buf, m, copy: pass_on(bufs[buf], m, copy),
            sent=remote.sent,
            loads=loads,
            project=lambda m, other: project(m, 1 - chip if other else chip),
            scan=scan,
            attend=attend,
            save=lambda m: local.start(pr, pr_hbm.at[m]),
            fetch=lambda m: local.start(pr_hbm.at[m], pr),
            branch=branch,
            owed=lambda kind, offers, m: owed(offers, *sets[kind], m),
            norm_second=lambda m, of, cp: norm_second(m, summed(of, cp, *sets["a"], m)),
            norm_second_back=lambda m, of, cp: norm_second_back(m, summed(of, cp, *sets["b"], m)),
            norm_first_back=lambda m, of, cp: norm_first_back(m, summed(of, cp, *sets["b"], m)),
            mix=lambda m, of, cp: mix(m, summed(of, cp, *sets["a"], m)),
            feed=lambda m, other: feed(m, 1 - chip if other else chip, other),
            heads_back=heads_back,
            attend_back=attend_back,
            scan_back=scan_back,
            pull_back=pull_back,
            tile_give=tile_give,
            tile_keep=tile_keep,
            swap_y=swap_y,
            sum_y=sum_y,
            sum_z=sum_z,
            spread_y=spread_y,
            finish=finish,
            make_out=make_out,
            send_gains=send_gains,
            pack=pack,
        )
        gain_acc[...] = jnp.zeros_like(gain_acc)
        run(o)
        remote.drain()
        assert remote.used <= n_remote and local.used <= n_local, (remote.used, local.used)

    pieces = (count, 4, rows)
    vm = pltpu.VMEM
    any_out = [
        shape((count, rows, width), BF16),
        shape((count, rows, width), F32),
        shape((count, heads, 2, BLK, BLK + CTX), BF16),
    ]
    any_out += [shape(sizes[n], BF16) for n in names]
    any_out += [
        shape((sizes[n][0] // 2 // share[n], share[n], sizes[n][1]), BF16) for n in names
    ]
    any_out += [
        shape((sizes[n][0] // 2 // share[n], nz - 1, share[n] // nz, sizes[n][1]), BF16)
        for n in names
    ]
    results = pl.pallas_call(
        kernel,
        in_specs=[SMEM, VMEM, ANY, VMEM, VMEM, ANY, VMEM, VMEM, VMEM, VMEM, ANY, ANY, ANY],
        out_specs=[ANY] * len(any_out),
        out_shape=any_out,
        scratch_shapes=[
            vm(w_in.shape, BF16),
            vm(w_out.shape, BF16),
            vm(w_up.shape, BF16),
            vm(w_down.shape, BF16),
            vm(pieces + (width,), BF16),
            vm(pieces + (width,), BF16),
            vm(pieces + (width,), BF16),
            vm(pieces + (width,), BF16),
            vm(pieces + (hidden,), BF16),
            vm(pieces + (hidden,), BF16),
            vm((count, total, 3 * chans), BF16),
            vm((count, BLK, chans), F32),
            vm((heads, 2, BLK, BLK + CTX), BF16),
            vm(pieces + (chans,), BF16),
            vm((count, CTX, chans), BF16),
            vm((count, heads, CTX, 2 * HD), BF16),
            vm((total, chans), BF16),
            vm((CTX, chans), F32),
            vm((2, 2, rows, width), BF16),
            vm((count, 2, rows, width), BF16),
            vm((count, 2, rows, width), BF16),
            vm((count, 2, rows, width), BF16),
            vm((count, 2, rows, width), BF16),
            vm((count, rows, width), BF16),
            vm((count, rows, width), BF16),
            vm((count, rows, width), F32),
            vm((rows, width), F32),
            vm((misc_rows // 2, chans), BF16),
            vm((rows, width), BF16),
            vm((misc_rows, chans), BF16),
            vm((8, width), F32),
            vm((3, 8, width), F32),
            vm((count, heads, CTX, 2 * HD), F32),
            vm((count, 3, NS, chans), F32),
            pltpu.SemaphoreType.DMA((n_remote,)),
            pltpu.SemaphoreType.DMA((n_remote,)),
            pltpu.SemaphoreType.DMA((n_local,)),
        ],
        compiler_params=pltpu.CompilerParams(
            collective_id=0, has_side_effects=True, vmem_limit_bytes=63 << 20
        ),
        cost_estimate=cost(45e9, 60e6),
    )(lengths, tokens, cotangent, gain_one, gain_two, w_in, *ssm, ctx_w, w_out, w_up, w_down)
    return results[0], results[1], dict(zip(names, results[3:7]))


def body(
    tokens,
    lengths,
    cotangent,
    attn_gain,
    in_weights,
    ssm_rate,
    ssm_input,
    ssm_output,
    ctx_weights,
    out_weights,
    mlp_gain,
    up_weights,
    down_weights,
):
    width = tokens.shape[2]
    chans = out_weights.shape[0]
    heads = ctx_weights.shape[0]
    mixed, grad_tokens, grads = layer(
        lax.axis_size("dp") // 2,
        tokens,
        lengths[0],
        cotangent,
        attn_gain.reshape(1, width),
        mlp_gain.reshape(1, width),
        in_weights.reshape(width, 4 * chans),
        (ssm_rate, ssm_input, ssm_output),
        ctx_weights,
        out_weights,
        up_weights,
        down_weights,
    )
    misc = grads["misc"].astype(F32)
    parts = width // chans
    grad_out = jnp.concatenate([misc[j * chans : (j + 1) * chans] for j in range(parts)], axis=1)
    at = width
    grad_ctx = misc[at : at + heads * CTX].reshape(ctx_weights.shape)
    at += heads * CTX
    grad_ssm = misc[at : at + 3 * NS].reshape(3, NS, chans)
    at += 3 * NS
    gains = misc[at : at + 2 * parts].reshape(2, width)
    return (
        mixed,
        grad_tokens,
        gains[0],
        grads["inp"].astype(F32).reshape(in_weights.shape),
        grad_ssm[0],
        grad_ssm[1],
        grad_ssm[2],
        grad_ctx,
        grad_out,
        gains[1],
        grads["up"].astype(F32),
        grads["down"].astype(F32),
    )


def solution(mesh):
    rows = P(None, ("dp", "mp"), None)
    return jax.shard_map(
        body,
        mesh=mesh,
        in_specs=(
            rows,
            P("dp", None, None),
            rows,
            P(),
            P(None, None, "mp"),
            P(None, "mp"),
            P(None, "mp"),
            P(None, "mp"),
            P("mp", None, None),
            P("mp", None),
            P(),
            P(None, "mp"),
            P("mp", None),
        ),
        out_specs=(
            rows,
            rows,
            P(),
            P(None, None, "mp"),
            P(None, "mp"),
            P(None, "mp"),
            P(None, "mp"),
            P("mp", None, None),
            P("mp", None),
            P(),
            P(None, "mp"),
            P("mp", None),
        ),
        check_vma=False,
    )
```

```python
import functools
import math
import types

import jax
import jax.numpy as jnp
from jax import lax
from jax.experimental import pallas as pl
from jax.experimental.pallas import tpu as pltpu
from jax.sharding import PartitionSpec as P

HD = 128
BLK = 512
CTX = 128
HEAD = BLK - CTX
NS = 16
EPS = 1e-05
SCALE = 1.0 / math.sqrt(HD)
SCALE2 = SCALE * math.log2(math.e)
NEG = -1e30
F32 = jnp.float32
BF16 = jnp.bfloat16

VMEM = pl.BlockSpec(memory_space=pltpu.VMEM)
SMEM = pl.BlockSpec(memory_space=pltpu.SMEM)
ANY = pl.BlockSpec(memory_space=pl.ANY)


def params(mib):
    return pltpu.CompilerParams(vmem_limit_bytes=mib << 20)


def cost(flops, nbytes):
    return pl.CostEstimate(flops=int(flops), bytes_accessed=int(nbytes), transcendentals=0)


def dot(a, b):
    return lax.dot_general(a, b, (((1,), (0,)), ((), ())), preferred_element_type=F32)


def dot_nt(a, b):
    return lax.dot_general(a, b, (((1,), (1,)), ((), ())), preferred_element_type=F32)


def dot_tn(a, b):
    return lax.dot_general(a, b, (((0,), (0,)), ((), ())), preferred_element_type=F32)


def shape(dims, kind):
    return jax.ShapeDtypeStruct(dims, kind)


def triangle(upper):
    row = lax.broadcasted_iota(jnp.int32, (CTX, 2 * CTX), 0)
    col = lax.broadcasted_iota(jnp.int32, (CTX, 2 * CTX), 1) % CTX
    keep = (row <= col) if upper else (row >= col)
    return jnp.where(keep, 1.0, 0.0).astype(BF16)


def running(tri, values):
    high = values.astype(BF16)
    rest = (values - high.astype(F32)).astype(BF16)
    return dot(tri, jnp.concatenate([high, rest], axis=0))


def head_sums(u_ref, rate_ref, moment):
    width = rate_ref.shape[1]
    place = lax.broadcasted_iota(jnp.int32, (8, width), 0).astype(F32)
    sums, moments = [], []
    group = 4 if moment else 8
    for base in range(0, NS, group):
        rates = [rate_ref[n : n + 1, :] for n in range(base, base + group)]
        steps = [jnp.broadcast_to(jnp.exp(-8.0 * r), (8, width)) for r in rates]

        def body(chunk, carry):
            start = pl.multiple_of(chunk * 8, 8)
            rows = u_ref[pl.ds(start, 8), :]
            first = [acc * step + rows for acc, step in zip(carry[0], steps)]
            if not moment:
                return (first, carry[1])
            scaled = rows * (place + (chunk * 8 - HEAD).astype(F32))
            second = [acc * step + scaled for acc, step in zip(carry[1], steps)]
            return (first, second)

        zero = [jnp.zeros((8, width), F32) for _ in range(group)]
        first, second = lax.fori_loop(
            0, HEAD // 8, body, (zero, list(zero) if moment else []), unroll=4
        )
        for k, rate in enumerate(rates):
            last = jnp.exp(rate * (place - 8.0))
            sums.append(jnp.sum(first[k] * last, axis=0, keepdims=True))
            if moment:
                moments.append(jnp.sum(second[k] * last, axis=0, keepdims=True))
    return sums, moments


def state_forward(u_ref, rate_ref, in_ref, out_ref):
    width = rate_ref.shape[1]
    sums, _ = head_sums(u_ref, rate_ref, False)
    tail = u_ref[pl.ds(HEAD, CTX), :]
    time = lax.broadcasted_iota(jnp.int32, (CTX, width), 0).astype(F32)
    tri = triangle(False)
    total = jnp.zeros((CTX, width), F32)
    for n in range(NS):
        rate = rate_ref[n : n + 1, :]
        gain = in_ref[n : n + 1, :] * jnp.sqrt(1.0 - jnp.exp(-2.0 * rate))
        weight = gain * out_ref[n : n + 1, :]
        prefix = running(tri, jnp.exp(rate * time) * tail)
        total = total + weight * (jnp.exp(-rate * time) * (sums[n] + prefix))
    return total


def state_backward(grad, u_ref, du_ref, rate_ref, in_ref, out_ref, gs_ref):
    width = rate_ref.shape[1]
    sums, moments = head_sums(u_ref, rate_ref, True)
    tail = u_ref[pl.ds(HEAD, CTX), :]
    time = lax.broadcasted_iota(jnp.int32, (CTX, width), 0).astype(F32)
    place = lax.broadcasted_iota(jnp.int32, (8, width), 0).astype(F32)
    lower, upper = triangle(False), triangle(True)
    total = jnp.zeros((CTX, width), F32)
    starts = []
    for n in range(NS):
        rate = rate_ref[n : n + 1, :]
        root = jnp.sqrt(1.0 - jnp.exp(-2.0 * rate))
        enter = in_ref[n : n + 1, :]
        leave = out_ref[n : n + 1, :]
        gain = enter * root
        rising = jnp.exp(rate * time)
        driven = rising * tail
        states = sums[n] + running(lower, driven)
        seen = jnp.exp(-rate * time) * grad
        later = running(upper, seen)
        product = seen * states
        energy = jnp.sum(product, axis=0, keepdims=True)
        slope = jnp.sum(time * (product - driven * later), axis=0, keepdims=True)
        slope = slope - later[0:1] * moments[n]
        total = total + (gain * leave) * (rising * later)
        starts.append((gain * leave) * later[0:1])
        gs_ref[0, n : n + 1, :] = leave * (
            energy * enter * jnp.exp(-2.0 * rate) / root - gain * slope
        )
        gs_ref[1, n : n + 1, :] = leave * energy * root
        gs_ref[2, n : n + 1, :] = gain * energy
    du_ref[pl.ds(HEAD, CTX), :] = total
    group = 8
    for base in range(0, NS, group):
        rates = [rate_ref[n : n + 1, :] for n in range(base, base + group)]
        steps = [jnp.broadcast_to(jnp.exp(-8.0 * r), (8, width)) for r in rates]
        begin = [
            starts[base + k] * jnp.exp(rate * (place - 8.0)) for k, rate in enumerate(rates)
        ]

        def body(index, carry):
            start = pl.multiple_of(HEAD - 8 - index * 8, 8)
            value = functools.reduce(lambda a, b: a + b, carry)
            if base:
                value = value + du_ref[pl.ds(start, 8), :]
            du_ref[pl.ds(start, 8), :] = value
            return [c * step for c, step in zip(carry, steps)]

        lax.fori_loop(0, HEAD // 8, body, begin, unroll=4)


def layout_scalars(len_ref, micro):
    first, second = len_ref[micro, 0], len_ref[micro, 1]
    first_blocks = (first + (BLK - 1)) // BLK
    second_blocks = (second + (BLK - 1)) // BLK
    docs, valid = [], []
    for b in range(2):
        doc = jnp.where(b < first_blocks, 0, jnp.where(b < first_blocks + second_blocks, 1, 2))
        start = jnp.where(doc == 0, 0, first_blocks)
        extent = jnp.where(doc == 0, first, jnp.where(doc == 1, second, 0))
        docs.append(doc)
        valid.append(extent - (b - start) * BLK)
    return valid, docs[0] == docs[1]


JOBS = (("down", 0), ("down", 1), ("up", 0), ("up", 1), ("inp", 0), ("inp", 1), ("misc", 0))


ORDER = (
    "nf0", "nx0", "cn", "nf1", "pa0", "pa1", "nx1", "np0", "pb0", "sc0", "at0", "cx0", "br0",
    "np1", "oa0", "pb1", "sc1", "at1", "cp0", "br1", "fe0", "oa1", "ns0", "mx0", "fa0", "ns1",
    "mx1", "mp0", "fb0", "cx1", "fa1", "ob0", "mp1", "cp1", "fb1", "gdown0", "nb0", "ob1",
    "kup1", "gup0", "bx0", "kdown0", "kup0", "ydown0", "nb1", "kdown1", "gup1", "xdown0",
    "oc1", "yup0", "gdown1", "zdown0", "bp0", "hb0", "xup0", "yup1", "bx1", "ab0", "zup0",
    "sb0", "xup1", "fe1", "sdown0", "bp1", "oc0", "pu0", "sup0", "zup1", "ydown1", "tdown0",
    "hb1", "ab1", "sup1", "tup0", "sb1", "pu1", "tup1", "ginp0", "od1", "xdown1", "kinp0",
    "mi0", "ginp1", "zdown1", "mi1", "od0", "kinp1", "yinp0", "nr1", "sdown1", "mo", "xinp0",
    "yinp1", "tdown1", "nr0", "gs", "zinp0", "pk", "gmisc0", "xinp1", "sinp0", "zinp1",
    "tinp0", "ymisc0", "sinp1", "xmisc0", "tinp1", "zmisc0", "smisc0", "tmisc0",
)


def make_tasks(o, st):
    tasks, needs = {}, {}

    def task(name, *before):
        def put(work):
            tasks[name] = work
            needs[name] = before

        return put

    def recv(*names):
        for name in names:
            st[name].wait_recv()

    def sent(*names):
        for name in names:
            for copy in st[name] if isinstance(st[name], (list, tuple)) else [st[name]]:
                o.sent(copy)

    @task("cn")
    def _():
        o.loads["cot0"].wait()
        o.loads["cot1"].wait()
        st["c_near0"] = o.share("cot", 0)
        st["c_near1"] = o.share("cot", 1)

    def per_micro(m):
        n = str(m)
        other = str(1 - m)

        @task("nf" + n)
        def _():
            o.norm_first(m)
            st["n_near" + n] = o.share("xn", m)

        @task("nx" + n, "nf" + n)
        def _():
            st["n_far" + n] = o.cross("xn", m)

        @task("np" + n, "nx" + n)
        def _():
            st["n_both" + n] = o.pass_on("xn", m, st["n_far" + n])

        @task("pa" + n, "nf" + n)
        def _():
            if m == 0:
                o.loads["in"].wait()
            recv("n_near" + n)
            o.project(m, False)

        @task("pb" + n, "np" + n, *(["pa0"] if m else []))
        def _():
            recv("n_both" + n)
            o.project(m, True)

        @task("sc" + n, "pa" + n, "pb" + n)
        def _():
            o.scan(m)

        @task("at" + n, "sc" + n, *(["at0"] if m else []))
        def _():
            if m:
                st["save"].wait()
            o.attend(m)
            st["save"] = o.save(m)

        @task("cx" + n, "cn")
        def _():
            st["c_far" + n] = o.cross("cot", m)

        @task("cp" + n, "cx" + n)
        def _():
            st["c_both" + n] = o.pass_on("cot", m, st["c_far" + n])

        @task("br" + n, "at" + n, *(["br0"] if m else []))
        def _():
            if m == 0:
                o.loads["out"].wait()
            st["br" + n] = o.branch(m, st["br0"] if m else [])

        @task("oa" + n, "br" + n)
        def _():
            st["oa" + n] = o.owed("a", st["br" + n], m)

        @task("ns" + n, "oa" + n)
        def _():
            o.norm_second(m, st["br" + n], st["oa" + n])
            st["m_near" + n] = o.share("n2", m)

        @task("mx" + n, "ns" + n)
        def _():
            st["m_far" + n] = o.cross("n2", m)

        @task("mp" + n, "mx" + n)
        def _():
            st["m_both" + n] = o.pass_on("n2", m, st["m_far" + n])

        @task("fa" + n, "ns" + n, "cn", *(["fb0"] if m else ["br1"]))
        def _():
            if m == 0:
                o.loads["up"].wait()
                o.loads["down"].wait()
                sent("br1")
            else:
                sent("fa0")
            sent("oa" + n)
            recv("c_near" + n, "m_near" + n)
            st["fa" + n] = o.feed(m, False)

        @task("fb" + n, "fa" + n, "mp" + n, "cp" + n)
        def _():
            if m:
                sent("fb0")
            recv("c_both" + n, "m_both" + n)
            st["fb" + n] = o.feed(m, True)

        @task("ob" + n, "fb" + n)
        def _():
            st["ob" + n] = o.owed("b", (st["fa" + n][1], st["fb" + n][1]), m)

        @task("oc" + n, "fb" + n)
        def _():
            st["oc" + n] = o.owed("a", (st["fa" + n][0], st["fb" + n][0]), m)

        @task("nb" + n, "ob" + n)
        def _():
            o.norm_second_back(m, (st["fa" + n][1], st["fb" + n][1]), st["ob" + n])
            st["b_near" + n] = o.share("gbr", m)

        @task("bx" + n, "nb" + n)
        def _():
            st["b_far" + n] = o.cross("gbr", m)

        @task("bp" + n, "bx" + n)
        def _():
            st["b_both" + n] = o.pass_on("gbr", m, st["b_far" + n])

        @task("fe" + n, "at1", *(["ab0"] if m else []))
        def _():
            if m == 0:
                st["save"].wait()
            st["fetch"] = o.fetch(m)

        @task("hb" + n, "bp" + n, *(["ab0"] if m else ["gdown0", "gdown1", "kdown0", "kdown1"]))
        def _():
            recv("b_near" + n, "b_both" + n)
            o.heads_back(m)

        @task("ab" + n, "hb" + n, "fe" + n, *(["sb0"] if m else []))
        def _():
            st["fetch"].wait()
            o.attend_back(m)

        @task("sb" + n, "ab" + n)
        def _():
            o.scan_back(m)

        @task("pu" + n, "sb" + n, *(["pu0"] if m else ["fb1"]))
        def _():
            sent("ob" + n)
            if m == 0:
                sent("fa1", "fb1")
            st["pu" + n] = o.pull_back(m, st["pu0"] if m else [])

        @task("od" + n, "pu" + n)
        def _():
            st["od" + n] = o.owed("b", st["pu" + n], m)

        @task("mi" + n, "oc" + n)
        def _():
            sent("oc" + n)
            st["end" + n] = o.mix(m, (st["fa" + n][0], st["fb" + n][0]), st["oc" + n])

        @task("nr" + n, "od" + n, "mi" + n)
        def _():
            st["fin" + n] = o.norm_first_back(m, st["pu" + n], st["od" + n])

    per_micro(0)
    per_micro(1)

    @task("mo", "hb0", "hb1", "br1")
    def _():
        o.make_out()

    @task("gs", "nr0", "nr1", "nb0", "nb1")
    def _():
        st["gains"] = o.send_gains()

    @task("pk", "gs", "mo", "sb0", "sb1")
    def _():
        o.pack(st["gains"])

    ready = dict(down=("fb0", "fb1"), up=("fb0", "fb1"), inp=("pu0", "pu1"), misc=("pk",))

    def per_job(job):
        name = job[0] + str(job[1])
        last = ready[job[0]]
        if job[0] != "misc":

            @task("g" + name, *last)
            def _():
                o.tile_give(job)
                st[name] = o.swap_y(job)

            @task("k" + name, *last)
            def _():
                o.tile_keep(job)

            ahead = ("g" + name, "k" + name)
        else:

            @task("g" + name, *last)
            def _():
                st[name] = o.swap_y(job)

            ahead = ("g" + name,)

        @task("y" + name, *ahead)
        def _():
            st[name] = o.sum_y(job, st[name])

        @task("x" + name, "y" + name)
        def _():
            st[name] = o.sum_x(job, st[name])

        @task("z" + name, "x" + name)
        def _():
            st[name] = o.sum_z(job, st[name])

        @task("s" + name, "z" + name)
        def _():
            st[name] = o.spread_y(job, st[name])

        @task("t" + name, "s" + name)
        def _():
            st[name] = o.spread_t(job, st[name])

    for job in JOBS:
        per_job(job)
    return tasks, needs


def run(o):
    st = {}
    tasks, needs = make_tasks(o, st)
    done = set()
    for name in ORDER:
        assert all(ahead in done for ahead in needs[name]), name
        tasks[name]()
        done.add(name)
    assert len(done) == len(tasks)
    for job in JOBS:
        o.finish(st[job[0] + str(job[1])])
    for name in ("end0", "end1", "fin0", "fin1"):
        st[name].wait()


class Copies:
    def __init__(self, send, recv):
        self.send, self.recv, self.used, self.open = send, recv, 0, []

    def start(self, source, target, device):
        copy = pltpu.make_async_remote_copy(
            src_ref=source,
            dst_ref=target,
            send_sem=self.send.at[self.used],
            recv_sem=self.recv.at[self.used],
            device_id=device,
            device_id_type=pl.DeviceIdType.MESH,
        )
        self.used += 1
        copy.start()
        self.open.append(copy)
        return copy

    def sent(self, copy):
        copy.wait_send()
        self.open = [other for other in self.open if other is not copy]

    def drain(self):
        for copy in self.open:
            copy.wait_send()
        self.open = []


class Moves:
    def __init__(self, sems):
        self.sems, self.used = sems, 0

    def start(self, source, target):
        copy = pltpu.make_async_copy(source, target, self.sems.at[self.used])
        self.used += 1
        copy.start()
        return copy


def layer(
    nz, tokens, lengths, cotangent, gain_one, gain_two, w_in, ssm, ctx_w, w_out, w_up, w_down
):
    count, rows, width = tokens.shape
    chans = w_out.shape[0]
    heads = chans // HD
    hidden = w_up.shape[1]
    total = 4 * rows
    pair = 2 * rows
    small_rows = heads * CTX + 3 * NS + 8
    unit = 2 * nz * 16
    misc_rows = width + small_rows + (-small_rows % unit)
    sizes = dict(down=(hidden, width), up=(width, hidden), inp=(width, 4 * chans), misc=(misc_rows, chans))
    names = list(sizes)
    share = {n: rows if sizes[n][1] == width else sizes[n][0] // 2 for n in names}
    n_jobs = sum(sizes[n][0] // 2 // share[n] for n in names)
    root = math.sqrt(2.0 / math.pi)
    n_remote = 51 + n_jobs * (1 + 2 * (nz - 1) + nz)
    n_local = 14 + n_jobs * (nz + 1)

    def kernel(*refs):
        (
            len_ref, tok, cot_hbm, g1, g2, in_hbm, rate, enter, leave, cw, out_hbm, up_hbm, down_hbm,
        ) = refs[:13]
        mixed_hbm, gtok_hbm, pr_hbm = refs[13:16]
        grads = dict(zip(names, refs[16:20]))
        ry = dict(zip(names, refs[20:24]))
        rz = dict(zip(names, refs[24:28]))
        (
            w_i, w_o, w_u, w_d, xn, cot, n2, gbr, hid, gbf, qkv, u0, pr, ho, cx, ckv, dh, gctx,
            give, keep_a, keep_b, sib_a, sib_b, far_a, far_b, mid, acc, tmp, land, misc,
            gain_acc, gain_got, gcw, gss, send_sems, recv_sems, local_sems,
        ) = refs[28:]
        me = lax.axis_index("mp")
        core, chip = me % 2, me // 2
        near, far, both = chip * 2 + 1 - core, (1 - chip) * 2 + core, (1 - chip) * 2 + 1 - core
        dp = lax.axis_index("dp")
        y, z = dp % 2, dp // 2
        to_near, to_far, to_both = {"mp": near}, {"mp": far}, {"mp": both}
        to_y = {"dp": z * 2 + 1 - y}
        zs = [(z + k) % nz for k in range(nz)]
        to_z = [{"dp": zk * 2 + y} for zk in zs]
        paired = nz == 4
        z_pair, z_cross = z + 1 - 2 * (z % 2), (z + 2) % nz
        z_other = (z_pair + 2) % nz
        to_pair, to_cross = {"dp": z_pair * 2 + y}, {"dp": z_cross * 2 + y}
        remote, local = Copies(send_sems, recv_sems), Moves(local_sems)

        loads = {
            "in": local.start(in_hbm, w_i),
            "cot0": local.start(cot_hbm.at[0], cot.at[0, me]),
            "cot1": local.start(cot_hbm.at[1], cot.at[1, me]),
            "out": local.start(out_hbm, w_o),
            "up": local.start(up_hbm, w_u),
            "down": local.start(down_hbm, w_d),
        }
        barrier = pltpu.get_barrier_semaphore()
        for device in [to_near, to_far, to_both, to_y] + to_z[1:]:
            pl.semaphore_signal(
                barrier, inc=1, device_id=device, device_id_type=pl.DeviceIdType.MESH
            )
        pl.semaphore_wait(barrier, 3 + nz)

        def share_piece(buf, m):
            return remote.start(buf.at[m, me], buf.at[m, me], to_near)

        def cross(buf, m):
            return remote.start(buf.at[m, me], buf.at[m, me], to_far)

        def pass_on(buf, m, copy):
            copy.wait_recv()
            return remote.start(buf.at[m, far], buf.at[m, far], to_near)

        def offer(kind, slot, sib, m):
            return remote.start(give.at[kind, slot], sib.at[m, slot], to_near)

        def by_rows(work):
            step = 64

            def body(i, carry):
                work(pl.ds(pl.multiple_of(i * step, step), step))
                return carry

            lax.fori_loop(0, rows // step, body, 0)

        def owed(offers, keep, sib, far_buf, m):
            offers[1].wait_recv()

            def work(at):
                keep[m, 1, at, :] = (
                    keep[m, 1, at, :].astype(F32) + sib[m, 1, at, :].astype(F32)
                ).astype(BF16)

            by_rows(work)
            return remote.start(keep.at[m, 1], far_buf.at[m], to_far)

        def summed(offers, copy, keep, sib, far_buf, m):
            offers[0].wait_recv()
            copy.wait_recv()
            return lambda at: (
                keep[m, 0, at, :].astype(F32)
                + sib[m, 0, at, :].astype(F32)
                + far_buf[m, at, :].astype(F32)
            )

        def inverse_root(value):
            return lax.rsqrt(jnp.mean(value * value, axis=-1, keepdims=True) + EPS)

        def norm_first(m):
            def work(at):
                x = tok[m, at, :].astype(F32)
                xn[m, me, at, :] = (x * inverse_root(x) * g1[...]).astype(BF16)

            by_rows(work)

        def norm_second(m, branch):
            def work(at):
                value = tok[m, at, :].astype(F32) + branch(at)
                mid[m, at, :] = value
                n2[m, me, at, :] = (value * inverse_root(value) * g2[...]).astype(BF16)

            by_rows(work)

        def pulled(value, grad, gain, line):
            scale = inverse_root(value)
            unit_row = value * scale
            gain_acc[line : line + 1, :] += jnp.sum(grad * unit_row, axis=0, keepdims=True)
            inner = grad * gain[...]
            return scale * (inner - unit_row * jnp.mean(inner * unit_row, axis=-1, keepdims=True))

        def norm_second_back(m, grad):
            def work(at):
                value = cot[m, me, at, :].astype(F32) + pulled(mid[m, at, :], grad(at), g2, 1)
                gbr[m, me, at, :] = value.astype(BF16)

            by_rows(work)

        def norm_first_back(m, grad):
            def work(at):
                x = tok[m, at, :].astype(F32)
                mid[m, at, :] = gbr[m, me, at, :].astype(F32) + pulled(x, grad(at), g1, 0)

            by_rows(work)
            return local.start(mid.at[m], gtok_hbm.at[m])

        def mix(m, branch):
            def work(at):
                keep_a[m, 0, at, :] = (mid[m, at, :] + branch(at)).astype(BF16)

            by_rows(work)
            return local.start(keep_a.at[m, 0], mixed_hbm.at[m])

        def project(m, side):
            def body(i, carry):
                t = side * 2 + i
                at = pl.ds(pl.multiple_of(t * rows, rows), rows)
                x = xn[m, t]
                qkv[m, at, :] = dot(x, w_i[:, : 3 * chans]).astype(BF16)

                @pl.when(t < 2)
                def _():
                    u0[m, at, :] = dot(x, w_i[:, 3 * chans :])

                return carry

            lax.fori_loop(0, 2, body, 0)

        def scan(m):
            context = state_forward(u0.at[m], rate, enter, leave).astype(BF16)
            cx[m] = context
            for h in range(heads):
                ckv[m, h] = dot(context[:, h * HD : (h + 1) * HD], cw[h]).astype(BF16)

        def attend(m):
            valid, linked = layout_scalars(len_ref, m)
            for h in range(heads):
                lanes = slice(h * HD, (h + 1) * HD)
                klanes = slice(chans + h * HD, chans + (h + 1) * HD)
                vlanes = slice(2 * chans + h * HD, 2 * chans + (h + 1) * HD)
                for b in range(2):
                    for half in range(2):
                        row0 = half * rows
                        keys = row0 + rows
                        spot = b * BLK + row0
                        q = qkv[m, spot : spot + rows, lanes]
                        k = qkv[m, b * BLK : b * BLK + keys, klanes]
                        v = qkv[m, b * BLK : b * BLK + keys, vlanes]
                        s = dot_nt(q, k) * SCALE2
                        row = lax.broadcasted_iota(jnp.int32, (rows, keys), 0) + row0
                        col = lax.broadcasted_iota(jnp.int32, (rows, keys), 1)
                        allowed = (col < jnp.minimum(row, valid[b])) | (col == row)
                        s = jnp.where(allowed, s, NEG)
                        peak = jnp.max(s, axis=-1, keepdims=True)
                        if b:
                            sc = dot_nt(q, ckv[m, h, :, :HD]) * SCALE2
                            sc = jnp.where(linked, sc, NEG)
                            peak = jnp.maximum(peak, jnp.max(sc, axis=-1, keepdims=True))
                            ec = jnp.exp2(sc - peak)
                        e = jnp.exp2(s - peak)
                        norm = jnp.sum(e, axis=-1, keepdims=True)
                        if b:
                            norm = norm + jnp.sum(ec, axis=-1, keepdims=True)
                        inverse = 1.0 / norm
                        p = (e * inverse).astype(BF16)
                        pr[h, b, row0 : row0 + rows, CTX : CTX + keys] = p
                        o = dot(p, v)
                        if b:
                            pc = (ec * inverse).astype(BF16)
                            pr[h, b, row0 : row0 + rows, :CTX] = pc
                            o = o + dot(pc, ckv[m, h, :, HD:])
                        ho[m, 2 * b + half, :, lanes] = o.astype(BF16)

        def spread(product, keep, kind, sib, m, before):
            for copy in before:
                remote.sent(copy)
            give[kind, 1] = product(both).astype(BF16)
            second = offer(kind, 1, sib, m)
            give[kind, 0] = product(near).astype(BF16)
            first = offer(kind, 0, sib, m)
            keep[m, 1] = product(far).astype(BF16)
            keep[m, 0] = product(me).astype(BF16)
            return [first, second]

        def feed(m, side, other):
            slot = 1 if other else 0

            def body(i, carry):
                t = side * 2 + jnp.where(i == 0, 1 - core, core)
                for start in range(0, hidden, 256):
                    cut = slice(start, start + 256)
                    before = dot(n2[m, t], w_u[:, cut])
                    square = before * before
                    th = jnp.tanh(root * (before * (1.0 + 0.044715 * square)))
                    half = 0.5 + 0.5 * th
                    hid[m, t, :, cut] = (before * half).astype(BF16)
                    slope = half + (0.5 * root) * before * (1.0 - th * th) * (
                        1.0 + 0.134145 * square
                    )
                    gbf[m, t, :, cut] = (dot_nt(cot[m, t], w_d[cut, :]) * slope).astype(BF16)
                branch = dot(hid[m, t], w_d[...]).astype(BF16)
                gn = dot_nt(gbf[m, t], w_u[...]).astype(BF16)

                @pl.when(i == 0)
                def _():
                    give[0, slot] = branch
                    give[1, slot] = gn

                @pl.when(i == 1)
                def _():
                    keep_a[m, slot] = branch
                    keep_b[m, slot] = gn

                return carry

            lax.fori_loop(0, 2, body, 0)
            return offer(0, slot, sib_a, m), offer(1, slot, sib_b, m)

        def heads_back(m):
            def body(t, carry):
                at = pl.ds(pl.multiple_of(t * rows, rows), rows)
                dh[at, :] = dot_nt(gbr[m, t], w_o[...]).astype(BF16)
                return carry

            lax.fori_loop(0, 4, body, 0)

        def attend_back(m):
            for h in range(heads):
                lanes = slice(h * HD, (h + 1) * HD)
                klanes = slice(chans + h * HD, chans + (h + 1) * HD)
                vlanes = slice(2 * chans + h * HD, 2 * chans + (h + 1) * HD)
                for b in range(2):
                    grad_k, grad_v = [None, None], [None, None]
                    grad_c = grad_cv = None
                    for half in (1, 0):
                        row0 = half * rows
                        keys = row0 + rows
                        spot = slice(b * BLK + row0, b * BLK + row0 + rows)
                        go = dh[spot, lanes]
                        qh = qkv[m, spot, lanes]
                        kh = qkv[m, b * BLK : b * BLK + keys, klanes]
                        vh = qkv[m, b * BLK : b * BLK + keys, vlanes]
                        p = pr[h, b, row0 : row0 + rows, CTX : CTX + keys]
                        pf = p.astype(F32)
                        dprob = dot_nt(go, vh)
                        delta = jnp.sum(dprob * pf, axis=-1, keepdims=True)
                        if b:
                            pc = pr[h, b, row0 : row0 + rows, :CTX]
                            pcf = pc.astype(F32)
                            dpc = dot_nt(go, ckv[m, h, :, HD:])
                            delta = delta + jnp.sum(dpc * pcf, axis=-1, keepdims=True)
                            dsc = (pcf * (dpc - delta)).astype(BF16)
                        ds = (pf * (dprob - delta)).astype(BF16)
                        dq = dot(ds, kh)
                        if b:
                            dq = dq + dot(dsc, ckv[m, h, :, :HD])
                            one = dot_tn(dsc, qh)
                            two = dot_tn(pc, go)
                            grad_c = one if grad_c is None else grad_c + one
                            grad_cv = two if grad_cv is None else grad_cv + two
                        hid[m, 2 * b + half, :, lanes] = (dq * SCALE).astype(BF16)
                        dk = dot_tn(ds, qh)
                        dv = dot_tn(p, go)
                        if half:
                            grad_k = [dk[:rows], dk[rows:]]
                            grad_v = [dv[:rows], dv[rows:]]
                        else:
                            grad_k[0] = grad_k[0] + dk
                            grad_v[0] = grad_v[0] + dv
                    for part in range(2):
                        t = 2 * b + part
                        hid[m, t, :, klanes] = (grad_k[part] * SCALE).astype(BF16)
                        hid[m, t, :, vlanes] = grad_v[part].astype(BF16)
                    if b:
                        low_c = (grad_c * SCALE).astype(BF16)
                        low_cv = grad_cv.astype(BF16)
                        ch = cx[m, :, lanes]
                        gcw[m, h, :, :HD] = dot_tn(ch, low_c)
                        gcw[m, h, :, HD:] = dot_tn(ch, low_cv)
                        gctx[:, lanes] = dot_nt(low_c, cw[h, :, :HD]) + dot_nt(
                            low_cv, cw[h, :, HD:]
                        )

        def scan_back(m):
            state_backward(gctx[...], u0.at[m], u0.at[m], rate, enter, leave, gss.at[m])
            for t in range(2):
                hid[m, t, :, 3 * chans :] = u0[m, t * rows : (t + 1) * rows, :].astype(BF16)
                hid[m, 2 + t, :, 3 * chans :] = jnp.zeros((rows, chans), BF16)

        def gather_tile(left, right, tile):
            lanes = pl.ds(pl.multiple_of(tile * rows, rows), rows)
            acc[...] = jnp.zeros_like(acc)

            def body(i, carry):
                m, t = i // 4, i % 4
                acc[...] += dot_tn(left[m, t, :, lanes], right[m, t])
                return carry

            lax.fori_loop(0, 4 * count, body, 0)

        def part(ref, start, size):
            return ref.at[pl.ds(pl.multiple_of(start, 16), size), :]

        def job_rows(job, side):
            name, i = job
            span = sizes[name][0] // 2
            if sizes[name][1] != width:
                return side * span, span
            return side * span + i * rows, rows

        stages = dict(down=w_d, up=w_u, inp=w_i, misc=misc)
        sides = dict(down=(hid, cot), up=(n2, gbf), inp=(xn, hid))

        def tile(job, side):
            start, size = job_rows(job, side)
            gather_tile(*sides[job[0]], start // size)
            stages[job[0]][pl.ds(pl.multiple_of(start, size), size), :] = acc[...].astype(BF16)

        def tile_give(job):
            tile(job, 1 - y)

        def tile_keep(job):
            tile(job, y)

        def landing(job, size):
            if sizes[job[0]][1] != width:
                return tmp.at[pl.ds(0, size), :]
            return land.at[pl.ds(0, size), :]

        def swap_y(job):
            name, i = job
            start, size = job_rows(job, 1 - y)
            return remote.start(part(stages[name], start, size), ry[name].at[i], to_y)

        def sum_y(job, copy):
            name, i = job
            stage = stages[name]
            start, size = job_rows(job, y)
            piece = size // nz
            copy.wait_recv()
            got = landing(job, size)
            local.start(ry[name].at[i], got).wait()
            at = pl.ds(pl.multiple_of(start, 16), size)
            stage[at, :] = (stage[at, :].astype(F32) + got[...].astype(F32)).astype(BF16)
            if paired:
                return [
                    remote.start(part(stage, start + t * piece, piece), rz[name].at[i, k], to_pair)
                    for k, t in enumerate((z_pair, z_other))
                ]
            return [
                remote.start(
                    part(stage, start + zs[k] * piece, piece), rz[name].at[i, k - 1], to_z[k]
                )
                for k in range(1, nz)
            ]

        def add_landed(job, at, slots):
            name, i = job
            stage = stages[name]
            piece = job_rows(job, y)[1] // nz
            got = landing(job, len(slots) * piece)
            moves = [
                local.start(rz[name].at[i, slot], got.at[pl.ds(k * piece, piece), :])
                for k, slot in enumerate(slots)
            ]
            for move in moves:
                move.wait()
            value = stage[at, :].astype(F32)
            for k in range(len(slots)):
                value = value + got[k * piece : (k + 1) * piece, :].astype(F32)
            stage[at, :] = value.astype(BF16)

        def sum_x(job, copies):
            if not paired:
                return copies
            name, i = job
            start, size = job_rows(job, y)
            piece = size // nz
            spot = start + z_cross * piece
            copies[1].wait_recv()
            add_landed(job, pl.ds(pl.multiple_of(spot, 16), piece), (1,))
            mine = part(stages[name], spot, piece)
            return [copies[0], remote.start(mine, rz[name].at[i, 2], to_cross)]

        def sum_z(job, copies):
            name, i = job
            start, size = job_rows(job, y)
            piece = size // nz
            for copy in copies:
                copy.wait_recv()
            spot = start + z * piece
            slots = (0, 2) if paired else tuple(range(nz - 1))
            add_landed(job, pl.ds(pl.multiple_of(spot, 16), piece), slots)
            mine = part(stages[name], spot, piece)
            place = part(grads[name], spot, piece)
            outs = [remote.start(mine, place, d) for d in ([to_pair, to_cross] if paired else to_z[1:])]
            last = [remote.start(mine, place, to_y)]
            return outs, last, local.start(mine, place)

        def spread_y(job, state):
            name, i = job
            start, size = job_rows(job, y)
            piece = size // nz
            outs, last, move = state
            if paired:
                whose = (z_pair, z_cross)
            else:
                whose = [(z + nz - k) % nz for k in range(1, nz)]
            on = None
            for copy, owner in zip(outs, whose):
                copy.wait_recv()
                place = part(grads[name], start + owner * piece, piece)
                last.append(remote.start(place, place, to_y))
                if paired and owner is z_cross:
                    on = remote.start(place, place, to_pair)
            return last, move, on

        def spread_t(job, state):
            name, i = job
            start, size = job_rows(job, y)
            last, move, on = state
            if paired:
                on.wait_recv()
                piece = size // nz
                place = part(grads[name], start + z_other * piece, piece)
                last.append(remote.start(place, place, to_y))
            return last, move

        def finish(state):
            last, move = state
            for copy in last:
                copy.wait_recv()
            move.wait()

        def make_out():
            gather_tile(ho, gbr, 0)
            for j in range(width // chans):
                misc[j * chans : (j + 1) * chans, :] = acc[:, j * chans : (j + 1) * chans].astype(
                    BF16
                )

        def send_gains():
            return [
                remote.start(gain_acc, gain_got.at[k], device)
                for k, device in enumerate((to_near, to_far, to_both))
            ]

        def pack(copies):
            base = width
            for h in range(heads):
                misc[base + h * CTX : base + (h + 1) * CTX, :] = (gcw[0, h] + gcw[1, h]).astype(BF16)
            base += heads * CTX
            for k in range(3):
                misc[base + k * NS : base + (k + 1) * NS, :] = (gss[0, k] + gss[1, k]).astype(BF16)
            base += 3 * NS
            for copy in copies:
                copy.wait_recv()
            value = gain_acc[...] + gain_got[0] + gain_got[1] + gain_got[2]
            line = jnp.concatenate(
                [value[r : r + 1, j * chans : (j + 1) * chans] for r in range(2) for j in range(4)],
                axis=0,
            )
            misc[base:, :] = jnp.concatenate(
                [line, jnp.zeros((misc_rows - base - 8, chans), F32)], axis=0
            ).astype(BF16)

        def branch(m, before):
            return spread(lambda t: dot(ho[m, t], w_o[...]), keep_a, 0, sib_a, m, before)

        def pull_back(m, before):
            return spread(lambda t: dot_nt(hid[m, t], w_i[...]), keep_b, 1, sib_b, m, before)

        bufs = dict(xn=xn, cot=cot, n2=n2, gbr=gbr)
        sets = dict(a=(keep_a, sib_a, far_a), b=(keep_b, sib_b, far_b))
        o = types.SimpleNamespace(
            count=count,
            norm_first=norm_first,
            share=lambda buf, m: share_piece(bufs[buf], m),
            cross=lambda buf, m: cross(bufs[buf], m),
            pass_on=lambda buf, m, copy: pass_on(bufs[buf], m, copy),
            sent=remote.sent,
            loads=loads,
            project=lambda m, other: project(m, 1 - chip if other else chip),
            scan=scan,
            attend=attend,
            save=lambda m: local.start(pr, pr_hbm.at[m]),
            fetch=lambda m: local.start(pr_hbm.at[m], pr),
            branch=branch,
            owed=lambda kind, offers, m: owed(offers, *sets[kind], m),
            norm_second=lambda m, of, cp: norm_second(m, summed(of, cp, *sets["a"], m)),
            norm_second_back=lambda m, of, cp: norm_second_back(m, summed(of, cp, *sets["b"], m)),
            norm_first_back=lambda m, of, cp: norm_first_back(m, summed(of, cp, *sets["b"], m)),
            mix=lambda m, of, cp: mix(m, summed(of, cp, *sets["a"], m)),
            feed=lambda m, other: feed(m, 1 - chip if other else chip, other),
            heads_back=heads_back,
            attend_back=attend_back,
            scan_back=scan_back,
            pull_back=pull_back,
            tile_give=tile_give,
            tile_keep=tile_keep,
            swap_y=swap_y,
            sum_y=sum_y,
            sum_x=sum_x,
            sum_z=sum_z,
            spread_y=spread_y,
            spread_t=spread_t,
            finish=finish,
            make_out=make_out,
            send_gains=send_gains,
            pack=pack,
        )
        gain_acc[...] = jnp.zeros_like(gain_acc)
        run(o)
        remote.drain()
        assert remote.used <= n_remote and local.used <= n_local, (remote.used, local.used)

    pieces = (count, 4, rows)
    vm = pltpu.VMEM
    any_out = [
        shape((count, rows, width), BF16),
        shape((count, rows, width), F32),
        shape((count, heads, 2, BLK, BLK + CTX), BF16),
    ]
    any_out += [shape(sizes[n], BF16) for n in names]
    any_out += [
        shape((sizes[n][0] // 2 // share[n], share[n], sizes[n][1]), BF16) for n in names
    ]
    any_out += [
        shape((sizes[n][0] // 2 // share[n], nz - 1, share[n] // nz, sizes[n][1]), BF16)
        for n in names
    ]
    results = pl.pallas_call(
        kernel,
        in_specs=[SMEM, VMEM, ANY, VMEM, VMEM, ANY, VMEM, VMEM, VMEM, VMEM, ANY, ANY, ANY],
        out_specs=[ANY] * len(any_out),
        out_shape=any_out,
        scratch_shapes=[
            vm(w_in.shape, BF16),
            vm(w_out.shape, BF16),
            vm(w_up.shape, BF16),
            vm(w_down.shape, BF16),
            vm(pieces + (width,), BF16),
            vm(pieces + (width,), BF16),
            vm(pieces + (width,), BF16),
            vm(pieces + (width,), BF16),
            vm(pieces + (hidden,), BF16),
            vm(pieces + (hidden,), BF16),
            vm((count, total, 3 * chans), BF16),
            vm((count, BLK, chans), F32),
            vm((heads, 2, BLK, BLK + CTX), BF16),
            vm(pieces + (chans,), BF16),
            vm((count, CTX, chans), BF16),
            vm((count, heads, CTX, 2 * HD), BF16),
            vm((total, chans), BF16),
            vm((CTX, chans), F32),
            vm((2, 2, rows, width), BF16),
            vm((count, 2, rows, width), BF16),
            vm((count, 2, rows, width), BF16),
            vm((count, 2, rows, width), BF16),
            vm((count, 2, rows, width), BF16),
            vm((count, rows, width), BF16),
            vm((count, rows, width), BF16),
            vm((count, rows, width), F32),
            vm((rows, width), F32),
            vm((misc_rows // 2, chans), BF16),
            vm((rows, width), BF16),
            vm((misc_rows, chans), BF16),
            vm((8, width), F32),
            vm((3, 8, width), F32),
            vm((count, heads, CTX, 2 * HD), F32),
            vm((count, 3, NS, chans), F32),
            pltpu.SemaphoreType.DMA((n_remote,)),
            pltpu.SemaphoreType.DMA((n_remote,)),
            pltpu.SemaphoreType.DMA((n_local,)),
        ],
        compiler_params=pltpu.CompilerParams(
            collective_id=0, has_side_effects=True, vmem_limit_bytes=63 << 20
        ),
        cost_estimate=cost(45e9, 60e6),
    )(lengths, tokens, cotangent, gain_one, gain_two, w_in, *ssm, ctx_w, w_out, w_up, w_down)
    return results[0], results[1], dict(zip(names, results[3:7]))


def publish(mixed, grad_tokens, grads, in_shape, ctx_shape, out_shape):
    count, rows, width = mixed.shape
    heads = ctx_shape[0]
    chans = in_shape[2]
    steps = 8
    parts = width // chans
    misc_rows = grads["misc"].shape[0]

    def kernel(m_ref, t_ref, d_ref, u_ref, i_ref, misc_ref, *outs):
        mo, to, do, uo, io, oo, co, ra, en, le, ga, gb = outs
        mo[...] = m_ref[...]
        to[...] = t_ref[...]
        do[...] = d_ref[...].astype(F32)
        uo[...] = u_ref[...].astype(F32)
        for k in range(in_shape[1]):
            io[:, k, :] = i_ref[:, k * chans : (k + 1) * chans].astype(F32)

        @pl.when(pl.program_id(0) == 0)
        def _():
            for j in range(parts):
                oo[:, j * chans : (j + 1) * chans] = misc_ref[
                    j * chans : (j + 1) * chans, :
                ].astype(F32)
            at = width
            for h in range(heads):
                co[h] = misc_ref[at + h * CTX : at + (h + 1) * CTX, :].astype(F32)
            at += heads * CTX
            for k, ref in enumerate((ra, en, le)):
                ref[...] = misc_ref[at + k * NS : at + (k + 1) * NS, :].astype(F32)
            at += 3 * NS
            tail = misc_ref[at : at + 16, :].astype(F32)
            for r, ref in enumerate((ga, gb)):
                for j in range(parts):
                    ref[:, j * chans : (j + 1) * chans] = tail[r * parts + j : r * parts + j + 1, :]

    def blocks(dims):
        return pl.BlockSpec((dims[0] // steps,) + dims[1:], lambda i: (i,) + (0,) * (len(dims) - 1))

    def whole(dims):
        return pl.BlockSpec(dims, lambda i: (0,) * len(dims))

    token_block = pl.BlockSpec((count, rows // steps, width), lambda i: (0, i, 0))
    small = [out_shape, ctx_shape] + [(NS, chans)] * 3 + [(1, width)] * 2
    big = [grads["down"].shape, grads["up"].shape]
    return pl.pallas_call(
        kernel,
        grid=(steps,),
        in_specs=[token_block] * 2
        + [blocks(d) for d in big]
        + [blocks(grads["inp"].shape), whole((misc_rows, chans))],
        out_specs=[token_block] * 2
        + [blocks(d) for d in big]
        + [blocks(in_shape)]
        + [whole(d) for d in small],
        out_shape=[shape(mixed.shape, BF16), shape(mixed.shape, F32)]
        + [shape(d, F32) for d in big + [in_shape] + small],
        compiler_params=params(40),
        cost_estimate=cost(0, 28e6),
    )(mixed, grad_tokens, grads["down"], grads["up"], grads["inp"], grads["misc"])


def body(
    tokens,
    lengths,
    cotangent,
    attn_gain,
    in_weights,
    ssm_rate,
    ssm_input,
    ssm_output,
    ctx_weights,
    out_weights,
    mlp_gain,
    up_weights,
    down_weights,
):
    width = tokens.shape[2]
    chans = out_weights.shape[0]
    mixed, grad_tokens, grads = layer(
        lax.axis_size("dp") // 2,
        tokens,
        lengths[0],
        cotangent,
        attn_gain.reshape(1, width),
        mlp_gain.reshape(1, width),
        in_weights.reshape(width, 4 * chans),
        (ssm_rate, ssm_input, ssm_output),
        ctx_weights,
        out_weights,
        up_weights,
        down_weights,
    )
    mixed, grad_tokens, down, up, inp, out, ctx, rate, enter, leave, one, two = publish(
        mixed, grad_tokens, grads, in_weights.shape, ctx_weights.shape, out_weights.shape
    )
    return (
        mixed,
        grad_tokens,
        one.reshape(width),
        inp,
        rate,
        enter,
        leave,
        ctx,
        out,
        two.reshape(width),
        up,
        down,
    )


def solution(mesh):
    rows = P(None, ("dp", "mp"), None)
    return jax.shard_map(
        body,
        mesh=mesh,
        in_specs=(
            rows,
            P("dp", None, None),
            rows,
            P(),
            P(None, None, "mp"),
            P(None, "mp"),
            P(None, "mp"),
            P(None, "mp"),
            P("mp", None, None),
            P("mp", None),
            P(),
            P(None, "mp"),
            P("mp", None),
        ),
        out_specs=(
            rows,
            rows,
            P(),
            P(None, None, "mp"),
            P(None, "mp"),
            P(None, "mp"),
            P(None, "mp"),
            P("mp", None, None),
            P("mp", None),
            P(),
            P(None, "mp"),
            P("mp", None),
        ),
        check_vma=False,
    )
```

```python
import functools
import math
import types

import jax
import jax.numpy as jnp
from jax import lax
from jax.experimental import pallas as pl
from jax.experimental.pallas import tpu as pltpu
from jax.sharding import PartitionSpec as P

HD = 128
BLK = 512
CTX = 128
HEAD = BLK - CTX
NS = 16
EPS = 1e-05
SCALE = 1.0 / math.sqrt(HD)
SCALE2 = SCALE * math.log2(math.e)
NEG = -1e30
F32 = jnp.float32
BF16 = jnp.bfloat16

VMEM = pl.BlockSpec(memory_space=pltpu.VMEM)
SMEM = pl.BlockSpec(memory_space=pltpu.SMEM)
ANY = pl.BlockSpec(memory_space=pl.ANY)


def params(mib):
    return pltpu.CompilerParams(vmem_limit_bytes=mib << 20)


def cost(flops, nbytes):
    return pl.CostEstimate(flops=int(flops), bytes_accessed=int(nbytes), transcendentals=0)


def dot(a, b):
    return lax.dot_general(a, b, (((1,), (0,)), ((), ())), preferred_element_type=F32)


def dot_nt(a, b):
    return lax.dot_general(a, b, (((1,), (1,)), ((), ())), preferred_element_type=F32)


def dot_tn(a, b):
    return lax.dot_general(a, b, (((0,), (0,)), ((), ())), preferred_element_type=F32)


def shape(dims, kind):
    return jax.ShapeDtypeStruct(dims, kind)


def triangle(upper):
    row = lax.broadcasted_iota(jnp.int32, (CTX, 2 * CTX), 0)
    col = lax.broadcasted_iota(jnp.int32, (CTX, 2 * CTX), 1) % CTX
    keep = (row <= col) if upper else (row >= col)
    return jnp.where(keep, 1.0, 0.0).astype(BF16)


def running(tri, values):
    high = values.astype(BF16)
    rest = (values - high.astype(F32)).astype(BF16)
    return dot(tri, jnp.concatenate([high, rest], axis=0))


def head_sums(u_ref, rate_ref, moment):
    width = rate_ref.shape[1]
    place = lax.broadcasted_iota(jnp.int32, (8, width), 0).astype(F32)
    sums, moments = [], []
    group = 4 if moment else 8
    for base in range(0, NS, group):
        rates = [rate_ref[n : n + 1, :] for n in range(base, base + group)]
        steps = [jnp.broadcast_to(jnp.exp(-8.0 * r), (8, width)) for r in rates]

        def body(chunk, carry):
            start = pl.multiple_of(chunk * 8, 8)
            rows = u_ref[pl.ds(start, 8), :]
            first = [acc * step + rows for acc, step in zip(carry[0], steps)]
            if not moment:
                return (first, carry[1])
            scaled = rows * (place + (chunk * 8 - HEAD).astype(F32))
            second = [acc * step + scaled for acc, step in zip(carry[1], steps)]
            return (first, second)

        zero = [jnp.zeros((8, width), F32) for _ in range(group)]
        first, second = lax.fori_loop(
            0, HEAD // 8, body, (zero, list(zero) if moment else []), unroll=4
        )
        for k, rate in enumerate(rates):
            last = jnp.exp(rate * (place - 8.0))
            sums.append(jnp.sum(first[k] * last, axis=0, keepdims=True))
            if moment:
                moments.append(jnp.sum(second[k] * last, axis=0, keepdims=True))
    return sums, moments


def state_forward(u_ref, rate_ref, in_ref, out_ref):
    width = rate_ref.shape[1]
    sums, _ = head_sums(u_ref, rate_ref, False)
    tail = u_ref[pl.ds(HEAD, CTX), :]
    time = lax.broadcasted_iota(jnp.int32, (CTX, width), 0).astype(F32)
    tri = triangle(False)
    total = jnp.zeros((CTX, width), F32)
    for n in range(NS):
        rate = rate_ref[n : n + 1, :]
        gain = in_ref[n : n + 1, :] * jnp.sqrt(1.0 - jnp.exp(-2.0 * rate))
        weight = gain * out_ref[n : n + 1, :]
        prefix = running(tri, jnp.exp(rate * time) * tail)
        total = total + weight * (jnp.exp(-rate * time) * (sums[n] + prefix))
    return total


def state_backward(grad, u_ref, du_ref, rate_ref, in_ref, out_ref, gs_ref):
    width = rate_ref.shape[1]
    sums, moments = head_sums(u_ref, rate_ref, True)
    tail = u_ref[pl.ds(HEAD, CTX), :]
    time = lax.broadcasted_iota(jnp.int32, (CTX, width), 0).astype(F32)
    place = lax.broadcasted_iota(jnp.int32, (8, width), 0).astype(F32)
    lower, upper = triangle(False), triangle(True)
    total = jnp.zeros((CTX, width), F32)
    starts = []
    for n in range(NS):
        rate = rate_ref[n : n + 1, :]
        root = jnp.sqrt(1.0 - jnp.exp(-2.0 * rate))
        enter = in_ref[n : n + 1, :]
        leave = out_ref[n : n + 1, :]
        gain = enter * root
        rising = jnp.exp(rate * time)
        driven = rising * tail
        states = sums[n] + running(lower, driven)
        seen = jnp.exp(-rate * time) * grad
        later = running(upper, seen)
        product = seen * states
        energy = jnp.sum(product, axis=0, keepdims=True)
        slope = jnp.sum(time * (product - driven * later), axis=0, keepdims=True)
        slope = slope - later[0:1] * moments[n]
        total = total + (gain * leave) * (rising * later)
        starts.append((gain * leave) * later[0:1])
        gs_ref[0, n : n + 1, :] = leave * (
            energy * enter * jnp.exp(-2.0 * rate) / root - gain * slope
        )
        gs_ref[1, n : n + 1, :] = leave * energy * root
        gs_ref[2, n : n + 1, :] = gain * energy
    du_ref[pl.ds(HEAD, CTX), :] = total
    group = 8
    for base in range(0, NS, group):
        rates = [rate_ref[n : n + 1, :] for n in range(base, base + group)]
        steps = [jnp.broadcast_to(jnp.exp(-8.0 * r), (8, width)) for r in rates]
        begin = [
            starts[base + k] * jnp.exp(rate * (place - 8.0)) for k, rate in enumerate(rates)
        ]

        def body(index, carry):
            start = pl.multiple_of(HEAD - 8 - index * 8, 8)
            value = functools.reduce(lambda a, b: a + b, carry)
            if base:
                value = value + du_ref[pl.ds(start, 8), :]
            du_ref[pl.ds(start, 8), :] = value
            return [c * step for c, step in zip(carry, steps)]

        lax.fori_loop(0, HEAD // 8, body, begin, unroll=4)


def layout_scalars(len_ref, micro):
    first, second = len_ref[micro, 0], len_ref[micro, 1]
    first_blocks = (first + (BLK - 1)) // BLK
    second_blocks = (second + (BLK - 1)) // BLK
    docs, valid = [], []
    for b in range(2):
        doc = jnp.where(b < first_blocks, 0, jnp.where(b < first_blocks + second_blocks, 1, 2))
        start = jnp.where(doc == 0, 0, first_blocks)
        extent = jnp.where(doc == 0, first, jnp.where(doc == 1, second, 0))
        docs.append(doc)
        valid.append(extent - (b - start) * BLK)
    return valid, docs[0] == docs[1]


ALL = (("down", 0), ("down", 1), ("up", 0), ("up", 1), ("inp", 0), ("inp", 1), ("misc", 0))
ALONG_Z = (("down", 0),)
JOBS = tuple(job for job in ALL if job not in ALONG_Z)
FIRST = tuple((name, i + 2 * half) for name, i in ALONG_Z for half in range(2))


ORDER = (
    "nf0", "nx0", "cn", "nf1", "pa0", "pa1", "nx1", "np0", "pb0", "sc0", "at0", "cx0", "br0",
    "np1", "oa0", "pb1", "sc1", "at1", "br1", "cp0", "fe0", "oa1", "ns0", "mx0", "fa0", "ns1",
    "mx1", "mp0", "fb0", "cx1", "fa1", "mp1", "ob0", "cp1", "fb1", "gdown1", "gfdown2", "nb0",
    "ob1", "kup0", "gfdown0", "bx0", "kdown1", "xfdown2", "gup0", "gup1", "ydown1", "xfdown0",
    "kup1", "zfdown2", "nb1", "xdown1", "bx1", "yup0", "zfdown0", "bp0", "zdown1", "hb0",
    "ab0", "xup0", "oc1", "fe1", "yup1", "bp1", "sb0", "zup0", "sdown1", "hb1", "ab1", "pu0",
    "mi1", "xup1", "wfdown0", "sup0", "oc0", "sb1", "tdown1", "pu1", "ginp0", "kinp1", "od1",
    "sfdown0", "kinp0", "zup1", "mi0", "tup0", "ginp1", "od0", "mo", "wfdown2", "yinp0",
    "sup1", "nr1", "sfdown2", "xinp0", "tup1", "nr0", "gs", "yinp1", "pk", "gmisc0", "zinp0",
    "xinp1", "sinp0", "ymisc0", "zinp1", "tinp0", "xmisc0", "sinp1", "zmisc0", "tinp1",
    "smisc0", "tmisc0",
)


def make_tasks(o, st):
    tasks, needs = {}, {}

    def task(name, *before):
        def put(work):
            tasks[name] = work
            needs[name] = before

        return put

    def recv(*names):
        for name in names:
            st[name].wait_recv()

    def sent(*names):
        for name in names:
            for copy in st[name] if isinstance(st[name], (list, tuple)) else [st[name]]:
                o.sent(copy)

    @task("cn")
    def _():
        o.loads["cot0"].wait()
        o.loads["cot1"].wait()
        st["c_near0"] = o.share("cot", 0)
        st["c_near1"] = o.share("cot", 1)

    def per_micro(m):
        n = str(m)
        other = str(1 - m)

        @task("nf" + n)
        def _():
            o.norm_first(m)
            st["n_near" + n] = o.share("xn", m)

        @task("nx" + n, "nf" + n)
        def _():
            st["n_far" + n] = o.cross("xn", m)

        @task("np" + n, "nx" + n)
        def _():
            st["n_both" + n] = o.pass_on("xn", m, st["n_far" + n])

        @task("pa" + n, "nf" + n)
        def _():
            if m == 0:
                o.loads["in"].wait()
            recv("n_near" + n)
            o.project(m, False)

        @task("pb" + n, "np" + n, *(["pa0"] if m else []))
        def _():
            recv("n_both" + n)
            o.project(m, True)

        @task("sc" + n, "pa" + n, "pb" + n)
        def _():
            o.scan(m)

        @task("at" + n, "sc" + n, *(["at0"] if m else []))
        def _():
            if m:
                st["save"].wait()
            o.attend(m)
            st["save"] = o.save(m)

        @task("cx" + n, "cn")
        def _():
            st["c_far" + n] = o.cross("cot", m)

        @task("cp" + n, "cx" + n)
        def _():
            st["c_both" + n] = o.pass_on("cot", m, st["c_far" + n])

        @task("br" + n, "at" + n, *(["br0"] if m else []))
        def _():
            if m == 0:
                o.loads["out"].wait()
            st["br" + n] = o.branch(m, st["br0"] if m else [])

        @task("oa" + n, "br" + n)
        def _():
            st["oa" + n] = o.owed("a", st["br" + n], m)

        @task("ns" + n, "oa" + n)
        def _():
            o.norm_second(m, st["br" + n], st["oa" + n])
            st["m_near" + n] = o.share("n2", m)

        @task("mx" + n, "ns" + n)
        def _():
            st["m_far" + n] = o.cross("n2", m)

        @task("mp" + n, "mx" + n)
        def _():
            st["m_both" + n] = o.pass_on("n2", m, st["m_far" + n])

        @task("fa" + n, "ns" + n, "cn", *(["fb0"] if m else ["br1"]))
        def _():
            if m == 0:
                o.loads["up"].wait()
                o.loads["down"].wait()
                sent("br1")
            else:
                sent("fa0")
            sent("oa" + n)
            recv("c_near" + n, "m_near" + n)
            st["fa" + n] = o.feed(m, False)

        @task("fb" + n, "fa" + n, "mp" + n, "cp" + n)
        def _():
            if m:
                sent("fb0")
            recv("c_both" + n, "m_both" + n)
            st["fb" + n] = o.feed(m, True)

        @task("ob" + n, "fb" + n)
        def _():
            st["ob" + n] = o.owed("b", (st["fa" + n][1], st["fb" + n][1]), m)

        @task("oc" + n, "fb" + n)
        def _():
            st["oc" + n] = o.owed("a", (st["fa" + n][0], st["fb" + n][0]), m)

        @task("nb" + n, "ob" + n)
        def _():
            o.norm_second_back(m, (st["fa" + n][1], st["fb" + n][1]), st["ob" + n])
            st["b_near" + n] = o.share("gbr", m)

        @task("bx" + n, "nb" + n)
        def _():
            st["b_far" + n] = o.cross("gbr", m)

        @task("bp" + n, "bx" + n)
        def _():
            st["b_both" + n] = o.pass_on("gbr", m, st["b_far" + n])

        @task("fe" + n, "at1", *(["ab0"] if m else []))
        def _():
            if m == 0:
                st["save"].wait()
            st["fetch"] = o.fetch(m)

        @task("hb" + n, "bp" + n, *(["ab0"] if m else []))
        def _():
            recv("b_near" + n, "b_both" + n)
            o.heads_back(m)

        @task("ab" + n, "hb" + n, "fe" + n, *(["sb0"] if m else []))
        def _():
            st["fetch"].wait()
            o.attend_back(m)

        @task("sb" + n, "ab" + n)
        def _():
            o.scan_back(m)

        @task("pu" + n, "sb" + n, *(["pu0"] if m else ["fb1"]))
        def _():
            sent("ob" + n)
            if m == 0:
                sent("fa1", "fb1")
            st["pu" + n] = o.pull_back(m, st["pu0"] if m else [])

        @task("od" + n, "pu" + n)
        def _():
            st["od" + n] = o.owed("b", st["pu" + n], m)

        @task("mi" + n, "oc" + n)
        def _():
            sent("oc" + n)
            st["end" + n] = o.mix(m, (st["fa" + n][0], st["fb" + n][0]), st["oc" + n])

        @task("nr" + n, "od" + n, "mi" + n)
        def _():
            st["fin" + n] = o.norm_first_back(m, st["pu" + n], st["od" + n])

    per_micro(0)
    per_micro(1)

    @task("mo", "hb0", "hb1", "br1")
    def _():
        o.make_out()

    @task("gs", "nr0", "nr1", "nb0", "nb1")
    def _():
        st["gains"] = o.send_gains()

    @task("pk", "gs", "mo", "sb0", "sb1")
    def _():
        o.pack(st["gains"])

    ready = dict(down=("fb0", "fb1"), up=("fb0", "fb1"), inp=("pu0", "pu1"), misc=("pk",))

    def per_job(job):
        name = job[0] + str(job[1])
        last = ready[job[0]]
        if job[0] != "misc":

            @task("g" + name, *last)
            def _():
                o.tile_give(job)
                st[name] = o.swap_y(job)

            @task("k" + name, *last)
            def _():
                o.tile_keep(job)

            ahead = ("g" + name, "k" + name)
        else:

            @task("g" + name, *last)
            def _():
                st[name] = o.swap_y(job)

            ahead = ("g" + name,)

        @task("y" + name, *ahead)
        def _():
            st[name] = o.sum_y(job, st[name])

        @task("x" + name, "y" + name)
        def _():
            st[name] = o.sum_x(job, st[name])

        @task("z" + name, "x" + name)
        def _():
            st[name] = o.sum_z(job, st[name])

        @task("s" + name, "z" + name)
        def _():
            st[name] = o.spread_y(job, st[name])

        @task("t" + name, "s" + name)
        def _():
            st[name] = o.spread_t(job, st[name])

    for job in JOBS:
        per_job(job)

    def per_tile(job):
        name = "f" + job[0] + str(job[1])

        @task("g" + name, *ready[job[0]])
        def _():
            st[name] = o.first_give(job)

        @task("x" + name, "g" + name)
        def _():
            st[name] = o.first_x(job, st[name])

        @task("z" + name, "x" + name)
        def _():
            st[name] = o.first_z(job, st[name])

        @task("w" + name, "z" + name)
        def _():
            st[name] = o.first_w(job, st[name])

        @task("s" + name, "w" + name)
        def _():
            st[name] = o.first_s(job, st[name])

    for job in FIRST:
        per_tile(job)
    tiles = {
        name: ["f" + n + str(i) for n, i in FIRST if n == name]
        + [n + str(i) for n, i in JOBS if n == name]
        for name in ready
    }
    needs["hb0"] += tuple(k + n for n in tiles["down"] for k in "gk" if k + n in tasks)
    return tasks, needs


def run(o):
    st = {}
    tasks, needs = make_tasks(o, st)
    done = set()
    for name in ORDER:
        assert all(ahead in done for ahead in needs[name]), name
        tasks[name]()
        done.add(name)
    assert len(done) == len(tasks)
    for name, i in JOBS:
        o.finish(st[name + str(i)])
    for name, i in FIRST:
        o.finish(st["f" + name + str(i)])
    for name in ("end0", "end1", "fin0", "fin1"):
        st[name].wait()


class Copies:
    def __init__(self, send, recv):
        self.send, self.recv, self.used, self.open = send, recv, 0, []

    def start(self, source, target, device):
        copy = pltpu.make_async_remote_copy(
            src_ref=source,
            dst_ref=target,
            send_sem=self.send.at[self.used],
            recv_sem=self.recv.at[self.used],
            device_id=device,
            device_id_type=pl.DeviceIdType.MESH,
        )
        self.used += 1
        copy.start()
        self.open.append(copy)
        return copy

    def sent(self, copy):
        copy.wait_send()
        self.open = [other for other in self.open if other is not copy]

    def drain(self):
        for copy in self.open:
            copy.wait_send()
        self.open = []


class Moves:
    def __init__(self, sems):
        self.sems, self.used = sems, 0

    def start(self, source, target):
        copy = pltpu.make_async_copy(source, target, self.sems.at[self.used])
        self.used += 1
        copy.start()
        return copy


def layer(
    nz, tokens, lengths, cotangent, gain_one, gain_two, w_in, ssm, ctx_w, w_out, w_up, w_down
):
    count, rows, width = tokens.shape
    chans = w_out.shape[0]
    heads = chans // HD
    hidden = w_up.shape[1]
    total = 4 * rows
    pair = 2 * rows
    small_rows = heads * CTX + 3 * NS + 8
    unit = 2 * nz * 16
    misc_rows = width + small_rows + (-small_rows % unit)
    sizes = dict(down=(hidden, width), up=(width, hidden), inp=(width, 4 * chans), misc=(misc_rows, chans))
    names = list(sizes)
    share = {n: rows if sizes[n][1] == width else sizes[n][0] // 2 for n in names}
    n_jobs = sum(sizes[n][0] // 2 // share[n] for n in names)
    root = math.sqrt(2.0 / math.pi)
    n_remote = 51 + n_jobs * (1 + 2 * (nz - 1) + nz) + len(FIRST) * 2 * nz
    n_local = 14 + n_jobs * (nz + 1) + len(FIRST) * (nz + 2)

    def kernel(*refs):
        (
            len_ref, tok, cot_hbm, g1, g2, in_hbm, rate, enter, leave, cw, out_hbm, up_hbm, down_hbm,
        ) = refs[:13]
        mixed_hbm, gtok_hbm, pr_hbm = refs[13:16]
        grads = dict(zip(names, refs[16:20]))
        ry = dict(zip(names, refs[20:24]))
        rz = dict(zip(names, refs[24:28]))
        fy, fz = refs[28:30]
        (
            w_i, w_o, w_u, w_d, xn, cot, n2, gbr, hid, gbf, qkv, u0, pr, ho, cx, ckv, dh, gctx,
            give, keep_a, keep_b, sib_a, sib_b, far_a, far_b, mid, acc, tmp, land, misc,
            gain_acc, gain_got, gcw, gss, send_sems, recv_sems, local_sems,
        ) = refs[30:]
        me = lax.axis_index("mp")
        core, chip = me % 2, me // 2
        near, far, both = chip * 2 + 1 - core, (1 - chip) * 2 + core, (1 - chip) * 2 + 1 - core
        dp = lax.axis_index("dp")
        y, z = dp % 2, dp // 2
        to_near, to_far, to_both = {"mp": near}, {"mp": far}, {"mp": both}
        to_y = {"dp": z * 2 + 1 - y}
        zs = [(z + k) % nz for k in range(nz)]
        to_z = [{"dp": zk * 2 + y} for zk in zs]
        paired = nz == 4
        z_pair, z_cross = z + 1 - 2 * (z % 2), (z + 2) % nz
        z_other = (z_pair + 2) % nz
        to_pair, to_cross = {"dp": z_pair * 2 + y}, {"dp": z_cross * 2 + y}
        remote, local = Copies(send_sems, recv_sems), Moves(local_sems)

        loads = {
            "in": local.start(in_hbm, w_i),
            "cot0": local.start(cot_hbm.at[0], cot.at[0, me]),
            "cot1": local.start(cot_hbm.at[1], cot.at[1, me]),
            "out": local.start(out_hbm, w_o),
            "up": local.start(up_hbm, w_u),
            "down": local.start(down_hbm, w_d),
        }
        barrier = pltpu.get_barrier_semaphore()
        for device in [to_near, to_far, to_both, to_y] + to_z[1:]:
            pl.semaphore_signal(
                barrier, inc=1, device_id=device, device_id_type=pl.DeviceIdType.MESH
            )
        pl.semaphore_wait(barrier, 3 + nz)

        def share_piece(buf, m):
            return remote.start(buf.at[m, me], buf.at[m, me], to_near)

        def cross(buf, m):
            return remote.start(buf.at[m, me], buf.at[m, me], to_far)

        def pass_on(buf, m, copy):
            copy.wait_recv()
            return remote.start(buf.at[m, far], buf.at[m, far], to_near)

        def offer(kind, slot, sib, m):
            return remote.start(give.at[kind, slot], sib.at[m, slot], to_near)

        def by_rows(work):
            step = 64

            def body(i, carry):
                work(pl.ds(pl.multiple_of(i * step, step), step))
                return carry

            lax.fori_loop(0, rows // step, body, 0)

        def owed(offers, keep, sib, far_buf, m):
            offers[1].wait_recv()

            def work(at):
                keep[m, 1, at, :] = (
                    keep[m, 1, at, :].astype(F32) + sib[m, 1, at, :].astype(F32)
                ).astype(BF16)

            by_rows(work)
            return remote.start(keep.at[m, 1], far_buf.at[m], to_far)

        def summed(offers, copy, keep, sib, far_buf, m):
            offers[0].wait_recv()
            copy.wait_recv()
            return lambda at: (
                keep[m, 0, at, :].astype(F32)
                + sib[m, 0, at, :].astype(F32)
                + far_buf[m, at, :].astype(F32)
            )

        def inverse_root(value):
            return lax.rsqrt(jnp.mean(value * value, axis=-1, keepdims=True) + EPS)

        def norm_first(m):
            def work(at):
                x = tok[m, at, :].astype(F32)
                xn[m, me, at, :] = (x * inverse_root(x) * g1[...]).astype(BF16)

            by_rows(work)

        def norm_second(m, branch):
            def work(at):
                value = tok[m, at, :].astype(F32) + branch(at)
                mid[m, at, :] = value
                n2[m, me, at, :] = (value * inverse_root(value) * g2[...]).astype(BF16)

            by_rows(work)

        def pulled(value, grad, gain, line):
            scale = inverse_root(value)
            unit_row = value * scale
            gain_acc[line : line + 1, :] += jnp.sum(grad * unit_row, axis=0, keepdims=True)
            inner = grad * gain[...]
            return scale * (inner - unit_row * jnp.mean(inner * unit_row, axis=-1, keepdims=True))

        def norm_second_back(m, grad):
            def work(at):
                value = cot[m, me, at, :].astype(F32) + pulled(mid[m, at, :], grad(at), g2, 1)
                gbr[m, me, at, :] = value.astype(BF16)

            by_rows(work)

        def norm_first_back(m, grad):
            def work(at):
                x = tok[m, at, :].astype(F32)
                mid[m, at, :] = gbr[m, me, at, :].astype(F32) + pulled(x, grad(at), g1, 0)

            by_rows(work)
            return local.start(mid.at[m], gtok_hbm.at[m])

        def mix(m, branch):
            def work(at):
                keep_a[m, 0, at, :] = (mid[m, at, :] + branch(at)).astype(BF16)

            by_rows(work)
            return local.start(keep_a.at[m, 0], mixed_hbm.at[m])

        def project(m, side):
            def body(i, carry):
                t = side * 2 + i
                at = pl.ds(pl.multiple_of(t * rows, rows), rows)
                x = xn[m, t]
                qkv[m, at, :] = dot(x, w_i[:, : 3 * chans]).astype(BF16)

                @pl.when(t < 2)
                def _():
                    u0[m, at, :] = dot(x, w_i[:, 3 * chans :])

                return carry

            lax.fori_loop(0, 2, body, 0)

        def scan(m):
            context = state_forward(u0.at[m], rate, enter, leave).astype(BF16)
            cx[m] = context
            for h in range(heads):
                ckv[m, h] = dot(context[:, h * HD : (h + 1) * HD], cw[h]).astype(BF16)

        def attend(m):
            valid, linked = layout_scalars(len_ref, m)
            for h in range(heads):
                lanes = slice(h * HD, (h + 1) * HD)
                klanes = slice(chans + h * HD, chans + (h + 1) * HD)
                vlanes = slice(2 * chans + h * HD, 2 * chans + (h + 1) * HD)
                for b in range(2):
                    for half in range(2):
                        row0 = half * rows
                        keys = row0 + rows
                        spot = b * BLK + row0
                        q = qkv[m, spot : spot + rows, lanes]
                        k = qkv[m, b * BLK : b * BLK + keys, klanes]
                        v = qkv[m, b * BLK : b * BLK + keys, vlanes]
                        s = dot_nt(q, k) * SCALE2
                        row = lax.broadcasted_iota(jnp.int32, (rows, keys), 0) + row0
                        col = lax.broadcasted_iota(jnp.int32, (rows, keys), 1)
                        allowed = (col < jnp.minimum(row, valid[b])) | (col == row)
                        s = jnp.where(allowed, s, NEG)
                        peak = jnp.max(s, axis=-1, keepdims=True)
                        if b:
                            sc = dot_nt(q, ckv[m, h, :, :HD]) * SCALE2
                            sc = jnp.where(linked, sc, NEG)
                            peak = jnp.maximum(peak, jnp.max(sc, axis=-1, keepdims=True))
                            ec = jnp.exp2(sc - peak)
                        e = jnp.exp2(s - peak)
                        norm = jnp.sum(e, axis=-1, keepdims=True)
                        if b:
                            norm = norm + jnp.sum(ec, axis=-1, keepdims=True)
                        inverse = 1.0 / norm
                        p = (e * inverse).astype(BF16)
                        pr[h, b, row0 : row0 + rows, CTX : CTX + keys] = p
                        o = dot(p, v)
                        if b:
                            pc = (ec * inverse).astype(BF16)
                            pr[h, b, row0 : row0 + rows, :CTX] = pc
                            o = o + dot(pc, ckv[m, h, :, HD:])
                        ho[m, 2 * b + half, :, lanes] = o.astype(BF16)

        def spread(product, keep, kind, sib, m, before):
            for copy in before:
                remote.sent(copy)
            give[kind, 1] = product(both).astype(BF16)
            second = offer(kind, 1, sib, m)
            give[kind, 0] = product(near).astype(BF16)
            first = offer(kind, 0, sib, m)
            keep[m, 1] = product(far).astype(BF16)
            keep[m, 0] = product(me).astype(BF16)
            return [first, second]

        def feed(m, side, other):
            slot = 1 if other else 0

            def body(i, carry):
                t = side * 2 + jnp.where(i == 0, 1 - core, core)
                for start in range(0, hidden, 256):
                    cut = slice(start, start + 256)
                    before = dot(n2[m, t], w_u[:, cut])
                    square = before * before
                    th = jnp.tanh(root * (before * (1.0 + 0.044715 * square)))
                    half = 0.5 + 0.5 * th
                    hid[m, t, :, cut] = (before * half).astype(BF16)
                    slope = half + (0.5 * root) * before * (1.0 - th * th) * (
                        1.0 + 0.134145 * square
                    )
                    gbf[m, t, :, cut] = (dot_nt(cot[m, t], w_d[cut, :]) * slope).astype(BF16)
                branch = dot(hid[m, t], w_d[...]).astype(BF16)
                gn = dot_nt(gbf[m, t], w_u[...]).astype(BF16)

                @pl.when(i == 0)
                def _():
                    give[0, slot] = branch
                    give[1, slot] = gn

                @pl.when(i == 1)
                def _():
                    keep_a[m, slot] = branch
                    keep_b[m, slot] = gn

                return carry

            lax.fori_loop(0, 2, body, 0)
            return offer(0, slot, sib_a, m), offer(1, slot, sib_b, m)

        def heads_back(m):
            def body(t, carry):
                at = pl.ds(pl.multiple_of(t * rows, rows), rows)
                dh[at, :] = dot_nt(gbr[m, t], w_o[...]).astype(BF16)
                return carry

            lax.fori_loop(0, 4, body, 0)

        def attend_back(m):
            for h in range(heads):
                lanes = slice(h * HD, (h + 1) * HD)
                klanes = slice(chans + h * HD, chans + (h + 1) * HD)
                vlanes = slice(2 * chans + h * HD, 2 * chans + (h + 1) * HD)
                for b in range(2):
                    grad_k, grad_v = [None, None], [None, None]
                    grad_c = grad_cv = None
                    for half in (1, 0):
                        row0 = half * rows
                        keys = row0 + rows
                        spot = slice(b * BLK + row0, b * BLK + row0 + rows)
                        go = dh[spot, lanes]
                        qh = qkv[m, spot, lanes]
                        kh = qkv[m, b * BLK : b * BLK + keys, klanes]
                        vh = qkv[m, b * BLK : b * BLK + keys, vlanes]
                        p = pr[h, b, row0 : row0 + rows, CTX : CTX + keys]
                        pf = p.astype(F32)
                        dprob = dot_nt(go, vh)
                        delta = jnp.sum(dprob * pf, axis=-1, keepdims=True)
                        if b:
                            pc = pr[h, b, row0 : row0 + rows, :CTX]
                            pcf = pc.astype(F32)
                            dpc = dot_nt(go, ckv[m, h, :, HD:])
                            delta = delta + jnp.sum(dpc * pcf, axis=-1, keepdims=True)
                            dsc = (pcf * (dpc - delta)).astype(BF16)
                        ds = (pf * (dprob - delta)).astype(BF16)
                        dq = dot(ds, kh)
                        if b:
                            dq = dq + dot(dsc, ckv[m, h, :, :HD])
                            one = dot_tn(dsc, qh)
                            two = dot_tn(pc, go)
                            grad_c = one if grad_c is None else grad_c + one
                            grad_cv = two if grad_cv is None else grad_cv + two
                        hid[m, 2 * b + half, :, lanes] = (dq * SCALE).astype(BF16)
                        dk = dot_tn(ds, qh)
                        dv = dot_tn(p, go)
                        if half:
                            grad_k = [dk[:rows], dk[rows:]]
                            grad_v = [dv[:rows], dv[rows:]]
                        else:
                            grad_k[0] = grad_k[0] + dk
                            grad_v[0] = grad_v[0] + dv
                    for part in range(2):
                        t = 2 * b + part
                        hid[m, t, :, klanes] = (grad_k[part] * SCALE).astype(BF16)
                        hid[m, t, :, vlanes] = grad_v[part].astype(BF16)
                    if b:
                        low_c = (grad_c * SCALE).astype(BF16)
                        low_cv = grad_cv.astype(BF16)
                        ch = cx[m, :, lanes]
                        gcw[m, h, :, :HD] = dot_tn(ch, low_c)
                        gcw[m, h, :, HD:] = dot_tn(ch, low_cv)
                        gctx[:, lanes] = dot_nt(low_c, cw[h, :, :HD]) + dot_nt(
                            low_cv, cw[h, :, HD:]
                        )

        def scan_back(m):
            state_backward(gctx[...], u0.at[m], u0.at[m], rate, enter, leave, gss.at[m])
            for t in range(2):
                hid[m, t, :, 3 * chans :] = u0[m, t * rows : (t + 1) * rows, :].astype(BF16)
                hid[m, 2 + t, :, 3 * chans :] = jnp.zeros((rows, chans), BF16)

        def gather_tile(left, right, tile):
            lanes = pl.ds(pl.multiple_of(tile * rows, rows), rows)
            acc[...] = jnp.zeros_like(acc)

            def body(i, carry):
                m, t = i // 4, i % 4
                acc[...] += dot_tn(left[m, t, :, lanes], right[m, t])
                return carry

            lax.fori_loop(0, 4 * count, body, 0)

        def part(ref, start, size):
            return ref.at[pl.ds(pl.multiple_of(start, 16), size), :]

        def job_rows(job, side):
            name, i = job
            span = sizes[name][0] // 2
            if sizes[name][1] != width:
                return side * span, span
            return side * span + i * rows, rows

        stages = dict(down=w_d, up=w_u, inp=w_i, misc=misc)
        sides = dict(down=(hid, cot), up=(n2, gbf), inp=(xn, hid))

        def tile(job, side):
            start, size = job_rows(job, side)
            gather_tile(*sides[job[0]], start // size)
            stages[job[0]][pl.ds(pl.multiple_of(start, size), size), :] = acc[...].astype(BF16)

        def tile_give(job):
            tile(job, 1 - y)

        def tile_keep(job):
            tile(job, y)

        def landing(job, size):
            if sizes[job[0]][1] != width:
                return tmp.at[pl.ds(0, size), :]
            return land.at[pl.ds(0, size), :]

        def swap_y(job):
            name, i = job
            start, size = job_rows(job, 1 - y)
            return remote.start(part(stages[name], start, size), ry[name].at[i], to_y)

        def sum_y(job, copy):
            name, i = job
            stage = stages[name]
            start, size = job_rows(job, y)
            piece = size // nz
            copy.wait_recv()
            got = landing(job, size)
            local.start(ry[name].at[i], got).wait()
            at = pl.ds(pl.multiple_of(start, 16), size)
            stage[at, :] = (stage[at, :].astype(F32) + got[...].astype(F32)).astype(BF16)
            if paired:
                return [
                    remote.start(part(stage, start + t * piece, piece), rz[name].at[i, k], to_pair)
                    for k, t in enumerate((z_pair, z_other))
                ]
            return [
                remote.start(
                    part(stage, start + zs[k] * piece, piece), rz[name].at[i, k - 1], to_z[k]
                )
                for k in range(1, nz)
            ]

        def add_landed(job, at, slots):
            name, i = job
            stage = stages[name]
            piece = job_rows(job, y)[1] // nz
            got = landing(job, len(slots) * piece)
            moves = [
                local.start(rz[name].at[i, slot], got.at[pl.ds(k * piece, piece), :])
                for k, slot in enumerate(slots)
            ]
            for move in moves:
                move.wait()
            value = stage[at, :].astype(F32)
            for k in range(len(slots)):
                value = value + got[k * piece : (k + 1) * piece, :].astype(F32)
            stage[at, :] = value.astype(BF16)

        def sum_x(job, copies):
            if not paired:
                return copies
            name, i = job
            start, size = job_rows(job, y)
            piece = size // nz
            spot = start + z_cross * piece
            copies[1].wait_recv()
            add_landed(job, pl.ds(pl.multiple_of(spot, 16), piece), (1,))
            mine = part(stages[name], spot, piece)
            return [copies[0], remote.start(mine, rz[name].at[i, 2], to_cross)]

        def sum_z(job, copies):
            name, i = job
            start, size = job_rows(job, y)
            piece = size // nz
            for copy in copies:
                copy.wait_recv()
            spot = start + z * piece
            slots = (0, 2) if paired else tuple(range(nz - 1))
            add_landed(job, pl.ds(pl.multiple_of(spot, 16), piece), slots)
            mine = part(stages[name], spot, piece)
            place = part(grads[name], spot, piece)
            outs = [remote.start(mine, place, d) for d in ([to_pair, to_cross] if paired else to_z[1:])]
            last = [remote.start(mine, place, to_y)]
            return outs, last, local.start(mine, place)

        def spread_y(job, state):
            name, i = job
            start, size = job_rows(job, y)
            piece = size // nz
            outs, last, move = state
            if paired:
                whose = (z_pair, z_cross)
            else:
                whose = [(z + nz - k) % nz for k in range(1, nz)]
            on = None
            for copy, owner in zip(outs, whose):
                copy.wait_recv()
                place = part(grads[name], start + owner * piece, piece)
                last.append(remote.start(place, place, to_y))
                if paired and owner is z_cross:
                    on = remote.start(place, place, to_pair)
            return last, move, on

        def spread_t(job, state):
            name, i = job
            start, size = job_rows(job, y)
            last, move, on = state
            if paired:
                on.wait_recv()
                piece = size // nz
                place = part(grads[name], start + z_other * piece, piece)
                last.append(remote.start(place, place, to_y))
            return last, move

        def add_refs(stage, at, refs):
            piece = rows // nz
            got = land.at[pl.ds(0, len(refs) * piece), :]
            moves = [
                local.start(ref, got.at[pl.ds(k * piece, piece), :]) for k, ref in enumerate(refs)
            ]
            for move in moves:
                move.wait()
            value = stage[at, :].astype(F32)
            for k in range(len(refs)):
                value = value + got[k * piece : (k + 1) * piece, :].astype(F32)
            stage[at, :] = value.astype(BF16)

        def first_give(job):
            name, i = job
            gather_tile(*sides[name], i)
            stage = stages[name]
            stage[i * rows : (i + 1) * rows, :] = acc[...].astype(BF16)
            piece = rows // nz
            if paired:
                ends = [(z_pair, to_pair), (z_other, to_pair)]
            else:
                ends = list(zip(zs, to_z))[1:]
            return [
                remote.start(
                    part(stage, i * rows + t * piece, piece), fz.at[FIRST.index(job), k], device
                )
                for k, (t, device) in enumerate(ends)
            ]

        def first_x(job, copies):
            if not paired:
                return copies
            name, i = job
            piece = rows // nz
            spot = i * rows + z_cross * piece
            copies[1].wait_recv()
            at = pl.ds(pl.multiple_of(spot, 16), piece)
            add_refs(stages[name], at, [fz.at[FIRST.index(job), 1]])
            mine = part(stages[name], spot, piece)
            return [copies[0], remote.start(mine, fz.at[FIRST.index(job), 2], to_cross)]

        def first_z(job, copies):
            name, i = job
            piece = rows // nz
            for copy in copies:
                copy.wait_recv()
            spot = i * rows + z * piece
            at = pl.ds(pl.multiple_of(spot, 16), piece)
            slots = (0, 2) if paired else range(nz - 1)
            add_refs(stages[name], at, [fz.at[FIRST.index(job), k] for k in slots])
            return remote.start(part(stages[name], spot, piece), fy.at[FIRST.index(job)], to_y)

        def first_w(job, copy):
            name, i = job
            piece = rows // nz
            copy.wait_recv()
            remote.sent(copy)
            spot = i * rows + z * piece
            at = pl.ds(pl.multiple_of(spot, 16), piece)
            add_refs(stages[name], at, [fy.at[FIRST.index(job)]])
            mine = part(stages[name], spot, piece)
            place = part(grads[name], spot, piece)
            outs = [remote.start(mine, place, d) for d in ([to_pair, to_cross] if paired else to_z[1:])]
            return outs, local.start(mine, place)

        def first_s(job, state):
            name, i = job
            outs, move = state
            if not paired:
                return outs, move
            piece = rows // nz
            outs[1].wait_recv()
            place = part(grads[name], i * rows + z_cross * piece, piece)
            return [outs[0], remote.start(place, place, to_pair)], move

        def finish(state):
            last, move = state
            for copy in last:
                copy.wait_recv()
            move.wait()

        def make_out():
            gather_tile(ho, gbr, 0)
            for j in range(width // chans):
                misc[j * chans : (j + 1) * chans, :] = acc[:, j * chans : (j + 1) * chans].astype(
                    BF16
                )

        def send_gains():
            return [
                remote.start(gain_acc, gain_got.at[k], device)
                for k, device in enumerate((to_near, to_far, to_both))
            ]

        def pack(copies):
            base = width
            for h in range(heads):
                misc[base + h * CTX : base + (h + 1) * CTX, :] = (gcw[0, h] + gcw[1, h]).astype(BF16)
            base += heads * CTX
            for k in range(3):
                misc[base + k * NS : base + (k + 1) * NS, :] = (gss[0, k] + gss[1, k]).astype(BF16)
            base += 3 * NS
            for copy in copies:
                copy.wait_recv()
            value = gain_acc[...] + gain_got[0] + gain_got[1] + gain_got[2]
            line = jnp.concatenate(
                [value[r : r + 1, j * chans : (j + 1) * chans] for r in range(2) for j in range(4)],
                axis=0,
            )
            misc[base:, :] = jnp.concatenate(
                [line, jnp.zeros((misc_rows - base - 8, chans), F32)], axis=0
            ).astype(BF16)

        def branch(m, before):
            return spread(lambda t: dot(ho[m, t], w_o[...]), keep_a, 0, sib_a, m, before)

        def pull_back(m, before):
            return spread(lambda t: dot_nt(hid[m, t], w_i[...]), keep_b, 1, sib_b, m, before)

        bufs = dict(xn=xn, cot=cot, n2=n2, gbr=gbr)
        sets = dict(a=(keep_a, sib_a, far_a), b=(keep_b, sib_b, far_b))
        o = types.SimpleNamespace(
            count=count,
            norm_first=norm_first,
            share=lambda buf, m: share_piece(bufs[buf], m),
            cross=lambda buf, m: cross(bufs[buf], m),
            pass_on=lambda buf, m, copy: pass_on(bufs[buf], m, copy),
            sent=remote.sent,
            loads=loads,
            project=lambda m, other: project(m, 1 - chip if other else chip),
            scan=scan,
            attend=attend,
            save=lambda m: local.start(pr, pr_hbm.at[m]),
            fetch=lambda m: local.start(pr_hbm.at[m], pr),
            branch=branch,
            owed=lambda kind, offers, m: owed(offers, *sets[kind], m),
            norm_second=lambda m, of, cp: norm_second(m, summed(of, cp, *sets["a"], m)),
            norm_second_back=lambda m, of, cp: norm_second_back(m, summed(of, cp, *sets["b"], m)),
            norm_first_back=lambda m, of, cp: norm_first_back(m, summed(of, cp, *sets["b"], m)),
            mix=lambda m, of, cp: mix(m, summed(of, cp, *sets["a"], m)),
            feed=lambda m, other: feed(m, 1 - chip if other else chip, other),
            heads_back=heads_back,
            attend_back=attend_back,
            scan_back=scan_back,
            pull_back=pull_back,
            tile_give=tile_give,
            tile_keep=tile_keep,
            swap_y=swap_y,
            sum_y=sum_y,
            sum_x=sum_x,
            sum_z=sum_z,
            spread_y=spread_y,
            spread_t=spread_t,
            first_give=first_give,
            first_x=first_x,
            first_z=first_z,
            first_w=first_w,
            first_s=first_s,
            finish=finish,
            make_out=make_out,
            send_gains=send_gains,
            pack=pack,
        )
        gain_acc[...] = jnp.zeros_like(gain_acc)
        run(o)
        remote.drain()
        assert remote.used <= n_remote and local.used <= n_local, (remote.used, local.used)

    pieces = (count, 4, rows)
    vm = pltpu.VMEM
    any_out = [
        shape((count, rows, width), BF16),
        shape((count, rows, width), F32),
        shape((count, heads, 2, BLK, BLK + CTX), BF16),
    ]
    any_out += [shape(sizes[n], BF16) for n in names]
    any_out += [
        shape((sizes[n][0] // 2 // share[n], share[n], sizes[n][1]), BF16) for n in names
    ]
    any_out += [
        shape((sizes[n][0] // 2 // share[n], nz - 1, share[n] // nz, sizes[n][1]), BF16)
        for n in names
    ]
    any_out += [
        shape((len(FIRST), rows // nz, width), BF16),
        shape((len(FIRST), nz - 1, rows // nz, width), BF16),
    ]
    results = pl.pallas_call(
        kernel,
        in_specs=[SMEM, VMEM, ANY, VMEM, VMEM, ANY, VMEM, VMEM, VMEM, VMEM, ANY, ANY, ANY],
        out_specs=[ANY] * len(any_out),
        out_shape=any_out,
        scratch_shapes=[
            vm(w_in.shape, BF16),
            vm(w_out.shape, BF16),
            vm(w_up.shape, BF16),
            vm(w_down.shape, BF16),
            vm(pieces + (width,), BF16),
            vm(pieces + (width,), BF16),
            vm(pieces + (width,), BF16),
            vm(pieces + (width,), BF16),
            vm(pieces + (hidden,), BF16),
            vm(pieces + (hidden,), BF16),
            vm((count, total, 3 * chans), BF16),
            vm((count, BLK, chans), F32),
            vm((heads, 2, BLK, BLK + CTX), BF16),
            vm(pieces + (chans,), BF16),
            vm((count, CTX, chans), BF16),
            vm((count, heads, CTX, 2 * HD), BF16),
            vm((total, chans), BF16),
            vm((CTX, chans), F32),
            vm((2, 2, rows, width), BF16),
            vm((count, 2, rows, width), BF16),
            vm((count, 2, rows, width), BF16),
            vm((count, 2, rows, width), BF16),
            vm((count, 2, rows, width), BF16),
            vm((count, rows, width), BF16),
            vm((count, rows, width), BF16),
            vm((count, rows, width), F32),
            vm((rows, width), F32),
            vm((misc_rows // 2, chans), BF16),
            vm((rows, width), BF16),
            vm((misc_rows, chans), BF16),
            vm((8, width), F32),
            vm((3, 8, width), F32),
            vm((count, heads, CTX, 2 * HD), F32),
            vm((count, 3, NS, chans), F32),
            pltpu.SemaphoreType.DMA((n_remote,)),
            pltpu.SemaphoreType.DMA((n_remote,)),
            pltpu.SemaphoreType.DMA((n_local,)),
        ],
        compiler_params=pltpu.CompilerParams(
            collective_id=0, has_side_effects=True, vmem_limit_bytes=63 << 20
        ),
        cost_estimate=cost(45e9, 60e6),
    )(lengths, tokens, cotangent, gain_one, gain_two, w_in, *ssm, ctx_w, w_out, w_up, w_down)
    return results[0], results[1], dict(zip(names, results[3:7]))


def publish(mixed, grad_tokens, grads, in_shape, ctx_shape, out_shape):
    count, rows, width = mixed.shape
    heads = ctx_shape[0]
    chans = in_shape[2]
    steps = 8
    parts = width // chans
    misc_rows = grads["misc"].shape[0]

    def kernel(m_ref, t_ref, d_ref, u_ref, i_ref, misc_ref, *outs):
        mo, to, do, uo, io, oo, co, ra, en, le, ga, gb = outs
        mo[...] = m_ref[...]
        to[...] = t_ref[...]
        do[...] = d_ref[...].astype(F32)
        uo[...] = u_ref[...].astype(F32)
        for k in range(in_shape[1]):
            io[:, k, :] = i_ref[:, k * chans : (k + 1) * chans].astype(F32)

        @pl.when(pl.program_id(0) == 0)
        def _():
            for j in range(parts):
                oo[:, j * chans : (j + 1) * chans] = misc_ref[
                    j * chans : (j + 1) * chans, :
                ].astype(F32)
            at = width
            for h in range(heads):
                co[h] = misc_ref[at + h * CTX : at + (h + 1) * CTX, :].astype(F32)
            at += heads * CTX
            for k, ref in enumerate((ra, en, le)):
                ref[...] = misc_ref[at + k * NS : at + (k + 1) * NS, :].astype(F32)
            at += 3 * NS
            tail = misc_ref[at : at + 16, :].astype(F32)
            for r, ref in enumerate((ga, gb)):
                for j in range(parts):
                    ref[:, j * chans : (j + 1) * chans] = tail[r * parts + j : r * parts + j + 1, :]

    def blocks(dims):
        return pl.BlockSpec((dims[0] // steps,) + dims[1:], lambda i: (i,) + (0,) * (len(dims) - 1))

    def whole(dims):
        return pl.BlockSpec(dims, lambda i: (0,) * len(dims))

    token_block = pl.BlockSpec((count, rows // steps, width), lambda i: (0, i, 0))
    small = [out_shape, ctx_shape] + [(NS, chans)] * 3 + [(1, width)] * 2
    big = [grads["down"].shape, grads["up"].shape]
    return pl.pallas_call(
        kernel,
        grid=(steps,),
        in_specs=[token_block] * 2
        + [blocks(d) for d in big]
        + [blocks(grads["inp"].shape), whole((misc_rows, chans))],
        out_specs=[token_block] * 2
        + [blocks(d) for d in big]
        + [blocks(in_shape)]
        + [whole(d) for d in small],
        out_shape=[shape(mixed.shape, BF16), shape(mixed.shape, F32)]
        + [shape(d, F32) for d in big + [in_shape] + small],
        compiler_params=params(62),
        cost_estimate=cost(0, 28e6),
    )(mixed, grad_tokens, grads["down"], grads["up"], grads["inp"], grads["misc"])


def body(
    tokens,
    lengths,
    cotangent,
    attn_gain,
    in_weights,
    ssm_rate,
    ssm_input,
    ssm_output,
    ctx_weights,
    out_weights,
    mlp_gain,
    up_weights,
    down_weights,
):
    width = tokens.shape[2]
    chans = out_weights.shape[0]
    mixed, grad_tokens, grads = layer(
        lax.axis_size("dp") // 2,
        tokens,
        lengths[0],
        cotangent,
        attn_gain.reshape(1, width),
        mlp_gain.reshape(1, width),
        in_weights.reshape(width, 4 * chans),
        (ssm_rate, ssm_input, ssm_output),
        ctx_weights,
        out_weights,
        up_weights,
        down_weights,
    )
    mixed, grad_tokens, down, up, inp, out, ctx, rate, enter, leave, one, two = publish(
        mixed, grad_tokens, grads, in_weights.shape, ctx_weights.shape, out_weights.shape
    )
    return (
        mixed,
        grad_tokens,
        one.reshape(width),
        inp,
        rate,
        enter,
        leave,
        ctx,
        out,
        two.reshape(width),
        up,
        down,
    )


def solution(mesh):
    rows = P(None, ("dp", "mp"), None)
    return jax.shard_map(
        body,
        mesh=mesh,
        in_specs=(
            rows,
            P("dp", None, None),
            rows,
            P(),
            P(None, None, "mp"),
            P(None, "mp"),
            P(None, "mp"),
            P(None, "mp"),
            P("mp", None, None),
            P("mp", None),
            P(),
            P(None, "mp"),
            P("mp", None),
        ),
        out_specs=(
            rows,
            rows,
            P(),
            P(None, None, "mp"),
            P(None, "mp"),
            P(None, "mp"),
            P(None, "mp"),
            P("mp", None, None),
            P("mp", None),
            P(),
            P(None, "mp"),
            P("mp", None),
        ),
        check_vma=False,
    )
```

```python
import functools
import math
import types

import jax
import jax.numpy as jnp
from jax import lax
from jax.experimental import pallas as pl
from jax.experimental.pallas import tpu as pltpu
from jax.sharding import PartitionSpec as P

HD = 128
BLK = 512
CTX = 128
HEAD = BLK - CTX
NS = 16
EPS = 1e-05
SCALE = 1.0 / math.sqrt(HD)
SCALE2 = SCALE * math.log2(math.e)
NEG = -1e30
F32 = jnp.float32
BF16 = jnp.bfloat16

VMEM = pl.BlockSpec(memory_space=pltpu.VMEM)
SMEM = pl.BlockSpec(memory_space=pltpu.SMEM)
ANY = pl.BlockSpec(memory_space=pl.ANY)


def params(mib):
    return pltpu.CompilerParams(vmem_limit_bytes=mib << 20)


def cost(flops, nbytes):
    return pl.CostEstimate(flops=int(flops), bytes_accessed=int(nbytes), transcendentals=0)


def dot(a, b):
    return lax.dot_general(a, b, (((1,), (0,)), ((), ())), preferred_element_type=F32)


def dot_nt(a, b):
    return lax.dot_general(a, b, (((1,), (1,)), ((), ())), preferred_element_type=F32)


def dot_tn(a, b):
    return lax.dot_general(a, b, (((0,), (0,)), ((), ())), preferred_element_type=F32)


def shape(dims, kind):
    return jax.ShapeDtypeStruct(dims, kind)


def triangle(upper):
    row = lax.broadcasted_iota(jnp.int32, (CTX, 2 * CTX), 0)
    col = lax.broadcasted_iota(jnp.int32, (CTX, 2 * CTX), 1) % CTX
    keep = (row <= col) if upper else (row >= col)
    return jnp.where(keep, 1.0, 0.0).astype(BF16)


def running(tri, values):
    high = values.astype(BF16)
    rest = (values - high.astype(F32)).astype(BF16)
    return dot(tri, jnp.concatenate([high, rest], axis=0))


def head_sums(u_ref, rate_ref, moment):
    width = rate_ref.shape[1]
    place = lax.broadcasted_iota(jnp.int32, (8, width), 0).astype(F32)
    sums, moments = [], []
    group = 4 if moment else 8
    for base in range(0, NS, group):
        rates = [rate_ref[n : n + 1, :] for n in range(base, base + group)]
        steps = [jnp.broadcast_to(jnp.exp(-8.0 * r), (8, width)) for r in rates]

        def body(chunk, carry):
            start = pl.multiple_of(chunk * 8, 8)
            rows = u_ref[pl.ds(start, 8), :]
            first = [acc * step + rows for acc, step in zip(carry[0], steps)]
            if not moment:
                return (first, carry[1])
            scaled = rows * (place + (chunk * 8 - HEAD).astype(F32))
            second = [acc * step + scaled for acc, step in zip(carry[1], steps)]
            return (first, second)

        zero = [jnp.zeros((8, width), F32) for _ in range(group)]
        first, second = lax.fori_loop(
            0, HEAD // 8, body, (zero, list(zero) if moment else []), unroll=4
        )
        for k, rate in enumerate(rates):
            last = jnp.exp(rate * (place - 8.0))
            sums.append(jnp.sum(first[k] * last, axis=0, keepdims=True))
            if moment:
                moments.append(jnp.sum(second[k] * last, axis=0, keepdims=True))
    return sums, moments


def state_forward(u_ref, rate_ref, in_ref, out_ref):
    width = rate_ref.shape[1]
    sums, _ = head_sums(u_ref, rate_ref, False)
    tail = u_ref[pl.ds(HEAD, CTX), :]
    time = lax.broadcasted_iota(jnp.int32, (CTX, width), 0).astype(F32)
    tri = triangle(False)
    total = jnp.zeros((CTX, width), F32)
    for n in range(NS):
        rate = rate_ref[n : n + 1, :]
        gain = in_ref[n : n + 1, :] * jnp.sqrt(1.0 - jnp.exp(-2.0 * rate))
        weight = gain * out_ref[n : n + 1, :]
        prefix = running(tri, jnp.exp(rate * time) * tail)
        total = total + weight * (jnp.exp(-rate * time) * (sums[n] + prefix))
    return total


def state_backward(grad, u_ref, du_ref, rate_ref, in_ref, out_ref, gs_ref):
    width = rate_ref.shape[1]
    sums, moments = head_sums(u_ref, rate_ref, True)
    tail = u_ref[pl.ds(HEAD, CTX), :]
    time = lax.broadcasted_iota(jnp.int32, (CTX, width), 0).astype(F32)
    place = lax.broadcasted_iota(jnp.int32, (8, width), 0).astype(F32)
    lower, upper = triangle(False), triangle(True)
    total = jnp.zeros((CTX, width), F32)
    starts = []
    for n in range(NS):
        rate = rate_ref[n : n + 1, :]
        root = jnp.sqrt(1.0 - jnp.exp(-2.0 * rate))
        enter = in_ref[n : n + 1, :]
        leave = out_ref[n : n + 1, :]
        gain = enter * root
        rising = jnp.exp(rate * time)
        driven = rising * tail
        states = sums[n] + running(lower, driven)
        seen = jnp.exp(-rate * time) * grad
        later = running(upper, seen)
        product = seen * states
        energy = jnp.sum(product, axis=0, keepdims=True)
        slope = jnp.sum(time * (product - driven * later), axis=0, keepdims=True)
        slope = slope - later[0:1] * moments[n]
        total = total + (gain * leave) * (rising * later)
        starts.append((gain * leave) * later[0:1])
        gs_ref[0, n : n + 1, :] = leave * (
            energy * enter * jnp.exp(-2.0 * rate) / root - gain * slope
        )
        gs_ref[1, n : n + 1, :] = leave * energy * root
        gs_ref[2, n : n + 1, :] = gain * energy
    du_ref[pl.ds(HEAD, CTX), :] = total
    group = 8
    for base in range(0, NS, group):
        rates = [rate_ref[n : n + 1, :] for n in range(base, base + group)]
        steps = [jnp.broadcast_to(jnp.exp(-8.0 * r), (8, width)) for r in rates]
        begin = [
            starts[base + k] * jnp.exp(rate * (place - 8.0)) for k, rate in enumerate(rates)
        ]

        def body(index, carry):
            start = pl.multiple_of(HEAD - 8 - index * 8, 8)
            value = functools.reduce(lambda a, b: a + b, carry)
            if base:
                value = value + du_ref[pl.ds(start, 8), :]
            du_ref[pl.ds(start, 8), :] = value
            return [c * step for c, step in zip(carry, steps)]

        lax.fori_loop(0, HEAD // 8, body, begin, unroll=4)


def layout_scalars(len_ref, micro):
    first, second = len_ref[micro, 0], len_ref[micro, 1]
    first_blocks = (first + (BLK - 1)) // BLK
    second_blocks = (second + (BLK - 1)) // BLK
    docs, valid = [], []
    for b in range(2):
        doc = jnp.where(b < first_blocks, 0, jnp.where(b < first_blocks + second_blocks, 1, 2))
        start = jnp.where(doc == 0, 0, first_blocks)
        extent = jnp.where(doc == 0, first, jnp.where(doc == 1, second, 0))
        docs.append(doc)
        valid.append(extent - (b - start) * BLK)
    return valid, docs[0] == docs[1]


ALL = (("down", 0), ("down", 1), ("up", 0), ("up", 1), ("inp", 0), ("inp", 1), ("misc", 0))
ALONG_Z = (("down", 0),)
JOBS = tuple(job for job in ALL if job not in ALONG_Z)
FIRST = tuple((name, i + 2 * half) for name, i in ALONG_Z for half in range(2))


ORDER = (
    "nf0", "nx0", "pa0", "nf1", "nx1", "np0", "cn", "pb0", "cx0", "pa1", "sc0", "at0", "np1",
    "br0", "oa0", "pb1", "sc1", "at1", "br1", "oa1", "ns0", "mx0", "ns1", "cp0", "mx1", "fa0",
    "cx1", "mp0", "fb0", "mp1", "fa1", "ob0", "cp1", "fb1", "gfdown2", "gdown1", "ob1",
    "gfdown0", "kdown1", "xfdown2", "kup0", "gup0", "nb0", "bx0", "ydown1", "gup1", "xfdown0",
    "kup1", "nb1", "bx1", "zfdown2", "xdown1", "yup0", "oc1", "bp0", "oc0", "zfdown0", "fe0",
    "zdown1", "hb0", "ab0", "xup0", "yup1", "bp1", "sb0", "fe1", "pu0", "zup0", "sdown1",
    "hb1", "ab1", "sb1", "sup0", "pu1", "xup1", "od0", "tdown1", "wfdown2", "ginp0", "ginp1",
    "zup1", "kinp0", "wfdown0", "mo", "od1", "yinp0", "mi1", "mi0", "nr0", "kinp1", "sup1",
    "nr1", "gs", "pk", "gmisc0", "xinp0", "tup0", "yinp1", "zinp0", "tup1", "xinp1", "ymisc0",
    "zinp1", "sinp0", "xmisc0", "sinp1", "zmisc0", "tinp0", "sfdown0", "smisc0", "sfdown2",
    "tinp1", "tmisc0",
)


def make_tasks(o, st):
    tasks, needs = {}, {}

    def task(name, *before):
        def put(work):
            tasks[name] = work
            needs[name] = before

        return put

    def recv(*names):
        for name in names:
            st[name].wait_recv()

    def sent(*names):
        for name in names:
            for copy in st[name] if isinstance(st[name], (list, tuple)) else [st[name]]:
                o.sent(copy)

    @task("cn")
    def _():
        o.loads["cot0"].wait()
        o.loads["cot1"].wait()
        st["c_near0"] = o.share("cot", 0)
        st["c_near1"] = o.share("cot", 1)

    def per_micro(m):
        n = str(m)
        other = str(1 - m)

        @task("nf" + n)
        def _():
            o.norm_first(m)
            st["n_near" + n] = o.share("xn", m)

        @task("nx" + n, "nf" + n)
        def _():
            st["n_far" + n] = o.cross("xn", m)

        @task("np" + n, "nx" + n)
        def _():
            st["n_both" + n] = o.pass_on("xn", m, st["n_far" + n])

        @task("pa" + n, "nf" + n, *(["pa0"] if m else []))
        def _():
            if m == 0:
                o.loads["in"].wait()
            recv("n_near" + n)
            o.project(m, False)

        @task("pb" + n, "np" + n, *(["pa0"] if m else []))
        def _():
            recv("n_both" + n)
            o.project(m, True)

        @task("sc" + n, "pa" + n, "pb" + n)
        def _():
            o.scan(m)

        @task("at" + n, "sc" + n, *(["at0"] if m else []))
        def _():
            if m:
                st["save"].wait()
            o.attend(m)
            st["save"] = o.save(m)

        @task("cx" + n, "cn")
        def _():
            st["c_far" + n] = o.cross("cot", m)

        @task("cp" + n, "cx" + n)
        def _():
            st["c_both" + n] = o.pass_on("cot", m, st["c_far" + n])

        @task("br" + n, "at" + n, *(["br0"] if m else []))
        def _():
            if m == 0:
                o.loads["out"].wait()
            st["br" + n] = o.branch(m, st["br0"] if m else [])

        @task("oa" + n, "br" + n)
        def _():
            st["oa" + n] = o.owed("a", st["br" + n], m)

        @task("ns" + n, "oa" + n)
        def _():
            o.norm_second(m, st["br" + n], st["oa" + n])
            st["m_near" + n] = o.share("n2", m)

        @task("mx" + n, "ns" + n)
        def _():
            st["m_far" + n] = o.cross("n2", m)

        @task("mp" + n, "mx" + n)
        def _():
            st["m_both" + n] = o.pass_on("n2", m, st["m_far" + n])

        @task("fa" + n, "ns" + n, "cn", *(["fb0"] if m else ["br1"]))
        def _():
            if m == 0:
                o.loads["up"].wait()
                o.loads["down"].wait()
                sent("br1")
            else:
                sent("fa0")
            sent("oa" + n)
            recv("c_near" + n, "m_near" + n)
            st["fa" + n] = o.feed(m, False)

        @task("fb" + n, "fa" + n, "mp" + n, "cp" + n)
        def _():
            if m:
                sent("fb0")
            recv("c_both" + n, "m_both" + n)
            st["fb" + n] = o.feed(m, True)

        @task("ob" + n, "fb" + n)
        def _():
            st["ob" + n] = o.owed("b", (st["fa" + n][1], st["fb" + n][1]), m)

        @task("oc" + n, "fb" + n)
        def _():
            st["oc" + n] = o.owed("a", (st["fa" + n][0], st["fb" + n][0]), m)

        @task("nb" + n, "ob" + n)
        def _():
            o.norm_second_back(m, (st["fa" + n][1], st["fb" + n][1]), st["ob" + n])
            st["b_near" + n] = o.share("gbr", m)

        @task("bx" + n, "nb" + n)
        def _():
            st["b_far" + n] = o.cross("gbr", m)

        @task("bp" + n, "bx" + n)
        def _():
            st["b_both" + n] = o.pass_on("gbr", m, st["b_far" + n])

        @task("fe" + n, "at1", *(["ab0"] if m else []))
        def _():
            if m == 0:
                st["save"].wait()
            st["fetch"] = o.fetch(m)

        @task("hb" + n, "bp" + n, *(["ab0"] if m else []))
        def _():
            recv("b_near" + n, "b_both" + n)
            o.heads_back(m)

        @task("ab" + n, "hb" + n, "fe" + n, *(["sb0"] if m else []))
        def _():
            st["fetch"].wait()
            o.attend_back(m)

        @task("sb" + n, "ab" + n)
        def _():
            o.scan_back(m)

        @task("pu" + n, "sb" + n, *(["pu0"] if m else ["fb1"]))
        def _():
            sent("ob" + n)
            if m == 0:
                sent("fa1", "fb1")
            st["pu" + n] = o.pull_back(m, st["pu0"] if m else [])

        @task("od" + n, "pu" + n)
        def _():
            st["od" + n] = o.owed("b", st["pu" + n], m)

        @task("mi" + n, "oc" + n)
        def _():
            sent("oc" + n)
            st["end" + n] = o.mix(m, (st["fa" + n][0], st["fb" + n][0]), st["oc" + n])

        @task("nr" + n, "od" + n, "mi" + n)
        def _():
            st["fin" + n] = o.norm_first_back(m, st["pu" + n], st["od" + n])

    per_micro(0)
    per_micro(1)

    @task("mo", "hb0", "hb1", "br1")
    def _():
        o.make_out()

    @task("gs", "nr0", "nr1", "nb0", "nb1")
    def _():
        st["gains"] = o.send_gains()

    @task("pk", "gs", "mo", "sb0", "sb1")
    def _():
        o.pack(st["gains"])

    ready = dict(down=("fb0", "fb1"), up=("fb0", "fb1"), inp=("pu0", "pu1"), misc=("pk",))

    def per_job(job):
        name = job[0] + str(job[1])
        last = ready[job[0]]
        if job[0] != "misc":

            @task("g" + name, *last)
            def _():
                o.tile_give(job)
                st[name] = o.swap_y(job)

            @task("k" + name, *last)
            def _():
                o.tile_keep(job)

            ahead = ("g" + name, "k" + name)
        else:

            @task("g" + name, *last)
            def _():
                st[name] = o.swap_y(job)

            ahead = ("g" + name,)

        @task("y" + name, *ahead)
        def _():
            st[name] = o.sum_y(job, st[name])

        @task("x" + name, "y" + name)
        def _():
            st[name] = o.sum_x(job, st[name])

        @task("z" + name, "x" + name)
        def _():
            st[name] = o.sum_z(job, st[name])

        @task("s" + name, "z" + name)
        def _():
            st[name] = o.spread_y(job, st[name])

        @task("t" + name, "s" + name)
        def _():
            st[name] = o.spread_t(job, st[name])

    for job in JOBS:
        per_job(job)

    def per_tile(job):
        name = "f" + job[0] + str(job[1])

        @task("g" + name, *ready[job[0]])
        def _():
            st[name] = o.first_give(job)

        @task("x" + name, "g" + name)
        def _():
            st[name] = o.first_x(job, st[name])

        @task("z" + name, "x" + name)
        def _():
            st[name] = o.first_z(job, st[name])

        @task("w" + name, "z" + name)
        def _():
            st[name] = o.first_w(job, st[name])

        @task("s" + name, "w" + name)
        def _():
            st[name] = o.first_s(job, st[name])

    for job in FIRST:
        per_tile(job)
    tiles = {
        name: ["f" + n + str(i) for n, i in FIRST if n == name]
        + [n + str(i) for n, i in JOBS if n == name]
        for name in ready
    }
    needs["hb0"] += tuple(k + n for n in tiles["down"] for k in "gk" if k + n in tasks)
    return tasks, needs


def run(o):
    st = {}
    tasks, needs = make_tasks(o, st)
    done = set()
    for name in ORDER:
        assert all(ahead in done for ahead in needs[name]), name
        tasks[name]()
        done.add(name)
    assert len(done) == len(tasks)
    for name, i in JOBS:
        o.finish(st[name + str(i)])
    for name, i in FIRST:
        o.finish(st["f" + name + str(i)])
    for name in ("end0", "end1", "fin0", "fin1"):
        st[name].wait()


class Copies:
    def __init__(self, send, recv):
        self.send, self.recv, self.used, self.open = send, recv, 0, []

    def start(self, source, target, device):
        copy = pltpu.make_async_remote_copy(
            src_ref=source,
            dst_ref=target,
            send_sem=self.send.at[self.used],
            recv_sem=self.recv.at[self.used],
            device_id=device,
            device_id_type=pl.DeviceIdType.MESH,
        )
        self.used += 1
        copy.start()
        self.open.append(copy)
        return copy

    def sent(self, copy):
        copy.wait_send()
        self.open = [other for other in self.open if other is not copy]

    def drain(self):
        for copy in self.open:
            copy.wait_send()
        self.open = []


class Moves:
    def __init__(self, sems):
        self.sems, self.used = sems, 0

    def start(self, source, target):
        copy = pltpu.make_async_copy(source, target, self.sems.at[self.used])
        self.used += 1
        copy.start()
        return copy


def layer(
    nz, tokens, lengths, cotangent, gain_one, gain_two, w_in, ssm, ctx_w, w_out, w_up, w_down
):
    count, rows, width = tokens.shape
    chans = w_out.shape[0]
    heads = chans // HD
    hidden = w_up.shape[1]
    total = 4 * rows
    pair = 2 * rows
    small_rows = heads * CTX + 3 * NS + 8
    unit = 2 * nz * 16
    misc_rows = width + small_rows + (-small_rows % unit)
    sizes = dict(down=(hidden, width), up=(width, hidden), inp=(width, 4 * chans), misc=(misc_rows, chans))
    names = list(sizes)
    share = {n: rows if sizes[n][1] == width else sizes[n][0] // 2 for n in names}
    n_jobs = sum(sizes[n][0] // 2 // share[n] for n in names)
    root = math.sqrt(2.0 / math.pi)
    n_remote = 51 + n_jobs * (1 + 2 * (nz - 1) + nz) + len(FIRST) * 2 * nz
    n_local = 14 + n_jobs * (nz + 1) + len(FIRST) * (nz + 2)

    def kernel(*refs):
        (
            len_ref, tok, cot_hbm, g1, g2, in_hbm, rate, enter, leave, cw, out_hbm, up_hbm, down_hbm,
        ) = refs[:13]
        mixed_hbm, gtok_hbm, pr_hbm = refs[13:16]
        grads = dict(zip(names, refs[16:20]))
        ry = dict(zip(names, refs[20:24]))
        rz = dict(zip(names, refs[24:28]))
        fy, fz = refs[28:30]
        (
            w_i, w_o, w_u, w_d, xn, cot, n2, gbr, hid, gbf, qkv, u0, pr, ho, cx, ckv, dh, gctx,
            give, keep_a, keep_b, sib_a, sib_b, far_a, far_b, mid, acc, tmp, land, misc,
            gain_acc, gain_got, gcw, gss, send_sems, recv_sems, local_sems,
        ) = refs[30:]
        me = lax.axis_index("mp")
        core, chip = me % 2, me // 2
        near, far, both = chip * 2 + 1 - core, (1 - chip) * 2 + core, (1 - chip) * 2 + 1 - core
        dp = lax.axis_index("dp")
        y, z = dp % 2, dp // 2
        to_near, to_far, to_both = {"mp": near}, {"mp": far}, {"mp": both}
        to_y = {"dp": z * 2 + 1 - y}
        zs = [(z + k) % nz for k in range(nz)]
        to_z = [{"dp": zk * 2 + y} for zk in zs]
        paired = nz == 4
        z_pair, z_cross = z + 1 - 2 * (z % 2), (z + 2) % nz
        z_other = (z_pair + 2) % nz
        to_pair, to_cross = {"dp": z_pair * 2 + y}, {"dp": z_cross * 2 + y}
        remote, local = Copies(send_sems, recv_sems), Moves(local_sems)

        loads = {
            "in": local.start(in_hbm, w_i),
            "cot0": local.start(cot_hbm.at[0], cot.at[0, me]),
            "cot1": local.start(cot_hbm.at[1], cot.at[1, me]),
            "out": local.start(out_hbm, w_o),
            "up": local.start(up_hbm, w_u),
            "down": local.start(down_hbm, w_d),
        }
        barrier = pltpu.get_barrier_semaphore()
        for device in [to_near, to_far, to_both, to_y] + to_z[1:]:
            pl.semaphore_signal(
                barrier, inc=1, device_id=device, device_id_type=pl.DeviceIdType.MESH
            )
        pl.semaphore_wait(barrier, 3 + nz)

        def share_piece(buf, m):
            return remote.start(buf.at[m, me], buf.at[m, me], to_near)

        def cross(buf, m):
            return remote.start(buf.at[m, me], buf.at[m, me], to_far)

        def pass_on(buf, m, copy):
            copy.wait_recv()
            return remote.start(buf.at[m, far], buf.at[m, far], to_near)

        def offer(kind, slot, sib, m):
            return remote.start(give.at[kind, slot], sib.at[m, slot], to_near)

        def by_rows(work):
            step = 64

            def body(i, carry):
                work(pl.ds(pl.multiple_of(i * step, step), step))
                return carry

            lax.fori_loop(0, rows // step, body, 0)

        def owed(offers, keep, sib, far_buf, m):
            offers[1].wait_recv()

            def work(at):
                keep[m, 1, at, :] = (
                    keep[m, 1, at, :].astype(F32) + sib[m, 1, at, :].astype(F32)
                ).astype(BF16)

            by_rows(work)
            return remote.start(keep.at[m, 1], far_buf.at[m], to_far)

        def summed(offers, copy, keep, sib, far_buf, m):
            offers[0].wait_recv()
            copy.wait_recv()
            return lambda at: (
                keep[m, 0, at, :].astype(F32)
                + sib[m, 0, at, :].astype(F32)
                + far_buf[m, at, :].astype(F32)
            )

        def inverse_root(value):
            return lax.rsqrt(jnp.mean(value * value, axis=-1, keepdims=True) + EPS)

        def norm_first(m):
            def work(at):
                x = tok[m, at, :].astype(F32)
                xn[m, me, at, :] = (x * inverse_root(x) * g1[...]).astype(BF16)

            by_rows(work)

        def norm_second(m, branch):
            def work(at):
                value = tok[m, at, :].astype(F32) + branch(at)
                mid[m, at, :] = value
                n2[m, me, at, :] = (value * inverse_root(value) * g2[...]).astype(BF16)

            by_rows(work)

        def pulled(value, grad, gain, line):
            scale = inverse_root(value)
            unit_row = value * scale
            gain_acc[line : line + 1, :] += jnp.sum(grad * unit_row, axis=0, keepdims=True)
            inner = grad * gain[...]
            return scale * (inner - unit_row * jnp.mean(inner * unit_row, axis=-1, keepdims=True))

        def norm_second_back(m, grad):
            def work(at):
                value = cot[m, me, at, :].astype(F32) + pulled(mid[m, at, :], grad(at), g2, 1)
                gbr[m, me, at, :] = value.astype(BF16)

            by_rows(work)

        def norm_first_back(m, grad):
            def work(at):
                x = tok[m, at, :].astype(F32)
                mid[m, at, :] = gbr[m, me, at, :].astype(F32) + pulled(x, grad(at), g1, 0)

            by_rows(work)
            return local.start(mid.at[m], gtok_hbm.at[m])

        def mix(m, branch):
            def work(at):
                keep_a[m, 0, at, :] = (mid[m, at, :] + branch(at)).astype(BF16)

            by_rows(work)
            return local.start(keep_a.at[m, 0], mixed_hbm.at[m])

        def project(m, side):
            def body(i, carry):
                t = side * 2 + i
                at = pl.ds(pl.multiple_of(t * rows, rows), rows)
                x = xn[m, t]
                qkv[m, at, :] = dot(x, w_i[:, : 3 * chans]).astype(BF16)

                @pl.when(t < 2)
                def _():
                    u0[m, at, :] = dot(x, w_i[:, 3 * chans :])

                return carry

            lax.fori_loop(0, 2, body, 0)

        def scan(m):
            context = state_forward(u0.at[m], rate, enter, leave).astype(BF16)
            cx[m] = context
            for h in range(heads):
                ckv[m, h] = dot(context[:, h * HD : (h + 1) * HD], cw[h]).astype(BF16)

        def attend(m):
            valid, linked = layout_scalars(len_ref, m)
            for h in range(heads):
                lanes = slice(h * HD, (h + 1) * HD)
                klanes = slice(chans + h * HD, chans + (h + 1) * HD)
                vlanes = slice(2 * chans + h * HD, 2 * chans + (h + 1) * HD)
                for b in range(2):
                    for half in range(2):
                        row0 = half * rows
                        keys = row0 + rows
                        spot = b * BLK + row0
                        q = qkv[m, spot : spot + rows, lanes]
                        k = qkv[m, b * BLK : b * BLK + keys, klanes]
                        v = qkv[m, b * BLK : b * BLK + keys, vlanes]
                        s = dot_nt(q, k) * SCALE2
                        row = lax.broadcasted_iota(jnp.int32, (rows, keys), 0) + row0
                        col = lax.broadcasted_iota(jnp.int32, (rows, keys), 1)
                        allowed = (col < jnp.minimum(row, valid[b])) | (col == row)
                        s = jnp.where(allowed, s, NEG)
                        peak = jnp.max(s, axis=-1, keepdims=True)
                        if b:
                            sc = dot_nt(q, ckv[m, h, :, :HD]) * SCALE2
                            sc = jnp.where(linked, sc, NEG)
                            peak = jnp.maximum(peak, jnp.max(sc, axis=-1, keepdims=True))
                            ec = jnp.exp2(sc - peak)
                        e = jnp.exp2(s - peak)
                        norm = jnp.sum(e, axis=-1, keepdims=True)
                        if b:
                            norm = norm + jnp.sum(ec, axis=-1, keepdims=True)
                        inverse = 1.0 / norm
                        p = (e * inverse).astype(BF16)
                        pr[h, b, row0 : row0 + rows, CTX : CTX + keys] = p
                        o = dot(p, v)
                        if b:
                            pc = (ec * inverse).astype(BF16)
                            pr[h, b, row0 : row0 + rows, :CTX] = pc
                            o = o + dot(pc, ckv[m, h, :, HD:])
                        ho[m, 2 * b + half, :, lanes] = o.astype(BF16)

        def spread(product, keep, kind, sib, m, before):
            for copy in before:
                remote.sent(copy)
            give[kind, 1] = product(both).astype(BF16)
            second = offer(kind, 1, sib, m)
            give[kind, 0] = product(near).astype(BF16)
            first = offer(kind, 0, sib, m)
            keep[m, 1] = product(far).astype(BF16)
            keep[m, 0] = product(me).astype(BF16)
            return [first, second]

        def feed(m, side, other):
            slot = 1 if other else 0

            def body(i, carry):
                t = side * 2 + jnp.where(i == 0, 1 - core, core)
                for start in range(0, hidden, 256):
                    cut = slice(start, start + 256)
                    before = dot(n2[m, t], w_u[:, cut])
                    square = before * before
                    th = jnp.tanh(root * (before * (1.0 + 0.044715 * square)))
                    half = 0.5 + 0.5 * th
                    hid[m, t, :, cut] = (before * half).astype(BF16)
                    slope = half + (0.5 * root) * before * (1.0 - th * th) * (
                        1.0 + 0.134145 * square
                    )
                    gbf[m, t, :, cut] = (dot_nt(cot[m, t], w_d[cut, :]) * slope).astype(BF16)
                branch = dot(hid[m, t], w_d[...]).astype(BF16)
                gn = dot_nt(gbf[m, t], w_u[...]).astype(BF16)

                @pl.when(i == 0)
                def _():
                    give[0, slot] = branch
                    give[1, slot] = gn

                @pl.when(i == 1)
                def _():
                    keep_a[m, slot] = branch
                    keep_b[m, slot] = gn

                return carry

            lax.fori_loop(0, 2, body, 0)
            return offer(0, slot, sib_a, m), offer(1, slot, sib_b, m)

        def heads_back(m):
            def body(t, carry):
                at = pl.ds(pl.multiple_of(t * rows, rows), rows)
                dh[at, :] = dot_nt(gbr[m, t], w_o[...]).astype(BF16)
                return carry

            lax.fori_loop(0, 4, body, 0)

        def attend_back(m):
            for h in range(heads):
                lanes = slice(h * HD, (h + 1) * HD)
                klanes = slice(chans + h * HD, chans + (h + 1) * HD)
                vlanes = slice(2 * chans + h * HD, 2 * chans + (h + 1) * HD)
                for b in range(2):
                    grad_k, grad_v = [None, None], [None, None]
                    grad_c = grad_cv = None
                    for half in (1, 0):
                        row0 = half * rows
                        keys = row0 + rows
                        spot = slice(b * BLK + row0, b * BLK + row0 + rows)
                        go = dh[spot, lanes]
                        qh = qkv[m, spot, lanes]
                        kh = qkv[m, b * BLK : b * BLK + keys, klanes]
                        vh = qkv[m, b * BLK : b * BLK + keys, vlanes]
                        p = pr[h, b, row0 : row0 + rows, CTX : CTX + keys]
                        pf = p.astype(F32)
                        dprob = dot_nt(go, vh)
                        delta = jnp.sum(dprob * pf, axis=-1, keepdims=True)
                        if b:
                            pc = pr[h, b, row0 : row0 + rows, :CTX]
                            pcf = pc.astype(F32)
                            dpc = dot_nt(go, ckv[m, h, :, HD:])
                            delta = delta + jnp.sum(dpc * pcf, axis=-1, keepdims=True)
                            dsc = (pcf * (dpc - delta)).astype(BF16)
                        ds = (pf * (dprob - delta)).astype(BF16)
                        dq = dot(ds, kh)
                        if b:
                            dq = dq + dot(dsc, ckv[m, h, :, :HD])
                            one = dot_tn(dsc, qh)
                            two = dot_tn(pc, go)
                            grad_c = one if grad_c is None else grad_c + one
                            grad_cv = two if grad_cv is None else grad_cv + two
                        hid[m, 2 * b + half, :, lanes] = (dq * SCALE).astype(BF16)
                        dk = dot_tn(ds, qh)
                        dv = dot_tn(p, go)
                        if half:
                            grad_k = [dk[:rows], dk[rows:]]
                            grad_v = [dv[:rows], dv[rows:]]
                        else:
                            grad_k[0] = grad_k[0] + dk
                            grad_v[0] = grad_v[0] + dv
                    for part in range(2):
                        t = 2 * b + part
                        hid[m, t, :, klanes] = (grad_k[part] * SCALE).astype(BF16)
                        hid[m, t, :, vlanes] = grad_v[part].astype(BF16)
                    if b:
                        low_c = (grad_c * SCALE).astype(BF16)
                        low_cv = grad_cv.astype(BF16)
                        ch = cx[m, :, lanes]
                        gcw[m, h, :, :HD] = dot_tn(ch, low_c)
                        gcw[m, h, :, HD:] = dot_tn(ch, low_cv)
                        gctx[:, lanes] = dot_nt(low_c, cw[h, :, :HD]) + dot_nt(
                            low_cv, cw[h, :, HD:]
                        )

        def scan_back(m):
            state_backward(gctx[...], u0.at[m], u0.at[m], rate, enter, leave, gss.at[m])
            for t in range(2):
                hid[m, t, :, 3 * chans :] = u0[m, t * rows : (t + 1) * rows, :].astype(BF16)
                hid[m, 2 + t, :, 3 * chans :] = jnp.zeros((rows, chans), BF16)

        def gather_tile(left, right, tile):
            lanes = pl.ds(pl.multiple_of(tile * rows, rows), rows)
            acc[...] = jnp.zeros_like(acc)

            def body(i, carry):
                m, t = i // 4, i % 4
                acc[...] += dot_tn(left[m, t, :, lanes], right[m, t])
                return carry

            lax.fori_loop(0, 4 * count, body, 0)

        def part(ref, start, size):
            return ref.at[pl.ds(pl.multiple_of(start, 16), size), :]

        def job_rows(job, side):
            name, i = job
            span = sizes[name][0] // 2
            if sizes[name][1] != width:
                return side * span, span
            return side * span + i * rows, rows

        stages = dict(down=w_d, up=w_u, inp=w_i, misc=misc)
        sides = dict(down=(hid, cot), up=(n2, gbf), inp=(xn, hid))

        def tile(job, side):
            start, size = job_rows(job, side)
            gather_tile(*sides[job[0]], start // size)
            stages[job[0]][pl.ds(pl.multiple_of(start, size), size), :] = acc[...].astype(BF16)

        def tile_give(job):
            tile(job, 1 - y)

        def tile_keep(job):
            tile(job, y)

        def landing(job, size):
            if sizes[job[0]][1] != width:
                return tmp.at[pl.ds(0, size), :]
            return land.at[pl.ds(0, size), :]

        def swap_y(job):
            name, i = job
            start, size = job_rows(job, 1 - y)
            return remote.start(part(stages[name], start, size), ry[name].at[i], to_y)

        def sum_y(job, copy):
            name, i = job
            stage = stages[name]
            start, size = job_rows(job, y)
            piece = size // nz
            copy.wait_recv()
            got = landing(job, size)
            local.start(ry[name].at[i], got).wait()
            at = pl.ds(pl.multiple_of(start, 16), size)
            stage[at, :] = (stage[at, :].astype(F32) + got[...].astype(F32)).astype(BF16)
            if paired:
                return [
                    remote.start(part(stage, start + t * piece, piece), rz[name].at[i, k], to_pair)
                    for k, t in enumerate((z_pair, z_other))
                ]
            return [
                remote.start(
                    part(stage, start + zs[k] * piece, piece), rz[name].at[i, k - 1], to_z[k]
                )
                for k in range(1, nz)
            ]

        def add_landed(job, at, slots):
            name, i = job
            stage = stages[name]
            piece = job_rows(job, y)[1] // nz
            got = landing(job, len(slots) * piece)
            moves = [
                local.start(rz[name].at[i, slot], got.at[pl.ds(k * piece, piece), :])
                for k, slot in enumerate(slots)
            ]
            for move in moves:
                move.wait()
            value = stage[at, :].astype(F32)
            for k in range(len(slots)):
                value = value + got[k * piece : (k + 1) * piece, :].astype(F32)
            stage[at, :] = value.astype(BF16)

        def sum_x(job, copies):
            if not paired:
                return copies
            name, i = job
            start, size = job_rows(job, y)
            piece = size // nz
            spot = start + z_cross * piece
            copies[1].wait_recv()
            add_landed(job, pl.ds(pl.multiple_of(spot, 16), piece), (1,))
            mine = part(stages[name], spot, piece)
            return [copies[0], remote.start(mine, rz[name].at[i, 2], to_cross)]

        def sum_z(job, copies):
            name, i = job
            start, size = job_rows(job, y)
            piece = size // nz
            for copy in copies:
                copy.wait_recv()
            spot = start + z * piece
            slots = (0, 2) if paired else tuple(range(nz - 1))
            add_landed(job, pl.ds(pl.multiple_of(spot, 16), piece), slots)
            mine = part(stages[name], spot, piece)
            place = part(grads[name], spot, piece)
            outs = [remote.start(mine, place, d) for d in ([to_pair, to_cross] if paired else to_z[1:])]
            last = [remote.start(mine, place, to_y)]
            return outs, last, local.start(mine, place)

        def spread_y(job, state):
            name, i = job
            start, size = job_rows(job, y)
            piece = size // nz
            outs, last, move = state
            if paired:
                whose = (z_pair, z_cross)
            else:
                whose = [(z + nz - k) % nz for k in range(1, nz)]
            on = None
            for copy, owner in zip(outs, whose):
                copy.wait_recv()
                place = part(grads[name], start + owner * piece, piece)
                last.append(remote.start(place, place, to_y))
                if paired and owner is z_cross:
                    on = remote.start(place, place, to_pair)
            return last, move, on

        def spread_t(job, state):
            name, i = job
            start, size = job_rows(job, y)
            last, move, on = state
            if paired:
                on.wait_recv()
                piece = size // nz
                place = part(grads[name], start + z_other * piece, piece)
                last.append(remote.start(place, place, to_y))
            return last, move

        def add_refs(stage, at, refs):
            piece = rows // nz
            got = land.at[pl.ds(0, len(refs) * piece), :]
            moves = [
                local.start(ref, got.at[pl.ds(k * piece, piece), :]) for k, ref in enumerate(refs)
            ]
            for move in moves:
                move.wait()
            value = stage[at, :].astype(F32)
            for k in range(len(refs)):
                value = value + got[k * piece : (k + 1) * piece, :].astype(F32)
            stage[at, :] = value.astype(BF16)

        def first_give(job):
            name, i = job
            gather_tile(*sides[name], i)
            stage = stages[name]
            stage[i * rows : (i + 1) * rows, :] = acc[...].astype(BF16)
            piece = rows // nz
            if paired:
                ends = [(z_pair, to_pair), (z_other, to_pair)]
            else:
                ends = list(zip(zs, to_z))[1:]
            return [
                remote.start(
                    part(stage, i * rows + t * piece, piece), fz.at[FIRST.index(job), k], device
                )
                for k, (t, device) in enumerate(ends)
            ]

        def first_x(job, copies):
            if not paired:
                return copies
            name, i = job
            piece = rows // nz
            spot = i * rows + z_cross * piece
            copies[1].wait_recv()
            at = pl.ds(pl.multiple_of(spot, 16), piece)
            add_refs(stages[name], at, [fz.at[FIRST.index(job), 1]])
            mine = part(stages[name], spot, piece)
            return [copies[0], remote.start(mine, fz.at[FIRST.index(job), 2], to_cross)]

        def first_z(job, copies):
            name, i = job
            piece = rows // nz
            for copy in copies:
                copy.wait_recv()
            spot = i * rows + z * piece
            at = pl.ds(pl.multiple_of(spot, 16), piece)
            slots = (0, 2) if paired else range(nz - 1)
            add_refs(stages[name], at, [fz.at[FIRST.index(job), k] for k in slots])
            return remote.start(part(stages[name], spot, piece), fy.at[FIRST.index(job)], to_y)

        def first_w(job, copy):
            name, i = job
            piece = rows // nz
            copy.wait_recv()
            remote.sent(copy)
            spot = i * rows + z * piece
            at = pl.ds(pl.multiple_of(spot, 16), piece)
            add_refs(stages[name], at, [fy.at[FIRST.index(job)]])
            mine = part(stages[name], spot, piece)
            place = part(grads[name], spot, piece)
            outs = [remote.start(mine, place, d) for d in ([to_pair, to_cross] if paired else to_z[1:])]
            return outs, local.start(mine, place)

        def first_s(job, state):
            name, i = job
            outs, move = state
            if not paired:
                return outs, move
            piece = rows // nz
            outs[1].wait_recv()
            place = part(grads[name], i * rows + z_cross * piece, piece)
            return [outs[0], remote.start(place, place, to_pair)], move

        def finish(state):
            last, move = state
            for copy in last:
                copy.wait_recv()
            move.wait()

        def make_out():
            gather_tile(ho, gbr, 0)
            for j in range(width // chans):
                misc[j * chans : (j + 1) * chans, :] = acc[:, j * chans : (j + 1) * chans].astype(
                    BF16
                )

        def send_gains():
            return [
                remote.start(gain_acc, gain_got.at[k], device)
                for k, device in enumerate((to_near, to_far, to_both))
            ]

        def pack(copies):
            base = width
            for h in range(heads):
                misc[base + h * CTX : base + (h + 1) * CTX, :] = (gcw[0, h] + gcw[1, h]).astype(BF16)
            base += heads * CTX
            for k in range(3):
                misc[base + k * NS : base + (k + 1) * NS, :] = (gss[0, k] + gss[1, k]).astype(BF16)
            base += 3 * NS
            for copy in copies:
                copy.wait_recv()
            value = gain_acc[...] + gain_got[0] + gain_got[1] + gain_got[2]
            line = jnp.concatenate(
                [value[r : r + 1, j * chans : (j + 1) * chans] for r in range(2) for j in range(4)],
                axis=0,
            )
            misc[base:, :] = jnp.concatenate(
                [line, jnp.zeros((misc_rows - base - 8, chans), F32)], axis=0
            ).astype(BF16)

        def branch(m, before):
            return spread(lambda t: dot(ho[m, t], w_o[...]), keep_a, 0, sib_a, m, before)

        def pull_back(m, before):
            return spread(lambda t: dot_nt(hid[m, t], w_i[...]), keep_b, 1, sib_b, m, before)

        bufs = dict(xn=xn, cot=cot, n2=n2, gbr=gbr)
        sets = dict(a=(keep_a, sib_a, far_a), b=(keep_b, sib_b, far_b))
        o = types.SimpleNamespace(
            count=count,
            norm_first=norm_first,
            share=lambda buf, m: share_piece(bufs[buf], m),
            cross=lambda buf, m: cross(bufs[buf], m),
            pass_on=lambda buf, m, copy: pass_on(bufs[buf], m, copy),
            sent=remote.sent,
            loads=loads,
            project=lambda m, other: project(m, 1 - chip if other else chip),
            scan=scan,
            attend=attend,
            save=lambda m: local.start(pr, pr_hbm.at[m]),
            fetch=lambda m: local.start(pr_hbm.at[m], pr),
            branch=branch,
            owed=lambda kind, offers, m: owed(offers, *sets[kind], m),
            norm_second=lambda m, of, cp: norm_second(m, summed(of, cp, *sets["a"], m)),
            norm_second_back=lambda m, of, cp: norm_second_back(m, summed(of, cp, *sets["b"], m)),
            norm_first_back=lambda m, of, cp: norm_first_back(m, summed(of, cp, *sets["b"], m)),
            mix=lambda m, of, cp: mix(m, summed(of, cp, *sets["a"], m)),
            feed=lambda m, other: feed(m, 1 - chip if other else chip, other),
            heads_back=heads_back,
            attend_back=attend_back,
            scan_back=scan_back,
            pull_back=pull_back,
            tile_give=tile_give,
            tile_keep=tile_keep,
            swap_y=swap_y,
            sum_y=sum_y,
            sum_x=sum_x,
            sum_z=sum_z,
            spread_y=spread_y,
            spread_t=spread_t,
            first_give=first_give,
            first_x=first_x,
            first_z=first_z,
            first_w=first_w,
            first_s=first_s,
            finish=finish,
            make_out=make_out,
            send_gains=send_gains,
            pack=pack,
        )
        gain_acc[...] = jnp.zeros_like(gain_acc)
        run(o)
        remote.drain()
        assert remote.used <= n_remote and local.used <= n_local, (remote.used, local.used)

    pieces = (count, 4, rows)
    vm = pltpu.VMEM
    any_out = [
        shape((count, rows, width), BF16),
        shape((count, rows, width), F32),
        shape((count, heads, 2, BLK, BLK + CTX), BF16),
    ]
    any_out += [shape(sizes[n], BF16) for n in names]
    any_out += [
        shape((sizes[n][0] // 2 // share[n], share[n], sizes[n][1]), BF16) for n in names
    ]
    any_out += [
        shape((sizes[n][0] // 2 // share[n], nz - 1, share[n] // nz, sizes[n][1]), BF16)
        for n in names
    ]
    any_out += [
        shape((len(FIRST), rows // nz, width), BF16),
        shape((len(FIRST), nz - 1, rows // nz, width), BF16),
    ]
    results = pl.pallas_call(
        kernel,
        in_specs=[SMEM, VMEM, ANY, VMEM, VMEM, ANY, VMEM, VMEM, VMEM, VMEM, ANY, ANY, ANY],
        out_specs=[ANY] * len(any_out),
        out_shape=any_out,
        scratch_shapes=[
            vm(w_in.shape, BF16),
            vm(w_out.shape, BF16),
            vm(w_up.shape, BF16),
            vm(w_down.shape, BF16),
            vm(pieces + (width,), BF16),
            vm(pieces + (width,), BF16),
            vm(pieces + (width,), BF16),
            vm(pieces + (width,), BF16),
            vm(pieces + (hidden,), BF16),
            vm(pieces + (hidden,), BF16),
            vm((count, total, 3 * chans), BF16),
            vm((count, BLK, chans), F32),
            vm((heads, 2, BLK, BLK + CTX), BF16),
            vm(pieces + (chans,), BF16),
            vm((count, CTX, chans), BF16),
            vm((count, heads, CTX, 2 * HD), BF16),
            vm((total, chans), BF16),
            vm((CTX, chans), F32),
            vm((2, 2, rows, width), BF16),
            vm((count, 2, rows, width), BF16),
            vm((count, 2, rows, width), BF16),
            vm((count, 2, rows, width), BF16),
            vm((count, 2, rows, width), BF16),
            vm((count, rows, width), BF16),
            vm((count, rows, width), BF16),
            vm((count, rows, width), F32),
            vm((rows, width), F32),
            vm((misc_rows // 2, chans), BF16),
            vm((rows, width), BF16),
            vm((misc_rows, chans), BF16),
            vm((8, width), F32),
            vm((3, 8, width), F32),
            vm((count, heads, CTX, 2 * HD), F32),
            vm((count, 3, NS, chans), F32),
            pltpu.SemaphoreType.DMA((n_remote,)),
            pltpu.SemaphoreType.DMA((n_remote,)),
            pltpu.SemaphoreType.DMA((n_local,)),
        ],
        compiler_params=pltpu.CompilerParams(
            collective_id=0, has_side_effects=True, vmem_limit_bytes=63 << 20
        ),
        cost_estimate=cost(45e9, 60e6),
    )(lengths, tokens, cotangent, gain_one, gain_two, w_in, *ssm, ctx_w, w_out, w_up, w_down)
    return results[0], results[1], dict(zip(names, results[3:7]))


def publish(mixed, grad_tokens, grads, in_shape, ctx_shape, out_shape):
    count, rows, width = mixed.shape
    heads = ctx_shape[0]
    chans = in_shape[2]
    steps = 4
    parts = width // chans
    misc_rows = grads["misc"].shape[0]

    def kernel(m_ref, t_ref, d_ref, u_ref, i_ref, misc_ref, *outs):
        mo, to, do, uo, io, oo, co, ra, en, le, ga, gb = outs
        mo[...] = m_ref[...]
        to[...] = t_ref[...]
        do[...] = d_ref[...].astype(F32)
        uo[...] = u_ref[...].astype(F32)
        for k in range(in_shape[1]):
            io[:, k, :] = i_ref[:, k * chans : (k + 1) * chans].astype(F32)

        @pl.when(pl.program_id(0) == 0)
        def _():
            for j in range(parts):
                oo[:, j * chans : (j + 1) * chans] = misc_ref[
                    j * chans : (j + 1) * chans, :
                ].astype(F32)
            at = width
            for h in range(heads):
                co[h] = misc_ref[at + h * CTX : at + (h + 1) * CTX, :].astype(F32)
            at += heads * CTX
            for k, ref in enumerate((ra, en, le)):
                ref[...] = misc_ref[at + k * NS : at + (k + 1) * NS, :].astype(F32)
            at += 3 * NS
            tail = misc_ref[at : at + 16, :].astype(F32)
            for r, ref in enumerate((ga, gb)):
                for j in range(parts):
                    ref[:, j * chans : (j + 1) * chans] = tail[r * parts + j : r * parts + j + 1, :]

    def blocks(dims):
        return pl.BlockSpec((dims[0] // steps,) + dims[1:], lambda i: (i,) + (0,) * (len(dims) - 1))

    def whole(dims):
        return pl.BlockSpec(dims, lambda i: (0,) * len(dims))

    token_block = pl.BlockSpec((count, rows // steps, width), lambda i: (0, i, 0))
    small = [out_shape, ctx_shape] + [(NS, chans)] * 3 + [(1, width)] * 2
    big = [grads["down"].shape, grads["up"].shape]
    return pl.pallas_call(
        kernel,
        grid=(steps,),
        in_specs=[token_block] * 2
        + [blocks(d) for d in big]
        + [blocks(grads["inp"].shape), whole((misc_rows, chans))],
        out_specs=[token_block] * 2
        + [blocks(d) for d in big]
        + [blocks(in_shape)]
        + [whole(d) for d in small],
        out_shape=[shape(mixed.shape, BF16), shape(mixed.shape, F32)]
        + [shape(d, F32) for d in big + [in_shape] + small],
        compiler_params=params(62),
        cost_estimate=cost(0, 28e6),
    )(mixed, grad_tokens, grads["down"], grads["up"], grads["inp"], grads["misc"])


def body(
    tokens,
    lengths,
    cotangent,
    attn_gain,
    in_weights,
    ssm_rate,
    ssm_input,
    ssm_output,
    ctx_weights,
    out_weights,
    mlp_gain,
    up_weights,
    down_weights,
):
    width = tokens.shape[2]
    chans = out_weights.shape[0]
    mixed, grad_tokens, grads = layer(
        lax.axis_size("dp") // 2,
        tokens,
        lengths[0],
        cotangent,
        attn_gain.reshape(1, width),
        mlp_gain.reshape(1, width),
        in_weights.reshape(width, 4 * chans),
        (ssm_rate, ssm_input, ssm_output),
        ctx_weights,
        out_weights,
        up_weights,
        down_weights,
    )
    mixed, grad_tokens, down, up, inp, out, ctx, rate, enter, leave, one, two = publish(
        mixed, grad_tokens, grads, in_weights.shape, ctx_weights.shape, out_weights.shape
    )
    return (
        mixed,
        grad_tokens,
        one.reshape(width),
        inp,
        rate,
        enter,
        leave,
        ctx,
        out,
        two.reshape(width),
        up,
        down,
    )


def solution(mesh):
    rows = P(None, ("dp", "mp"), None)
    return jax.shard_map(
        body,
        mesh=mesh,
        in_specs=(
            rows,
            P("dp", None, None),
            rows,
            P(),
            P(None, None, "mp"),
            P(None, "mp"),
            P(None, "mp"),
            P(None, "mp"),
            P("mp", None, None),
            P("mp", None),
            P(),
            P(None, "mp"),
            P("mp", None),
        ),
        out_specs=(
            rows,
            rows,
            P(),
            P(None, None, "mp"),
            P(None, "mp"),
            P(None, "mp"),
            P(None, "mp"),
            P("mp", None, None),
            P("mp", None),
            P(),
            P(None, "mp"),
            P("mp", None),
        ),
        check_vma=False,
    )
```

```python
import functools
import math
import types

import jax
import jax.numpy as jnp
from jax import lax
from jax.experimental import pallas as pl
from jax.experimental.pallas import tpu as pltpu
from jax.sharding import PartitionSpec as P

HD = 128
BLK = 512
CTX = 128
HEAD = BLK - CTX
NS = 16
EPS = 1e-05
SCALE = 1.0 / math.sqrt(HD)
SCALE2 = SCALE * math.log2(math.e)
NEG = -1e30
F32 = jnp.float32
BF16 = jnp.bfloat16

VMEM = pl.BlockSpec(memory_space=pltpu.VMEM)
SMEM = pl.BlockSpec(memory_space=pltpu.SMEM)
ANY = pl.BlockSpec(memory_space=pl.ANY)


def params(mib):
    return pltpu.CompilerParams(vmem_limit_bytes=mib << 20)


def cost(flops, nbytes):
    return pl.CostEstimate(flops=int(flops), bytes_accessed=int(nbytes), transcendentals=0)


def dot(a, b):
    return lax.dot_general(a, b, (((1,), (0,)), ((), ())), preferred_element_type=F32)


def dot_nt(a, b):
    return lax.dot_general(a, b, (((1,), (1,)), ((), ())), preferred_element_type=F32)


def dot_tn(a, b):
    return lax.dot_general(a, b, (((0,), (0,)), ((), ())), preferred_element_type=F32)


def shape(dims, kind):
    return jax.ShapeDtypeStruct(dims, kind)


def triangle(upper):
    row = lax.broadcasted_iota(jnp.int32, (CTX, 2 * CTX), 0)
    col = lax.broadcasted_iota(jnp.int32, (CTX, 2 * CTX), 1) % CTX
    keep = (row <= col) if upper else (row >= col)
    return jnp.where(keep, 1.0, 0.0).astype(BF16)


def running(tri, values):
    high = values.astype(BF16)
    rest = (values - high.astype(F32)).astype(BF16)
    return dot(tri, jnp.concatenate([high, rest], axis=0))


def head_sums(u_ref, rate_ref, moment):
    width = rate_ref.shape[1]
    place = lax.broadcasted_iota(jnp.int32, (8, width), 0).astype(F32)
    sums, moments = [], []
    group = 4 if moment else 8
    for base in range(0, NS, group):
        rates = [rate_ref[n : n + 1, :] for n in range(base, base + group)]
        steps = [jnp.broadcast_to(jnp.exp(-8.0 * r), (8, width)) for r in rates]

        def body(chunk, carry):
            start = pl.multiple_of(chunk * 8, 8)
            rows = u_ref[pl.ds(start, 8), :]
            first = [acc * step + rows for acc, step in zip(carry[0], steps)]
            if not moment:
                return (first, carry[1])
            scaled = rows * (place + (chunk * 8 - HEAD).astype(F32))
            second = [acc * step + scaled for acc, step in zip(carry[1], steps)]
            return (first, second)

        zero = [jnp.zeros((8, width), F32) for _ in range(group)]
        first, second = lax.fori_loop(
            0, HEAD // 8, body, (zero, list(zero) if moment else []), unroll=4
        )
        for k, rate in enumerate(rates):
            last = jnp.exp(rate * (place - 8.0))
            sums.append(jnp.sum(first[k] * last, axis=0, keepdims=True))
            if moment:
                moments.append(jnp.sum(second[k] * last, axis=0, keepdims=True))
    return sums, moments


def state_forward(u_ref, rate_ref, in_ref, out_ref):
    width = rate_ref.shape[1]
    sums, _ = head_sums(u_ref, rate_ref, False)
    tail = u_ref[pl.ds(HEAD, CTX), :]
    time = lax.broadcasted_iota(jnp.int32, (CTX, width), 0).astype(F32)
    tri = triangle(False)
    total = jnp.zeros((CTX, width), F32)
    for n in range(NS):
        rate = rate_ref[n : n + 1, :]
        gain = in_ref[n : n + 1, :] * jnp.sqrt(1.0 - jnp.exp(-2.0 * rate))
        weight = gain * out_ref[n : n + 1, :]
        prefix = running(tri, jnp.exp(rate * time) * tail)
        total = total + weight * (jnp.exp(-rate * time) * (sums[n] + prefix))
    return total


def state_backward(grad, u_ref, du_ref, rate_ref, in_ref, out_ref, gs_ref):
    width = rate_ref.shape[1]
    sums, moments = head_sums(u_ref, rate_ref, True)
    tail = u_ref[pl.ds(HEAD, CTX), :]
    time = lax.broadcasted_iota(jnp.int32, (CTX, width), 0).astype(F32)
    place = lax.broadcasted_iota(jnp.int32, (8, width), 0).astype(F32)
    lower, upper = triangle(False), triangle(True)
    total = jnp.zeros((CTX, width), F32)
    starts = []
    for n in range(NS):
        rate = rate_ref[n : n + 1, :]
        root = jnp.sqrt(1.0 - jnp.exp(-2.0 * rate))
        enter = in_ref[n : n + 1, :]
        leave = out_ref[n : n + 1, :]
        gain = enter * root
        rising = jnp.exp(rate * time)
        driven = rising * tail
        states = sums[n] + running(lower, driven)
        seen = jnp.exp(-rate * time) * grad
        later = running(upper, seen)
        product = seen * states
        energy = jnp.sum(product, axis=0, keepdims=True)
        slope = jnp.sum(time * (product - driven * later), axis=0, keepdims=True)
        slope = slope - later[0:1] * moments[n]
        total = total + (gain * leave) * (rising * later)
        starts.append((gain * leave) * later[0:1])
        gs_ref[0, n : n + 1, :] = leave * (
            energy * enter * jnp.exp(-2.0 * rate) / root - gain * slope
        )
        gs_ref[1, n : n + 1, :] = leave * energy * root
        gs_ref[2, n : n + 1, :] = gain * energy
    du_ref[pl.ds(HEAD, CTX), :] = total
    group = 8
    for base in range(0, NS, group):
        rates = [rate_ref[n : n + 1, :] for n in range(base, base + group)]
        steps = [jnp.broadcast_to(jnp.exp(-8.0 * r), (8, width)) for r in rates]
        begin = [
            starts[base + k] * jnp.exp(rate * (place - 8.0)) for k, rate in enumerate(rates)
        ]

        def body(index, carry):
            start = pl.multiple_of(HEAD - 8 - index * 8, 8)
            value = functools.reduce(lambda a, b: a + b, carry)
            if base:
                value = value + du_ref[pl.ds(start, 8), :]
            du_ref[pl.ds(start, 8), :] = value
            return [c * step for c, step in zip(carry, steps)]

        lax.fori_loop(0, HEAD // 8, body, begin, unroll=4)


def layout_scalars(len_ref, micro):
    first, second = len_ref[micro, 0], len_ref[micro, 1]
    first_blocks = (first + (BLK - 1)) // BLK
    second_blocks = (second + (BLK - 1)) // BLK
    docs, valid = [], []
    for b in range(2):
        doc = jnp.where(b < first_blocks, 0, jnp.where(b < first_blocks + second_blocks, 1, 2))
        start = jnp.where(doc == 0, 0, first_blocks)
        extent = jnp.where(doc == 0, first, jnp.where(doc == 1, second, 0))
        docs.append(doc)
        valid.append(extent - (b - start) * BLK)
    return valid, docs[0] == docs[1]


ALL = (("down", 0), ("down", 1), ("up", 0), ("up", 1), ("inp", 0), ("inp", 1), ("misc", 0))
ALONG_Z = (("down", 0),)
JOBS = tuple(job for job in ALL if job not in ALONG_Z)
FIRST = tuple((name, i + 2 * half) for name, i in ALONG_Z for half in range(2))


ORDER = (
    "nf0", "nx0", "cn", "nf1", "pa0", "nx1", "pa1", "np0", "pb0", "sc0", "cx0", "np1", "at0",
    "br0", "pb1", "oa0", "sc1", "at1", "br1", "oa1", "ns0", "mx0", "ns1", "fe0", "fa0", "cp0",
    "mx1", "cx1", "mp0", "fb0", "fa1", "mp1", "cp1", "ob0", "fb1", "gfdown2", "gdown1", "ob1",
    "gfdown0", "kup1", "gup0", "xfdown2", "nb0", "kdown1", "bx0", "ydown1", "gup1", "xfdown0",
    "kup0", "nb1", "xdown1", "bx1", "oc0", "yup0", "bp0", "zfdown0", "zfdown2", "hb0",
    "zdown1", "oc1", "ab0", "xup0", "yup1", "bp1", "sb0", "sdown1", "hb1", "zup0", "wfdown2",
    "fe1", "pu0", "ab1", "xup1", "tdown1", "sb1", "od0", "sup0", "pu1", "ginp0", "wfdown0",
    "kinp0", "zup1", "ginp1", "mi1", "od1", "yinp0", "mi0", "nr0", "sup1", "kinp1", "nr1",
    "mo", "xinp0", "yinp1", "gs", "pk", "gmisc0", "tup1", "tup0", "zinp0", "xinp1", "ymisc0",
    "zinp1", "xmisc0", "sinp0", "sinp1", "zmisc0", "tinp1", "sfdown2", "smisc0", "tinp0",
    "sfdown0", "tmisc0",
)


def make_tasks(o, st):
    tasks, needs = {}, {}

    def task(name, *before):
        def put(work):
            tasks[name] = work
            needs[name] = before

        return put

    def recv(*names):
        for name in names:
            st[name].wait_recv()

    def sent(*names):
        for name in names:
            for copy in st[name] if isinstance(st[name], (list, tuple)) else [st[name]]:
                o.sent(copy)

    @task("cn")
    def _():
        o.loads["cot0"].wait()
        o.loads["cot1"].wait()
        st["c_near0"] = o.share("cot", 0)
        st["c_near1"] = o.share("cot", 1)

    def per_micro(m):
        n = str(m)
        other = str(1 - m)

        @task("nf" + n)
        def _():
            o.norm_first(m)
            st["n_near" + n] = o.share("xn", m)

        @task("nx" + n, "nf" + n)
        def _():
            st["n_far" + n] = o.cross("xn", m)

        @task("np" + n, "nx" + n)
        def _():
            st["n_both" + n] = o.pass_on("xn", m, st["n_far" + n])

        @task("pa" + n, "nf" + n, *(["pa0"] if m else []))
        def _():
            if m == 0:
                o.loads["in"].wait()
            recv("n_near" + n)
            o.project(m, False)

        @task("pb" + n, "np" + n, *(["pa0"] if m else []))
        def _():
            recv("n_both" + n)
            o.project(m, True)

        @task("sc" + n, "pa" + n, "pb" + n)
        def _():
            o.scan(m)

        @task("at" + n, "sc" + n, *(["at0"] if m else []))
        def _():
            if m:
                st["save"].wait()
            o.attend(m)
            st["save"] = o.save(m)

        @task("cx" + n, "cn")
        def _():
            st["c_far" + n] = o.cross("cot", m)

        @task("cp" + n, "cx" + n)
        def _():
            st["c_both" + n] = o.pass_on("cot", m, st["c_far" + n])

        @task("br" + n, "at" + n, *(["br0"] if m else []))
        def _():
            if m == 0:
                o.loads["out"].wait()
            st["br" + n] = o.branch(m, st["br0"] if m else [])

        @task("oa" + n, "br" + n)
        def _():
            st["oa" + n] = o.owed("a", st["br" + n], m)

        @task("ns" + n, "oa" + n)
        def _():
            o.norm_second(m, st["br" + n], st["oa" + n])
            st["m_near" + n] = o.share("n2", m)

        @task("mx" + n, "ns" + n)
        def _():
            st["m_far" + n] = o.cross("n2", m)

        @task("mp" + n, "mx" + n)
        def _():
            st["m_both" + n] = o.pass_on("n2", m, st["m_far" + n])

        @task("fa" + n, "ns" + n, "cn", *(["fb0"] if m else ["br1"]))
        def _():
            if m == 0:
                o.loads["up"].wait()
                o.loads["down"].wait()
                sent("br1")
            else:
                sent("fa0")
            sent("oa" + n)
            recv("c_near" + n, "m_near" + n)
            st["fa" + n] = o.feed(m, False)

        @task("fb" + n, "fa" + n, "mp" + n, "cp" + n)
        def _():
            if m:
                sent("fb0")
            recv("c_both" + n, "m_both" + n)
            st["fb" + n] = o.feed(m, True)

        @task("ob" + n, "fb" + n)
        def _():
            st["ob" + n] = o.owed("b", (st["fa" + n][1], st["fb" + n][1]), m)

        @task("oc" + n, "fb" + n)
        def _():
            st["oc" + n] = o.owed("a", (st["fa" + n][0], st["fb" + n][0]), m)

        @task("nb" + n, "ob" + n)
        def _():
            o.norm_second_back(m, (st["fa" + n][1], st["fb" + n][1]), st["ob" + n])
            st["b_near" + n] = o.share("gbr", m)

        @task("bx" + n, "nb" + n)
        def _():
            st["b_far" + n] = o.cross("gbr", m)

        @task("bp" + n, "bx" + n)
        def _():
            st["b_both" + n] = o.pass_on("gbr", m, st["b_far" + n])

        @task("fe" + n, "at1", *(["ab0"] if m else []))
        def _():
            if m == 0:
                st["save"].wait()
            st["fetch"] = o.fetch(m)

        @task("hb" + n, "bp" + n, *(["ab0"] if m else []))
        def _():
            recv("b_near" + n, "b_both" + n)
            o.heads_back(m)

        @task("ab" + n, "hb" + n, "fe" + n, *(["sb0"] if m else []))
        def _():
            st["fetch"].wait()
            o.attend_back(m)

        @task("sb" + n, "ab" + n)
        def _():
            o.scan_back(m)

        @task("pu" + n, "sb" + n, *(["pu0"] if m else ["fb1"]))
        def _():
            sent("ob" + n)
            if m == 0:
                sent("fa1", "fb1")
            st["pu" + n] = o.pull_back(m, st["pu0"] if m else [])

        @task("od" + n, "pu" + n)
        def _():
            st["od" + n] = o.owed("b", st["pu" + n], m)

        @task("mi" + n, "oc" + n)
        def _():
            sent("oc" + n)
            st["end" + n] = o.mix(m, (st["fa" + n][0], st["fb" + n][0]), st["oc" + n])

        @task("nr" + n, "od" + n, "mi" + n)
        def _():
            st["fin" + n] = o.norm_first_back(m, st["pu" + n], st["od" + n])

    per_micro(0)
    per_micro(1)

    @task("mo", "hb0", "hb1", "br1")
    def _():
        o.make_out()

    @task("gs", "nr0", "nr1", "nb0", "nb1")
    def _():
        st["gains"] = o.send_gains()

    @task("pk", "gs", "mo", "sb0", "sb1")
    def _():
        o.pack(st["gains"])

    ready = dict(down=("fb0", "fb1"), up=("fb0", "fb1"), inp=("pu0", "pu1"), misc=("pk",))

    def per_job(job):
        name = job[0] + str(job[1])
        last = ready[job[0]]
        if job[0] != "misc":

            @task("g" + name, *last)
            def _():
                o.tile_give(job)
                st[name] = o.swap_y(job)

            @task("k" + name, *last)
            def _():
                o.tile_keep(job)

            ahead = ("g" + name, "k" + name)
        else:

            @task("g" + name, *last)
            def _():
                st[name] = o.swap_y(job)

            ahead = ("g" + name,)

        @task("y" + name, *ahead)
        def _():
            st[name] = o.sum_y(job, st[name])

        @task("x" + name, "y" + name)
        def _():
            st[name] = o.sum_x(job, st[name])

        @task("z" + name, "x" + name)
        def _():
            st[name] = o.sum_z(job, st[name])

        @task("s" + name, "z" + name)
        def _():
            st[name] = o.spread_y(job, st[name])

        @task("t" + name, "s" + name)
        def _():
            st[name] = o.spread_t(job, st[name])

    for job in JOBS:
        per_job(job)

    def per_tile(job):
        name = "f" + job[0] + str(job[1])

        @task("g" + name, *ready[job[0]])
        def _():
            st[name] = o.first_give(job)

        @task("x" + name, "g" + name)
        def _():
            st[name] = o.first_x(job, st[name])

        @task("z" + name, "x" + name)
        def _():
            st[name] = o.first_z(job, st[name])

        @task("w" + name, "z" + name)
        def _():
            st[name] = o.first_w(job, st[name])

        @task("s" + name, "w" + name)
        def _():
            st[name] = o.first_s(job, st[name])

    for job in FIRST:
        per_tile(job)
    tiles = {
        name: ["f" + n + str(i) for n, i in FIRST if n == name]
        + [n + str(i) for n, i in JOBS if n == name]
        for name in ready
    }
    needs["hb0"] += tuple(k + n for n in tiles["down"] for k in "gk" if k + n in tasks)
    return tasks, needs


def run(o):
    st = {}
    tasks, needs = make_tasks(o, st)
    done = set()
    for name in ORDER:
        assert all(ahead in done for ahead in needs[name]), name
        tasks[name]()
        done.add(name)
    assert len(done) == len(tasks)
    for name, i in JOBS:
        o.finish(st[name + str(i)])
    for name, i in FIRST:
        o.finish(st["f" + name + str(i)])
    for name in ("end0", "end1", "fin0", "fin1"):
        st[name].wait()


class Copies:
    def __init__(self, send, recv):
        self.send, self.recv, self.used, self.open = send, recv, 0, []

    def start(self, source, target, device):
        copy = pltpu.make_async_remote_copy(
            src_ref=source,
            dst_ref=target,
            send_sem=self.send.at[self.used],
            recv_sem=self.recv.at[self.used],
            device_id=device,
            device_id_type=pl.DeviceIdType.MESH,
        )
        self.used += 1
        copy.start()
        self.open.append(copy)
        return copy

    def sent(self, copy):
        copy.wait_send()
        self.open = [other for other in self.open if other is not copy]

    def drain(self):
        for copy in self.open:
            copy.wait_send()
        self.open = []


class Moves:
    def __init__(self, sems):
        self.sems, self.used = sems, 0

    def start(self, source, target):
        copy = pltpu.make_async_copy(source, target, self.sems.at[self.used])
        self.used += 1
        copy.start()
        return copy


def layer(
    nz, tokens, lengths, cotangent, gain_one, gain_two, w_in, ssm, ctx_w, w_out, w_up, w_down
):
    count, rows, width = tokens.shape
    chans = w_out.shape[0]
    heads = chans // HD
    hidden = w_up.shape[1]
    total = 4 * rows
    pair = 2 * rows
    small_rows = heads * CTX + 3 * NS + 8
    unit = 2 * nz * 16
    misc_rows = width + small_rows + (-small_rows % unit)
    sizes = dict(down=(hidden, width), up=(width, hidden), inp=(width, 4 * chans), misc=(misc_rows, chans))
    names = list(sizes)
    share = {n: rows if sizes[n][1] == width else sizes[n][0] // 2 for n in names}
    n_jobs = sum(sizes[n][0] // 2 // share[n] for n in names)
    root = math.sqrt(2.0 / math.pi)
    n_remote = 51 + n_jobs * (1 + 2 * (nz - 1) + nz) + len(FIRST) * 2 * nz
    n_local = 14 + n_jobs * (nz + 1) + len(FIRST) * (nz + 2)

    def kernel(*refs):
        (
            len_ref, tok, cot_hbm, g1, g2, in_hbm, rate, enter, leave, cw, out_hbm, up_hbm, down_hbm,
        ) = refs[:13]
        mixed_hbm, gtok_hbm, pr_hbm = refs[13:16]
        grads = dict(zip(names, refs[16:20]))
        ry = dict(zip(names, refs[20:24]))
        rz = dict(zip(names, refs[24:28]))
        fy, fz = refs[28:30]
        (
            w_i, w_o, w_u, w_d, xn, cot, n2, gbr, hid, gbf, qkv, u0, pr, ho, cx, ckv, dh, gctx,
            give, keep_a, keep_b, sib_a, sib_b, far_a, far_b, mid, acc, tmp, land, misc,
            gain_acc, gain_got, gcw, gss, send_sems, recv_sems, local_sems,
        ) = refs[30:]
        me = lax.axis_index("mp")
        core, chip = me % 2, me // 2
        near, far, both = chip * 2 + 1 - core, (1 - chip) * 2 + core, (1 - chip) * 2 + 1 - core
        dp = lax.axis_index("dp")
        y, z = dp % 2, dp // 2
        to_near, to_far, to_both = {"mp": near}, {"mp": far}, {"mp": both}
        to_y = {"dp": z * 2 + 1 - y}
        zs = [(z + k) % nz for k in range(nz)]
        to_z = [{"dp": zk * 2 + y} for zk in zs]
        paired = nz == 4
        z_pair, z_cross = z + 1 - 2 * (z % 2), (z + 2) % nz
        z_other = (z_pair + 2) % nz
        to_pair, to_cross = {"dp": z_pair * 2 + y}, {"dp": z_cross * 2 + y}
        remote, local = Copies(send_sems, recv_sems), Moves(local_sems)

        loads = {
            "in": local.start(in_hbm, w_i),
            "cot0": local.start(cot_hbm.at[0], cot.at[0, me]),
            "cot1": local.start(cot_hbm.at[1], cot.at[1, me]),
            "out": local.start(out_hbm, w_o),
            "up": local.start(up_hbm, w_u),
            "down": local.start(down_hbm, w_d),
        }
        barrier = pltpu.get_barrier_semaphore()
        for device in [to_near, to_far, to_both, to_y] + to_z[1:]:
            pl.semaphore_signal(
                barrier, inc=1, device_id=device, device_id_type=pl.DeviceIdType.MESH
            )
        pl.semaphore_wait(barrier, 3 + nz)

        def share_piece(buf, m):
            return remote.start(buf.at[m, me], buf.at[m, me], to_near)

        def cross(buf, m):
            return remote.start(buf.at[m, me], buf.at[m, me], to_far)

        def pass_on(buf, m, copy):
            copy.wait_recv()
            return remote.start(buf.at[m, far], buf.at[m, far], to_near)

        def offer(kind, slot, sib, m):
            return remote.start(give.at[kind, slot], sib.at[m, slot], to_near)

        def by_rows(work):
            step = 64

            def body(i, carry):
                work(pl.ds(pl.multiple_of(i * step, step), step))
                return carry

            lax.fori_loop(0, rows // step, body, 0)

        def owed(offers, keep, sib, far_buf, m):
            offers[1].wait_recv()

            def work(at):
                keep[m, 1, at, :] = (
                    keep[m, 1, at, :].astype(F32) + sib[m, 1, at, :].astype(F32)
                ).astype(BF16)

            by_rows(work)
            return remote.start(keep.at[m, 1], far_buf.at[m], to_far)

        def summed(offers, copy, keep, sib, far_buf, m):
            offers[0].wait_recv()
            copy.wait_recv()
            return lambda at: (
                keep[m, 0, at, :].astype(F32)
                + sib[m, 0, at, :].astype(F32)
                + far_buf[m, at, :].astype(F32)
            )

        def inverse_root(value):
            return lax.rsqrt(jnp.mean(value * value, axis=-1, keepdims=True) + EPS)

        def norm_first(m):
            def work(at):
                x = tok[m, at, :].astype(F32)
                xn[m, me, at, :] = (x * inverse_root(x) * g1[...]).astype(BF16)

            by_rows(work)

        def norm_second(m, branch):
            def work(at):
                value = tok[m, at, :].astype(F32) + branch(at)
                mid[m, at, :] = value
                n2[m, me, at, :] = (value * inverse_root(value) * g2[...]).astype(BF16)

            by_rows(work)

        def pulled(value, grad, gain, line):
            scale = inverse_root(value)
            unit_row = value * scale
            gain_acc[line : line + 1, :] += jnp.sum(grad * unit_row, axis=0, keepdims=True)
            inner = grad * gain[...]
            return scale * (inner - unit_row * jnp.mean(inner * unit_row, axis=-1, keepdims=True))

        def norm_second_back(m, grad):
            def work(at):
                value = cot[m, me, at, :].astype(F32) + pulled(mid[m, at, :], grad(at), g2, 1)
                gbr[m, me, at, :] = value.astype(BF16)

            by_rows(work)

        def norm_first_back(m, grad):
            def work(at):
                x = tok[m, at, :].astype(F32)
                mid[m, at, :] = gbr[m, me, at, :].astype(F32) + pulled(x, grad(at), g1, 0)

            by_rows(work)
            return local.start(mid.at[m], gtok_hbm.at[m])

        def mix(m, branch):
            def work(at):
                keep_a[m, 0, at, :] = (mid[m, at, :] + branch(at)).astype(BF16)

            by_rows(work)
            return local.start(keep_a.at[m, 0], mixed_hbm.at[m])

        def project(m, side):
            def body(i, carry):
                t = side * 2 + i
                at = pl.ds(pl.multiple_of(t * rows, rows), rows)
                x = xn[m, t]
                qkv[m, at, :] = dot(x, w_i[:, : 3 * chans]).astype(BF16)

                @pl.when(t < 2)
                def _():
                    u0[m, at, :] = dot(x, w_i[:, 3 * chans :])

                return carry

            lax.fori_loop(0, 2, body, 0)

        def scan(m):
            context = state_forward(u0.at[m], rate, enter, leave).astype(BF16)
            cx[m] = context
            for h in range(heads):
                ckv[m, h] = dot(context[:, h * HD : (h + 1) * HD], cw[h]).astype(BF16)

        def attend(m):
            valid, linked = layout_scalars(len_ref, m)
            for h in range(heads):
                lanes = slice(h * HD, (h + 1) * HD)
                klanes = slice(chans + h * HD, chans + (h + 1) * HD)
                vlanes = slice(2 * chans + h * HD, 2 * chans + (h + 1) * HD)
                for b in range(2):
                    for half in range(2):
                        row0 = half * rows
                        keys = row0 + rows
                        spot = b * BLK + row0
                        q = qkv[m, spot : spot + rows, lanes]
                        k = qkv[m, b * BLK : b * BLK + keys, klanes]
                        v = qkv[m, b * BLK : b * BLK + keys, vlanes]
                        s = dot_nt(q, k) * SCALE2
                        row = lax.broadcasted_iota(jnp.int32, (rows, keys), 0) + row0
                        col = lax.broadcasted_iota(jnp.int32, (rows, keys), 1)
                        allowed = (col < jnp.minimum(row, valid[b])) | (col == row)
                        s = jnp.where(allowed, s, NEG)
                        peak = jnp.max(s, axis=-1, keepdims=True)
                        if b:
                            sc = dot_nt(q, ckv[m, h, :, :HD]) * SCALE2
                            sc = jnp.where(linked, sc, NEG)
                            peak = jnp.maximum(peak, jnp.max(sc, axis=-1, keepdims=True))
                            ec = jnp.exp2(sc - peak)
                        e = jnp.exp2(s - peak)
                        norm = jnp.sum(e, axis=-1, keepdims=True)
                        if b:
                            norm = norm + jnp.sum(ec, axis=-1, keepdims=True)
                        inverse = 1.0 / norm
                        p = (e * inverse).astype(BF16)
                        pr[h, b, row0 : row0 + rows, CTX : CTX + keys] = p
                        o = dot(p, v)
                        if b:
                            pc = (ec * inverse).astype(BF16)
                            pr[h, b, row0 : row0 + rows, :CTX] = pc
                            o = o + dot(pc, ckv[m, h, :, HD:])
                        ho[m, 2 * b + half, :, lanes] = o.astype(BF16)

        def spread(product, keep, kind, sib, m, before):
            for copy in before:
                remote.sent(copy)
            give[kind, 1] = product(both).astype(BF16)
            second = offer(kind, 1, sib, m)
            give[kind, 0] = product(near).astype(BF16)
            first = offer(kind, 0, sib, m)
            keep[m, 1] = product(far).astype(BF16)
            keep[m, 0] = product(me).astype(BF16)
            return [first, second]

        def feed(m, side, other):
            slot = 1 if other else 0

            def body(i, carry):
                t = side * 2 + jnp.where(i == 0, 1 - core, core)
                for start in range(0, hidden, 256):
                    cut = slice(start, start + 256)
                    before = dot(n2[m, t], w_u[:, cut])
                    square = before * before
                    th = jnp.tanh(root * (before * (1.0 + 0.044715 * square)))
                    half = 0.5 + 0.5 * th
                    hid[m, t, :, cut] = (before * half).astype(BF16)
                    slope = half + (0.5 * root) * before * (1.0 - th * th) * (
                        1.0 + 0.134145 * square
                    )
                    gbf[m, t, :, cut] = (dot_nt(cot[m, t], w_d[cut, :]) * slope).astype(BF16)
                branch = dot(hid[m, t], w_d[...]).astype(BF16)
                gn = dot_nt(gbf[m, t], w_u[...]).astype(BF16)

                @pl.when(i == 0)
                def _():
                    give[0, slot] = branch
                    give[1, slot] = gn

                @pl.when(i == 1)
                def _():
                    keep_a[m, slot] = branch
                    keep_b[m, slot] = gn

                return carry

            lax.fori_loop(0, 2, body, 0)
            return offer(0, slot, sib_a, m), offer(1, slot, sib_b, m)

        def heads_back(m):
            def body(t, carry):
                at = pl.ds(pl.multiple_of(t * rows, rows), rows)
                dh[at, :] = dot_nt(gbr[m, t], w_o[...]).astype(BF16)
                return carry

            lax.fori_loop(0, 4, body, 0)

        def attend_back(m):
            for h in range(heads):
                lanes = slice(h * HD, (h + 1) * HD)
                klanes = slice(chans + h * HD, chans + (h + 1) * HD)
                vlanes = slice(2 * chans + h * HD, 2 * chans + (h + 1) * HD)
                for b in range(2):
                    grad_k, grad_v = [None, None], [None, None]
                    grad_c = grad_cv = None
                    for half in (1, 0):
                        row0 = half * rows
                        keys = row0 + rows
                        spot = slice(b * BLK + row0, b * BLK + row0 + rows)
                        go = dh[spot, lanes]
                        qh = qkv[m, spot, lanes]
                        kh = qkv[m, b * BLK : b * BLK + keys, klanes]
                        vh = qkv[m, b * BLK : b * BLK + keys, vlanes]
                        p = pr[h, b, row0 : row0 + rows, CTX : CTX + keys]
                        pf = p.astype(F32)
                        dprob = dot_nt(go, vh)
                        delta = jnp.sum(dprob * pf, axis=-1, keepdims=True)
                        if b:
                            pc = pr[h, b, row0 : row0 + rows, :CTX]
                            pcf = pc.astype(F32)
                            dpc = dot_nt(go, ckv[m, h, :, HD:])
                            delta = delta + jnp.sum(dpc * pcf, axis=-1, keepdims=True)
                            dsc = (pcf * (dpc - delta)).astype(BF16)
                        ds = (pf * (dprob - delta)).astype(BF16)
                        dq = dot(ds, kh)
                        if b:
                            dq = dq + dot(dsc, ckv[m, h, :, :HD])
                            one = dot_tn(dsc, qh)
                            two = dot_tn(pc, go)
                            grad_c = one if grad_c is None else grad_c + one
                            grad_cv = two if grad_cv is None else grad_cv + two
                        hid[m, 2 * b + half, :, lanes] = (dq * SCALE).astype(BF16)
                        dk = dot_tn(ds, qh)
                        dv = dot_tn(p, go)
                        if half:
                            grad_k = [dk[:rows], dk[rows:]]
                            grad_v = [dv[:rows], dv[rows:]]
                        else:
                            grad_k[0] = grad_k[0] + dk
                            grad_v[0] = grad_v[0] + dv
                    for part in range(2):
                        t = 2 * b + part
                        hid[m, t, :, klanes] = (grad_k[part] * SCALE).astype(BF16)
                        hid[m, t, :, vlanes] = grad_v[part].astype(BF16)
                    if b:
                        low_c = (grad_c * SCALE).astype(BF16)
                        low_cv = grad_cv.astype(BF16)
                        ch = cx[m, :, lanes]
                        gcw[m, h, :, :HD] = dot_tn(ch, low_c)
                        gcw[m, h, :, HD:] = dot_tn(ch, low_cv)
                        gctx[:, lanes] = dot_nt(low_c, cw[h, :, :HD]) + dot_nt(
                            low_cv, cw[h, :, HD:]
                        )

        def scan_back(m):
            state_backward(gctx[...], u0.at[m], u0.at[m], rate, enter, leave, gss.at[m])
            for t in range(2):
                hid[m, t, :, 3 * chans :] = u0[m, t * rows : (t + 1) * rows, :].astype(BF16)
                hid[m, 2 + t, :, 3 * chans :] = jnp.zeros((rows, chans), BF16)

        def gather_tile(left, right, tile):
            lanes = pl.ds(pl.multiple_of(tile * rows, rows), rows)
            acc[...] = jnp.zeros_like(acc)

            def body(i, carry):
                m, t = i // 4, i % 4
                acc[...] += dot_tn(left[m, t, :, lanes], right[m, t])
                return carry

            lax.fori_loop(0, 4 * count, body, 0)

        def part(ref, start, size):
            return ref.at[pl.ds(pl.multiple_of(start, 16), size), :]

        def job_rows(job, side):
            name, i = job
            span = sizes[name][0] // 2
            if sizes[name][1] != width:
                return side * span, span
            return side * span + i * rows, rows

        stages = dict(down=w_d, up=w_u, inp=w_i, misc=misc)
        sides = dict(down=(hid, cot), up=(n2, gbf), inp=(xn, hid))

        def tile(job, side):
            start, size = job_rows(job, side)
            gather_tile(*sides[job[0]], start // size)
            stages[job[0]][pl.ds(pl.multiple_of(start, size), size), :] = acc[...].astype(BF16)

        def tile_give(job):
            tile(job, 1 - y)

        def tile_keep(job):
            tile(job, y)

        def landing(job, size):
            if sizes[job[0]][1] != width:
                return tmp.at[pl.ds(0, size), :]
            return land.at[pl.ds(0, size), :]

        def swap_y(job):
            name, i = job
            start, size = job_rows(job, 1 - y)
            return remote.start(part(stages[name], start, size), ry[name].at[i], to_y)

        def sum_y(job, copy):
            name, i = job
            stage = stages[name]
            start, size = job_rows(job, y)
            piece = size // nz
            copy.wait_recv()
            got = landing(job, size)
            local.start(ry[name].at[i], got).wait()
            at = pl.ds(pl.multiple_of(start, 16), size)
            stage[at, :] = (stage[at, :].astype(F32) + got[...].astype(F32)).astype(BF16)
            if paired:
                return [
                    remote.start(part(stage, start + t * piece, piece), rz[name].at[i, k], to_pair)
                    for k, t in enumerate((z_pair, z_other))
                ]
            return [
                remote.start(
                    part(stage, start + zs[k] * piece, piece), rz[name].at[i, k - 1], to_z[k]
                )
                for k in range(1, nz)
            ]

        def add_landed(job, at, slots):
            name, i = job
            stage = stages[name]
            piece = job_rows(job, y)[1] // nz
            got = landing(job, len(slots) * piece)
            moves = [
                local.start(rz[name].at[i, slot], got.at[pl.ds(k * piece, piece), :])
                for k, slot in enumerate(slots)
            ]
            for move in moves:
                move.wait()
            value = stage[at, :].astype(F32)
            for k in range(len(slots)):
                value = value + got[k * piece : (k + 1) * piece, :].astype(F32)
            stage[at, :] = value.astype(BF16)

        def sum_x(job, copies):
            if not paired:
                return copies
            name, i = job
            start, size = job_rows(job, y)
            piece = size // nz
            spot = start + z_cross * piece
            copies[1].wait_recv()
            add_landed(job, pl.ds(pl.multiple_of(spot, 16), piece), (1,))
            mine = part(stages[name], spot, piece)
            return [copies[0], remote.start(mine, rz[name].at[i, 2], to_cross)]

        def sum_z(job, copies):
            name, i = job
            start, size = job_rows(job, y)
            piece = size // nz
            for copy in copies:
                copy.wait_recv()
            spot = start + z * piece
            slots = (0, 2) if paired else tuple(range(nz - 1))
            add_landed(job, pl.ds(pl.multiple_of(spot, 16), piece), slots)
            mine = part(stages[name], spot, piece)
            place = part(grads[name], spot, piece)
            outs = [remote.start(mine, place, d) for d in ([to_pair, to_cross] if paired else to_z[1:])]
            last = [remote.start(mine, place, to_y)]
            return outs, last, local.start(mine, place)

        def spread_y(job, state):
            name, i = job
            start, size = job_rows(job, y)
            piece = size // nz
            outs, last, move = state
            if paired:
                whose = (z_pair, z_cross)
            else:
                whose = [(z + nz - k) % nz for k in range(1, nz)]
            on = None
            for copy, owner in zip(outs, whose):
                copy.wait_recv()
                place = part(grads[name], start + owner * piece, piece)
                last.append(remote.start(place, place, to_y))
                if paired and owner is z_cross:
                    on = remote.start(place, place, to_pair)
            return last, move, on

        def spread_t(job, state):
            name, i = job
            start, size = job_rows(job, y)
            last, move, on = state
            if paired:
                on.wait_recv()
                piece = size // nz
                place = part(grads[name], start + z_other * piece, piece)
                last.append(remote.start(place, place, to_y))
            return last, move

        def add_refs(stage, at, refs):
            piece = rows // nz
            got = land.at[pl.ds(0, len(refs) * piece), :]
            moves = [
                local.start(ref, got.at[pl.ds(k * piece, piece), :]) for k, ref in enumerate(refs)
            ]
            for move in moves:
                move.wait()
            value = stage[at, :].astype(F32)
            for k in range(len(refs)):
                value = value + got[k * piece : (k + 1) * piece, :].astype(F32)
            stage[at, :] = value.astype(BF16)

        def first_give(job):
            name, i = job
            gather_tile(*sides[name], i)
            stage = stages[name]
            stage[i * rows : (i + 1) * rows, :] = acc[...].astype(BF16)
            piece = rows // nz
            if paired:
                ends = [(z_pair, to_pair), (z_other, to_pair)]
            else:
                ends = list(zip(zs, to_z))[1:]
            return [
                remote.start(
                    part(stage, i * rows + t * piece, piece), fz.at[FIRST.index(job), k], device
                )
                for k, (t, device) in enumerate(ends)
            ]

        def first_x(job, copies):
            if not paired:
                return copies
            name, i = job
            piece = rows // nz
            spot = i * rows + z_cross * piece
            copies[1].wait_recv()
            at = pl.ds(pl.multiple_of(spot, 16), piece)
            add_refs(stages[name], at, [fz.at[FIRST.index(job), 1]])
            mine = part(stages[name], spot, piece)
            return [copies[0], remote.start(mine, fz.at[FIRST.index(job), 2], to_cross)]

        def first_z(job, copies):
            name, i = job
            piece = rows // nz
            for copy in copies:
                copy.wait_recv()
            spot = i * rows + z * piece
            at = pl.ds(pl.multiple_of(spot, 16), piece)
            slots = (0, 2) if paired else range(nz - 1)
            add_refs(stages[name], at, [fz.at[FIRST.index(job), k] for k in slots])
            return remote.start(part(stages[name], spot, piece), fy.at[FIRST.index(job)], to_y)

        def first_w(job, copy):
            name, i = job
            piece = rows // nz
            copy.wait_recv()
            remote.sent(copy)
            spot = i * rows + z * piece
            at = pl.ds(pl.multiple_of(spot, 16), piece)
            add_refs(stages[name], at, [fy.at[FIRST.index(job)]])
            mine = part(stages[name], spot, piece)
            place = part(grads[name], spot, piece)
            outs = [remote.start(mine, place, d) for d in ([to_pair, to_cross] if paired else to_z[1:])]
            return outs, local.start(mine, place)

        def first_s(job, state):
            name, i = job
            outs, move = state
            if not paired:
                return outs, move
            piece = rows // nz
            outs[1].wait_recv()
            place = part(grads[name], i * rows + z_cross * piece, piece)
            return [outs[0], remote.start(place, place, to_pair)], move

        def finish(state):
            last, move = state
            for copy in last:
                copy.wait_recv()
            move.wait()

        def make_out():
            gather_tile(ho, gbr, 0)
            for j in range(width // chans):
                misc[j * chans : (j + 1) * chans, :] = acc[:, j * chans : (j + 1) * chans].astype(
                    BF16
                )

        def send_gains():
            return [
                remote.start(gain_acc, gain_got.at[k], device)
                for k, device in enumerate((to_near, to_far, to_both))
            ]

        def pack(copies):
            base = width
            for h in range(heads):
                misc[base + h * CTX : base + (h + 1) * CTX, :] = (gcw[0, h] + gcw[1, h]).astype(BF16)
            base += heads * CTX
            for k in range(3):
                misc[base + k * NS : base + (k + 1) * NS, :] = (gss[0, k] + gss[1, k]).astype(BF16)
            base += 3 * NS
            for copy in copies:
                copy.wait_recv()
            value = gain_acc[...] + gain_got[0] + gain_got[1] + gain_got[2]
            line = jnp.concatenate(
                [value[r : r + 1, j * chans : (j + 1) * chans] for r in range(2) for j in range(4)],
                axis=0,
            )
            misc[base:, :] = jnp.concatenate(
                [line, jnp.zeros((misc_rows - base - 8, chans), F32)], axis=0
            ).astype(BF16)

        def branch(m, before):
            return spread(lambda t: dot(ho[m, t], w_o[...]), keep_a, 0, sib_a, m, before)

        def pull_back(m, before):
            return spread(lambda t: dot_nt(hid[m, t], w_i[...]), keep_b, 1, sib_b, m, before)

        bufs = dict(xn=xn, cot=cot, n2=n2, gbr=gbr)
        sets = dict(a=(keep_a, sib_a, far_a), b=(keep_b, sib_b, far_b))
        o = types.SimpleNamespace(
            count=count,
            norm_first=norm_first,
            share=lambda buf, m: share_piece(bufs[buf], m),
            cross=lambda buf, m: cross(bufs[buf], m),
            pass_on=lambda buf, m, copy: pass_on(bufs[buf], m, copy),
            sent=remote.sent,
            loads=loads,
            project=lambda m, other: project(m, 1 - chip if other else chip),
            scan=scan,
            attend=attend,
            save=lambda m: local.start(pr, pr_hbm.at[m]),
            fetch=lambda m: local.start(pr_hbm.at[m], pr),
            branch=branch,
            owed=lambda kind, offers, m: owed(offers, *sets[kind], m),
            norm_second=lambda m, of, cp: norm_second(m, summed(of, cp, *sets["a"], m)),
            norm_second_back=lambda m, of, cp: norm_second_back(m, summed(of, cp, *sets["b"], m)),
            norm_first_back=lambda m, of, cp: norm_first_back(m, summed(of, cp, *sets["b"], m)),
            mix=lambda m, of, cp: mix(m, summed(of, cp, *sets["a"], m)),
            feed=lambda m, other: feed(m, 1 - chip if other else chip, other),
            heads_back=heads_back,
            attend_back=attend_back,
            scan_back=scan_back,
            pull_back=pull_back,
            tile_give=tile_give,
            tile_keep=tile_keep,
            swap_y=swap_y,
            sum_y=sum_y,
            sum_x=sum_x,
            sum_z=sum_z,
            spread_y=spread_y,
            spread_t=spread_t,
            first_give=first_give,
            first_x=first_x,
            first_z=first_z,
            first_w=first_w,
            first_s=first_s,
            finish=finish,
            make_out=make_out,
            send_gains=send_gains,
            pack=pack,
        )
        gain_acc[...] = jnp.zeros_like(gain_acc)
        run(o)
        remote.drain()
        assert remote.used <= n_remote and local.used <= n_local, (remote.used, local.used)

    pieces = (count, 4, rows)
    vm = pltpu.VMEM
    any_out = [
        shape((count, rows, width), BF16),
        shape((count, rows, width), F32),
        shape((count, heads, 2, BLK, BLK + CTX), BF16),
    ]
    any_out += [shape(sizes[n], BF16) for n in names]
    any_out += [
        shape((sizes[n][0] // 2 // share[n], share[n], sizes[n][1]), BF16) for n in names
    ]
    any_out += [
        shape((sizes[n][0] // 2 // share[n], nz - 1, share[n] // nz, sizes[n][1]), BF16)
        for n in names
    ]
    any_out += [
        shape((len(FIRST), rows // nz, width), BF16),
        shape((len(FIRST), nz - 1, rows // nz, width), BF16),
    ]
    results = pl.pallas_call(
        kernel,
        in_specs=[SMEM, VMEM, ANY, VMEM, VMEM, ANY, VMEM, VMEM, VMEM, VMEM, ANY, ANY, ANY],
        out_specs=[ANY] * len(any_out),
        out_shape=any_out,
        scratch_shapes=[
            vm(w_in.shape, BF16),
            vm(w_out.shape, BF16),
            vm(w_up.shape, BF16),
            vm(w_down.shape, BF16),
            vm(pieces + (width,), BF16),
            vm(pieces + (width,), BF16),
            vm(pieces + (width,), BF16),
            vm(pieces + (width,), BF16),
            vm(pieces + (hidden,), BF16),
            vm(pieces + (hidden,), BF16),
            vm((count, total, 3 * chans), BF16),
            vm((count, BLK, chans), F32),
            vm((heads, 2, BLK, BLK + CTX), BF16),
            vm(pieces + (chans,), BF16),
            vm((count, CTX, chans), BF16),
            vm((count, heads, CTX, 2 * HD), BF16),
            vm((total, chans), BF16),
            vm((CTX, chans), F32),
            vm((2, 2, rows, width), BF16),
            vm((count, 2, rows, width), BF16),
            vm((count, 2, rows, width), BF16),
            vm((count, 2, rows, width), BF16),
            vm((count, 2, rows, width), BF16),
            vm((count, rows, width), BF16),
            vm((count, rows, width), BF16),
            vm((count, rows, width), F32),
            vm((rows, width), F32),
            vm((misc_rows // 2, chans), BF16),
            vm((rows, width), BF16),
            vm((misc_rows, chans), BF16),
            vm((8, width), F32),
            vm((3, 8, width), F32),
            vm((count, heads, CTX, 2 * HD), F32),
            vm((count, 3, NS, chans), F32),
            pltpu.SemaphoreType.DMA((n_remote,)),
            pltpu.SemaphoreType.DMA((n_remote,)),
            pltpu.SemaphoreType.DMA((n_local,)),
        ],
        compiler_params=pltpu.CompilerParams(
            collective_id=0, has_side_effects=True, vmem_limit_bytes=63 << 20
        ),
        cost_estimate=cost(45e9, 60e6),
    )(lengths, tokens, cotangent, gain_one, gain_two, w_in, *ssm, ctx_w, w_out, w_up, w_down)
    return results[0], results[1], dict(zip(names, results[3:7]))


def publish(mixed, grad_tokens, grads, in_shape, ctx_shape, out_shape):
    count, rows, width = mixed.shape
    heads = ctx_shape[0]
    chans = in_shape[2]
    steps = 2
    parts = width // chans
    misc_rows = grads["misc"].shape[0]

    def kernel(m_ref, t_ref, d_ref, u_ref, i_ref, misc_ref, *outs):
        mo, to, do, uo, io, oo, co, ra, en, le, ga, gb = outs
        mo[...] = m_ref[...]
        to[...] = t_ref[...]
        do[...] = d_ref[...].astype(F32)
        uo[...] = u_ref[...].astype(F32)
        for k in range(in_shape[1]):
            io[:, k, :] = i_ref[:, k * chans : (k + 1) * chans].astype(F32)

        @pl.when(pl.program_id(0) == 0)
        def _():
            for j in range(parts):
                oo[:, j * chans : (j + 1) * chans] = misc_ref[
                    j * chans : (j + 1) * chans, :
                ].astype(F32)
            at = width
            for h in range(heads):
                co[h] = misc_ref[at + h * CTX : at + (h + 1) * CTX, :].astype(F32)
            at += heads * CTX
            for k, ref in enumerate((ra, en, le)):
                ref[...] = misc_ref[at + k * NS : at + (k + 1) * NS, :].astype(F32)
            at += 3 * NS
            tail = misc_ref[at : at + 16, :].astype(F32)
            for r, ref in enumerate((ga, gb)):
                for j in range(parts):
                    ref[:, j * chans : (j + 1) * chans] = tail[r * parts + j : r * parts + j + 1, :]

    def blocks(dims):
        return pl.BlockSpec((dims[0] // steps,) + dims[1:], lambda i: (i,) + (0,) * (len(dims) - 1))

    def whole(dims):
        return pl.BlockSpec(dims, lambda i: (0,) * len(dims))

    token_block = pl.BlockSpec((count, rows // steps, width), lambda i: (0, i, 0))
    small = [out_shape, ctx_shape] + [(NS, chans)] * 3 + [(1, width)] * 2
    big = [grads["down"].shape, grads["up"].shape]
    return pl.pallas_call(
        kernel,
        grid=(steps,),
        in_specs=[token_block] * 2
        + [blocks(d) for d in big]
        + [blocks(grads["inp"].shape), whole((misc_rows, chans))],
        out_specs=[token_block] * 2
        + [blocks(d) for d in big]
        + [blocks(in_shape)]
        + [whole(d) for d in small],
        out_shape=[shape(mixed.shape, BF16), shape(mixed.shape, F32)]
        + [shape(d, F32) for d in big + [in_shape] + small],
        compiler_params=params(62),
        cost_estimate=cost(0, 28e6),
    )(mixed, grad_tokens, grads["down"], grads["up"], grads["inp"], grads["misc"])


def body(
    tokens,
    lengths,
    cotangent,
    attn_gain,
    in_weights,
    ssm_rate,
    ssm_input,
    ssm_output,
    ctx_weights,
    out_weights,
    mlp_gain,
    up_weights,
    down_weights,
):
    width = tokens.shape[2]
    chans = out_weights.shape[0]
    mixed, grad_tokens, grads = layer(
        lax.axis_size("dp") // 2,
        tokens,
        lengths[0],
        cotangent,
        attn_gain.reshape(1, width),
        mlp_gain.reshape(1, width),
        in_weights.reshape(width, 4 * chans),
        (ssm_rate, ssm_input, ssm_output),
        ctx_weights,
        out_weights,
        up_weights,
        down_weights,
    )
    mixed, grad_tokens, down, up, inp, out, ctx, rate, enter, leave, one, two = publish(
        mixed, grad_tokens, grads, in_weights.shape, ctx_weights.shape, out_weights.shape
    )
    return (
        mixed,
        grad_tokens,
        one.reshape(width),
        inp,
        rate,
        enter,
        leave,
        ctx,
        out,
        two.reshape(width),
        up,
        down,
    )


def solution(mesh):
    rows = P(None, ("dp", "mp"), None)
    return jax.shard_map(
        body,
        mesh=mesh,
        in_specs=(
            rows,
            P("dp", None, None),
            rows,
            P(),
            P(None, None, "mp"),
            P(None, "mp"),
            P(None, "mp"),
            P(None, "mp"),
            P("mp", None, None),
            P("mp", None),
            P(),
            P(None, "mp"),
            P("mp", None),
        ),
        out_specs=(
            rows,
            rows,
            P(),
            P(None, None, "mp"),
            P(None, "mp"),
            P(None, "mp"),
            P(None, "mp"),
            P("mp", None, None),
            P("mp", None),
            P(),
            P(None, "mp"),
            P("mp", None),
        ),
        check_vma=False,
    )
```
